32 devices in a mesh: dp: 8 (over y, x, core), seq: 4 (over z).
Axes of the slice: x: 2, y: 2, z: 4, core: 2. Of those that a mesh axis runs over, the one named last changes fastest.
Arguments:
- tokens: bfloat16 [16384, 768], P(('dp', 'seq')), may hold values from -6 to 6
- clip_lengths: int32 [8, 4], P('dp'), may hold values from 1 to 1537, as said below
- ln1_gain: float32 [768], replicated, may hold values from 0.25 to 1.75
- ln1_shift: float32 [768], replicated, may hold values from -3 to 3
- w_qkv: bfloat16 [768, 2304], replicated, may hold values from -0.21875 to 0.21875
- bias_query: float32 [768], replicated, may hold values from -3 to 3
- bias_value: float32 [768], replicated, may hold values from -3 to 3
- w_out: bfloat16 [768, 768], replicated, may hold values from -1.75 to 1.75
- bias_out: float32 [768], replicated, may hold values from -3 to 3
- ln2_gain: float32 [768], replicated, may hold values from 0.25 to 1.75
- ln2_shift: float32 [768], replicated, may hold values from -3 to 3
- w_up: bfloat16 [768, 3072], replicated, may hold values from -0.21875 to 0.21875
- bias_up: float32 [3072], replicated, may hold values from -3 to 3
- w_down: bfloat16 [3072, 768], replicated, may hold values from -0.109375 to 0.109375
- bias_down: float32 [768], replicated, may hold values from -3 to 3
- cotangent: bfloat16 [16384, 768], P(('dp', 'seq')), may hold values from -6 to 6
Outputs:
- block_out: bfloat16 [16384, 768], P(('dp', 'seq'))
- grad_tokens: bfloat16 [16384, 768], P(('dp', 'seq'))
- grad_ln1_gain: float32 [768], P('dp')
- grad_ln1_shift: float32 [768], P('dp')
- grad_w_qkv: float32 [768, 2304], P('dp')
- grad_bias_query: float32 [768], P('dp')
- grad_bias_value: float32 [768], P('dp')
- grad_w_out: float32 [768, 768], P('dp')
- grad_bias_out: float32 [768], P('dp')
- grad_ln2_gain: float32 [768], P('dp')
- grad_ln2_shift: float32 [768], P('dp')
- grad_w_up: float32 [768, 3072], P('dp')
- grad_bias_up: float32 [3072], P('dp')
- grad_w_down: float32 [3072, 768], P('dp')
- grad_bias_down: float32 [768], P('dp')
The draws below stay inside these ranges and needn't reach their ends.
Inputs may be any that keep to these rules, and one draw needn't show every extreme that they name: `clip_lengths`: each row's 4 lengths sum to 2048. In each row one clip, at a place drawn from the seed, has 1537 patches and another has a single patch; the others share the rest.
All inputs are finite; a program needn't handle non-finite values.
Results may differ from the reference program's by a relative error of at most 0.012.
Values may be sent and summed in bfloat16 or wider, within the bound.
A program may use at most 192 MiB of HBM per device.

```python
import jax
import jax.numpy as jnp
from jax import lax

D = 768
HEADS = 12
HDIM = 64
FF = 3072
L_DEV = 512
CLIPS = 4
SEQ_LEN = 2048
SEQS = 8
TOKENS = 16384


def draw_clip_lengths(key, part):
    key = jax.random.fold_in(key, 11)
    key_place, key_weights, key_single = jax.random.split(key, 3)
    long_clip = 3 * L_DEV + 1
    spare = SEQ_LEN - long_clip - (CLIPS - 1)
    place = jax.random.randint(key_place, (SEQS, 1), 0, CLIPS)
    weights = jax.random.randint(key_weights, (SEQS, CLIPS - 1), 1, 1000)
    single = jax.random.randint(key_single, (SEQS, 1), 0, CLIPS - 1)
    others = jnp.arange(CLIPS - 1, dtype=jnp.int32)[None, :]
    weights = jnp.where(others == single, 0, weights)
    running = jnp.cumsum(weights, axis=1)
    bounds = spare * running // running[:, -1:]
    starts = jnp.concatenate([jnp.zeros((SEQS, 1), jnp.int32), bounds[:, :-1]], axis=1)
    small = 1 + bounds - starts
    column = jnp.arange(CLIPS, dtype=jnp.int32)[None, :]
    source = jnp.clip(column - (column > place).astype(jnp.int32), 0, CLIPS - 2)
    picked = jnp.take_along_axis(small, jnp.broadcast_to(source, (SEQS, CLIPS)), axis=1)
    return jnp.where(column == place, long_clip, picked).astype(jnp.int32)


def block_levels(rng, extent, cuts, low, largest):
    loudness, own = 1.0, jax.random.fold_in(rng, 6)
    for dim, parts in cuts:
        draws = jnp.exp(jax.random.uniform(jax.random.fold_in(own, dim), (parts,), jnp.float32, low / len(cuts), largest / len(cuts)))
        loudness = loudness * jnp.repeat(draws, extent[dim] // parts).reshape([-1 if axis == dim else 1 for axis in range(len(extent))])
    return loudness


def normal_values(own_key, shape, spread, bound, cuts=(), held_as=jnp.bfloat16):
    level = block_levels(own_key, shape, cuts, -0.22, 0.18) if cuts else 1.0
    values = jax.random.normal(own_key, shape, jnp.float32) * spread * level
    return jnp.minimum(jnp.maximum(values, -bound), bound).astype(held_as)


def setup_inputs(seed: int = 0) -> dict:
    key_list = jax.random.split(jax.random.key(seed), 17)
    return {
        "tokens": normal_values(key_list[0], (TOKENS, D), 1.0, 6.0, ((0, 32),)),
        "clip_lengths": draw_clip_lengths(jax.random.fold_in(key_list[16], 71), 0),
        "ln1_gain": jnp.clip(1.0 + 0.15 * jax.random.normal(key_list[2], (D,), jnp.float32), 0.25, 1.75),
        "ln1_shift": normal_values(key_list[3], (D,), 0.3, 3.0, (), jnp.float32),
        "w_qkv": normal_values(key_list[4], (D, 3 * D), D ** -0.5, 0.21875),
        "bias_query": normal_values(key_list[5], (D,), 0.3, 3.0, (), jnp.float32),
        "bias_value": normal_values(key_list[6], (D,), 0.3, 3.0, (), jnp.float32),
        "w_out": normal_values(key_list[7], (D, D), (D // 64) ** -0.5, 1.75),
        "bias_out": normal_values(key_list[8], (D,), 0.3, 3.0, (), jnp.float32),
        "ln2_gain": jnp.clip(1.0 + 0.15 * jax.random.normal(key_list[9], (D,), jnp.float32), 0.25, 1.75),
        "ln2_shift": normal_values(key_list[10], (D,), 0.3, 3.0, (), jnp.float32),
        "w_up": normal_values(key_list[11], (D, FF), D ** -0.5, 0.21875),
        "bias_up": normal_values(key_list[12], (FF,), 0.3, 3.0, (), jnp.float32),
        "w_down": normal_values(key_list[13], (FF, D), FF ** -0.5, 0.109375),
        "bias_down": normal_values(key_list[14], (D,), 0.3, 3.0, (), jnp.float32),
        "cotangent": normal_values(key_list[15], (TOKENS, D), 1.0, 6.0, ((0, 32),)),
    }


epsilon = 1e-06
masked_score = -1e+30

@jax.custom_vjp
def low(v):
    return lax.optimization_barrier(v.astype(jnp.bfloat16)).astype(jnp.float32)

@jax.custom_vjp
def low_back(v):
    return v

def low_keep(v):
    return (low(v), None)

def low_pass(kept, grad):
    return (grad,)

def back_keep(v):
    return (v, None)

def back_low(kept, grad):
    return (low(grad),)
low.defvjp(low_keep, low_pass)
low_back.defvjp(back_keep, back_low)

def layer_norm(values, gain, shift):
    center = values - lax.optimization_barrier(jnp.mean(values, -1, keepdims=True))
    inverse = lax.rsqrt(lax.optimization_barrier(jnp.mean(center * center, -1, keepdims=True)) + epsilon)
    return center * inverse * gain + shift

def dense(left, right):
    return jnp.dot(left, right, precision=lax.Precision.HIGHEST)

def clip_segments(clip_lengths, length):
    clip_ends = jnp.cumsum(clip_lengths.reshape(-1).astype(jnp.int32))
    position = jnp.arange(length, dtype=jnp.int32)
    return lax.optimization_barrier(jnp.sum((position[:, None] >= clip_ends[None, :]).astype(jnp.int32), 1))

def attention(queries, key_rows, value_rows, segment):
    length = queries.shape[0]
    block_rows = min(512, length)
    block_count = length // block_rows
    softness = HDIM ** (-0.5)
    key_heads = key_rows.reshape(length, HEADS, HDIM)
    value_heads = value_rows.reshape(length, HEADS, HDIM)

    def one_block(inputs):
        query_block, segment_block = inputs
        allowed = (segment_block[:, None] == segment[None, :])[None]
        scores = jnp.einsum('qhd,khd->hqk', query_block, key_heads, precision=lax.Precision.HIGHEST) * softness
        scores = low_back(scores)
        scores = jnp.where(allowed, scores, masked_score)
        highest_score = lax.optimization_barrier(jnp.max(scores, -1, keepdims=True))
        powers = jnp.exp(scores - highest_score)
        chances = low(powers / lax.optimization_barrier(jnp.sum(powers, -1, keepdims=True)))
        mixture = jnp.einsum('hqk,khd->qhd', chances, value_heads, precision=lax.Precision.HIGHEST)
        return mixture.reshape(block_rows, HEADS * HDIM)
    blocks = (queries.reshape(block_count, block_rows, HEADS, HDIM), segment.reshape(block_count, block_rows))
    mixture = lax.map(jax.checkpoint(one_block), blocks)
    return mixture.reshape(length, HEADS * HDIM)

def forward(tokens, segment, ln1_gain, ln1_shift, w_qkv, bias_query, bias_value, w_out, bias_out, ln2_gain, ln2_shift, w_up, bias_up, w_down, bias_down):
    model_width = tokens.shape[1]
    hidden1 = low(layer_norm(tokens, ln1_gain, ln1_shift))
    projected = dense(hidden1, w_qkv)
    queries = low_back(low(projected[:, :model_width] + bias_query))
    key_rows = low_back(low(projected[:, model_width:2 * model_width]))
    value_rows = low_back(low(projected[:, 2 * model_width:] + bias_value))
    attended = low_back(low(attention(queries, key_rows, value_rows, segment)))
    middle = tokens + low_back(dense(attended, w_out) + bias_out)
    hidden2 = low(layer_norm(middle, ln2_gain, ln2_shift))
    upper_pre = low_back(dense(hidden2, w_up) + bias_up)
    activated = low(jax.nn.gelu(upper_pre, approximate=False))
    return middle + dense(activated, w_down) + bias_down

def reference(tokens, clip_lengths, ln1_gain, ln1_shift, w_qkv, bias_query, bias_value, w_out, bias_out, ln2_gain, ln2_shift, w_up, bias_up, w_down, bias_down, cotangent):
    params = tuple((member.astype(jnp.float32) for member in (ln1_gain, ln1_shift, w_qkv, bias_query, bias_value, w_out, bias_out, ln2_gain, ln2_shift, w_up, bias_up, w_down, bias_down)))
    inputs = tokens.astype(jnp.float32).reshape(SEQS, SEQ_LEN, D)
    grads_in = cotangent.astype(jnp.float32).reshape(SEQS, SEQ_LEN, D)

    def one_sequence(running, pieces):
        sequence, lengths, grad_seq = pieces
        segment = clip_segments(lengths, SEQ_LEN)

        def apply_layer(seq_in, *weights):
            return forward(seq_in, segment, *weights)
        output, pullback = jax.vjp(apply_layer, sequence, *params)
        pulled = pullback(grad_seq)
        running = tuple((before + added for before, added in zip(running, pulled[1:])))
        return (running, (output.astype(jnp.bfloat16), pulled[0].astype(jnp.bfloat16)))
    zeroes = tuple((jnp.zeros_like(member) for member in params))
    summed, (outputs, gradients) = lax.scan(one_sequence, zeroes, (inputs, clip_lengths, grads_in))
    return (outputs.reshape(TOKENS, D), gradients.reshape(TOKENS, D), summed[0], summed[1], summed[2], summed[3], summed[4], summed[5], summed[6], summed[7], summed[8], summed[9], summed[10], summed[11], summed[12])
```

```python
import functools
import math

import jax
import jax.numpy as jnp
from jax import lax
from jax.experimental import pallas as pl
from jax.experimental.pallas import tpu as pltpu
from jax.sharding import PartitionSpec as P

HDIM = 64
LANES = 128
STATS = 16
F32 = jnp.float32
BF16 = jnp.bfloat16
VMEM_BYTES = 56 << 20
NT = (((1,), (1,)), ((), ()))
NN = (((1,), (0,)), ((), ()))

epsilon = 1e-06
masked_score = -1e30


def dot_as(left, right, dims):
    return lax.dot_general(left, right, dims, preferred_element_type=F32)


def matmul(left, right):
    return dot_as(left, right, NN)


def inner_rows(left, right):
    return dot_as(left, right, (((0,), (0,)), ((), ())))


def inner_cols(left, right):
    return dot_as(left, right, NT)


def layer_norm(values, gain, shift):
    center = values - jnp.mean(values, -1, keepdims=True)
    inverse = lax.rsqrt(jnp.mean(center * center, -1, keepdims=True) + epsilon)
    normed = center * inverse
    return (normed * gain + shift, normed, inverse)


def norm_back(grad_out, normed, inverse, gain):
    scaled = grad_out * gain
    grad_in = inverse * (
        scaled
        - jnp.mean(scaled, -1, keepdims=True)
        - normed * jnp.mean(scaled * normed, -1, keepdims=True)
    )
    return (grad_in, jnp.sum(grad_out * normed, 0), jnp.sum(grad_out, 0))


def head_lanes(rows, head):
    lane = lax.broadcasted_iota(jnp.int32, (rows, LANES), 1)
    return (lane < HDIM) if head == 0 else (lane >= HDIM)


def place_stats(stat, rows, pair, values):
    lane = lax.broadcasted_iota(jnp.int32, (values[0].shape[0], LANES), 1)
    old = stat[rows, :]
    stat[rows, :] = jnp.where(
        lane == 2 * pair, values[0], jnp.where(lane == 2 * pair + 1, values[1], old)
    )


def attend_kernel(sub, pieces, q_ref, *refs):
    k_refs, v_refs = refs[:pieces], refs[pieces : 2 * pieces]
    mark_q, mark_k, out_ref, chance_ref, lse_ref, stat = refs[2 * pieces :]
    pair = pl.program_id(0)
    keys = jnp.concatenate(
        [jnp.concatenate([ref[...] for ref in k_refs], 0), mark_k[...]], 1
    )
    values = jnp.concatenate([ref[...] for ref in v_refs], 0)

    def step(i, carry):
        rows = pl.ds(pl.multiple_of(i * sub, sub), sub)
        query = q_ref[rows, :] * jnp.asarray(1.0 / math.sqrt(HDIM), BF16)
        outs, totals = [], []
        for head in range(2):
            own = jnp.where(head_lanes(sub, head), query, jnp.zeros_like(query))
            scores = dot_as(jnp.concatenate([own, mark_q[rows, :]], 1), keys, NT)
            highest = jnp.max(scores, -1, keepdims=True)
            powers = jnp.exp(scores - highest)
            total = jnp.sum(powers, -1, keepdims=True)
            chances = (powers * (1.0 / total)).astype(BF16)
            chance_ref[head, rows, :] = chances
            outs.append(dot_as(chances, values, NN))
            totals.append(highest + jnp.log(total))
        out_ref[rows, :] = jnp.where(head_lanes(sub, 0), outs[0], outs[1]).astype(BF16)
        place_stats(stat, rows, pair, totals)
        return carry

    lax.fori_loop(0, q_ref.shape[0] // sub, step, 0)

    @pl.when(pair == pl.num_programs(0) - 1)
    def _():
        lse_ref[...] = jnp.transpose(stat[...])[:STATS]


def grad_query_kernel(sub, pieces, chance_ref, grad_ref, out_ref, *refs):
    k_refs, v_refs = refs[:pieces], refs[pieces : 2 * pieces]
    dq_ref, delta_ref, stat = refs[2 * pieces :]
    pair = pl.program_id(0)
    keys = jnp.concatenate([ref[...] for ref in k_refs], 0)
    values = jnp.concatenate([ref[...] for ref in v_refs], 0)

    def step(i, carry):
        rows = pl.ds(pl.multiple_of(i * sub, sub), sub)
        grad = grad_ref[rows, :]
        product = grad.astype(F32) * out_ref[rows, :].astype(F32)
        outs, deltas = [], []
        for head in range(2):
            own = head_lanes(sub, head)
            delta = jnp.sum(jnp.where(own, product, 0.0), -1, keepdims=True)
            grad_chances = dot_as(jnp.where(own, grad, jnp.zeros_like(grad)), values, NT)
            scores = (chance_ref[head, rows, :].astype(F32) * (grad_chances - delta)).astype(BF16)
            outs.append(dot_as(scores, keys, NN))
            deltas.append(delta)
        both = jnp.where(head_lanes(sub, 0), outs[0], outs[1])
        dq_ref[rows, :] = (both * (1.0 / math.sqrt(HDIM))).astype(BF16)
        place_stats(stat, rows, pair, deltas)
        return carry

    lax.fori_loop(0, grad_ref.shape[0] // sub, step, 0)

    @pl.when(pair == pl.num_programs(0) - 1)
    def _():
        delta_ref[...] = jnp.transpose(stat[...])[:STATS]


def grad_key_kernel(sub, pieces, k_ref, v_ref, *refs):
    q_refs, g_refs = refs[:pieces], refs[pieces : 2 * pieces]
    lse_refs, delta_refs = refs[2 * pieces : 3 * pieces], refs[3 * pieces : 4 * pieces]
    mark_k, mark_q, dk_ref, dv_ref = refs[4 * pieces :]
    pair = pl.program_id(0)
    queries = jnp.concatenate([ref[...] for ref in q_refs], 0)
    grads = jnp.concatenate([ref[...] for ref in g_refs], 0)
    scaled = jnp.concatenate(
        [queries * jnp.asarray(1.0 / math.sqrt(HDIM), BF16), mark_q[...]], 1
    )

    def stats(which, head):
        return jnp.concatenate([ref[pl.ds(2 * pair + head, 1), :] for ref in which], 1)

    log_totals = [stats(lse_refs, head) for head in range(2)]
    deltas = [stats(delta_refs, head) for head in range(2)]

    def step(i, carry):
        rows = pl.ds(pl.multiple_of(i * sub, sub), sub)
        key, value = k_ref[rows, :], v_ref[rows, :]
        dks, dvs = [], []
        for head in range(2):
            own = head_lanes(sub, head)
            key_own = jnp.where(own, key, jnp.zeros_like(key))
            value_own = jnp.where(own, value, jnp.zeros_like(value))
            scores = dot_as(jnp.concatenate([key_own, mark_k[rows, :]], 1), scaled, NT)
            chances = jnp.exp(scores - log_totals[head])
            grad_chances = dot_as(value_own, grads, NT)
            grad_scores = (chances * (grad_chances - deltas[head])).astype(BF16)
            dvs.append(dot_as(chances.astype(BF16), grads, NN))
            dks.append(dot_as(grad_scores, queries, NN))
        first = head_lanes(sub, 0)
        dk = jnp.where(first, dks[0], dks[1]) * (1.0 / math.sqrt(HDIM))
        dk_ref[rows, :] = dk.astype(BF16)
        dv_ref[rows, :] = jnp.where(first, dvs[0], dvs[1]).astype(BF16)
        return carry

    lax.fori_loop(0, k_ref.shape[0] // sub, step, 0)


def columns(rows, first):
    return pl.BlockSpec((rows, LANES), lambda t: (0, first + t))


def whole(array):
    return pl.BlockSpec(array.shape, lambda t: (0,) * array.ndim)


def kernel_call(kernel, name, grid, in_specs, out_specs, out_shape, scratch, flops, moved):
    return pl.pallas_call(
        kernel,
        grid=grid,
        in_specs=in_specs,
        out_specs=out_specs,
        out_shape=out_shape,
        scratch_shapes=scratch,
        compiler_params=pltpu.CompilerParams(vmem_limit_bytes=VMEM_BYTES),
        cost_estimate=pl.CostEstimate(flops=flops, bytes_accessed=moved, transcendentals=0),
        name=name,
    )


def attend(own, projected, mark_q, mark_k, sub=256):
    rows, width = own.shape[0], own.shape[1] // 3
    pieces, pairs = len(projected), width // LANES
    length = rows * pieces
    stats = jax.ShapeDtypeStruct((STATS, rows), F32)
    return kernel_call(
        functools.partial(attend_kernel, sub, pieces),
        "attend",
        (pairs,),
        [columns(rows, 0)]
        + [columns(rows, pairs)] * pieces
        + [columns(rows, 2 * pairs)] * pieces
        + [whole(mark_q), whole(mark_k)],
        [
            columns(rows, 0),
            pl.BlockSpec((2, rows, length), lambda t: (t, 0, 0)),
            whole(stats),
        ],
        [
            jax.ShapeDtypeStruct((rows, width), BF16),
            jax.ShapeDtypeStruct((2 * pairs, rows, length), BF16),
            stats,
        ],
        [pltpu.VMEM((rows, LANES), F32)],
        24 * rows * length * width,
        4 * pairs * rows * length,
    )(own, *projected, *projected, mark_q, mark_k)


def grad_query(chances, grad, attended, projected, sub=256):
    rows, width = grad.shape
    pieces, pairs = len(projected), width // LANES
    length = rows * pieces
    stats = jax.ShapeDtypeStruct((STATS, rows), F32)
    return kernel_call(
        functools.partial(grad_query_kernel, sub, pieces),
        "grad_query",
        (pairs,),
        [
            pl.BlockSpec((2, rows, length), lambda t: (t, 0, 0)),
            columns(rows, 0),
            columns(rows, 0),
        ]
        + [columns(rows, pairs)] * pieces
        + [columns(rows, 2 * pairs)] * pieces,
        [columns(rows, 0), whole(stats)],
        [jax.ShapeDtypeStruct((rows, width), BF16), stats],
        [pltpu.VMEM((rows, LANES), F32)],
        16 * rows * length * width,
        4 * pairs * rows * length,
    )(chances, grad, attended, *projected, *projected)


def grad_key_value(own, projected, grads, log_totals, deltas, mark_k, mark_q, sub=256):
    rows, width = grads[0].shape
    pieces, pairs = len(projected), width // LANES
    length = rows * pieces
    result = jax.ShapeDtypeStruct((rows, width), BF16)
    return kernel_call(
        functools.partial(grad_key_kernel, sub, pieces),
        "grad_key_value",
        (pairs,),
        [columns(rows, pairs), columns(rows, 2 * pairs)]
        + [columns(rows, 0)] * (2 * pieces)
        + [whole(log_totals[0])] * (2 * pieces)
        + [whole(mark_k), whole(mark_q)],
        [columns(rows, 0)] * 2,
        [result] * 2,
        [],
        32 * rows * length * width,
        8 * length * width,
    )(own, own, *projected, *grads, *log_totals, *deltas, mark_k, mark_q)


def grad_weight_kernel(parts, index_ref, left_ref, right_ref, keep_ref, send_ref, turned):
    @pl.when(pl.program_id(0) == 0)
    def _():
        turned[...] = jnp.transpose(left_ref[...])

    total = dot_as(turned[...], right_ref[...], NN)
    rows = total.shape[0] // parts
    me = index_ref[0]
    for part in range(parts):
        place = part ^ me
        block = total[part * rows : (part + 1) * rows].astype(BF16)

        @pl.when(place % 2 == 0)
        def _():
            keep_ref[place // 2] = block

        @pl.when(place % 2 == 1)
        def _():
            send_ref[place // 2] = block


def grad_weight_wide(left, right, me, parts, tile):
    length, height = left.shape
    width = right.shape[1]
    rows = height // parts
    half = jax.ShapeDtypeStruct((parts // 2, rows, width), BF16)
    out = pl.BlockSpec((parts // 2, rows, tile), lambda n, at: (0, 0, n))
    return pl.pallas_call(
        functools.partial(grad_weight_kernel, parts),
        grid_spec=pltpu.PrefetchScalarGridSpec(
            num_scalar_prefetch=1,
            grid=(width // tile,),
            in_specs=[
                pl.BlockSpec((length, height), lambda n, at: (0, 0)),
                pl.BlockSpec((length, tile), lambda n, at: (0, n)),
            ],
            out_specs=[out, out],
            scratch_shapes=[pltpu.VMEM((height, length), BF16)],
        ),
        out_shape=[half, half],
        compiler_params=pltpu.CompilerParams(vmem_limit_bytes=VMEM_BYTES),
        cost_estimate=pl.CostEstimate(
            flops=2 * length * height * width, bytes_accessed=2 * height * width, transcendentals=0
        ),
        name="grad_weight_wide",
    )(me, left, right)


def grad_weight_tall_kernel(index_ref, left_ref, right_ref, out_ref):
    out_ref[0] = inner_rows(left_ref[...], right_ref[...]).astype(BF16)


def grad_weight_tall(left, right, me, parts):
    length, height = left.shape
    width = right.shape[1]
    rows = height // parts

    def half(which):
        return pl.pallas_call(
            grad_weight_tall_kernel,
            grid_spec=pltpu.PrefetchScalarGridSpec(
                num_scalar_prefetch=1,
                grid=(parts // 2,),
                in_specs=[
                    pl.BlockSpec((length, rows), lambda b, at: (0, (2 * b + which) ^ at[0])),
                    pl.BlockSpec((length, width), lambda b, at: (0, 0)),
                ],
                out_specs=pl.BlockSpec((1, rows, width), lambda b, at: (b, 0, 0)),
            ),
            out_shape=jax.ShapeDtypeStruct((parts // 2, rows, width), BF16),
            compiler_params=pltpu.CompilerParams(vmem_limit_bytes=VMEM_BYTES),
            cost_estimate=pl.CostEstimate(
                flops=length * height * width, bytes_accessed=height * width, transcendentals=0
            ),
            name="grad_weight_tall",
        )(me, left, right)

    return half(0), half(1)


def added(one, other):
    return (one.astype(F32) + other.astype(F32)).astype(BF16)


class PlanePlan:
    PLANE = (0, 3, 1, 2)
    PLACE = ((0, 2, 3, 1), (2, 0, 1, 3))
    pieces = 4

    def __init__(self):
        self.there = []
        for place in self.PLACE:
            self.there.append(
                [
                    ((y * 4 + j) * 4 + z, (y * 4 + place[z]) * 4 + self.PLANE[j])
                    for y in range(2)
                    for j in range(4)
                    for z in range(4)
                ]
            )
        self.back = [[(b, a) for a, b in pairs] for pairs in self.there]

    def move(self, rows, pairs):
        half = rows.shape[0] // 2
        return jnp.concatenate(
            [
                lax.ppermute(rows[:half], ("dp", "seq"), pairs[0]),
                lax.ppermute(rows[half:], ("dp", "seq"), pairs[1]),
            ]
        )

    def to_work(self, rows):
        return self.move(rows, self.there)

    def to_home(self, rows):
        return self.move(rows, self.back)

    def lengths(self, clip_lengths):
        return lax.ppermute(clip_lengths, ("dp", "seq"), self.there[0])

    def gather(self, own):
        core = lax.ppermute(own, "dp", [(i, i ^ 1) for i in range(8)])
        across = lax.ppermute(own, "dp", [(i, i ^ 2) for i in range(8)])
        corner = lax.ppermute(across, "dp", [(i, i ^ 1) for i in range(8)])
        return [own, core, across, corner]

    def positions(self, rows):
        j = lax.axis_index("dp") % 4
        half = rows // 2
        sources = jnp.asarray([[place.index(p) for place in self.PLACE] for p in range(4)], jnp.int32)
        found = []
        for piece in range(4):
            shards = sources[j ^ piece]
            for part in range(2):
                start = shards[part] * rows + part * half
                found.append(start + jnp.arange(half, dtype=jnp.int32))
        return jnp.concatenate(found)

    def own(self, gathered):
        return gathered[: gathered.shape[0] // 4]

    def weight(self, left, right):
        me = lax.axis_index("dp").astype(jnp.int32).reshape(1)
        if left.shape[1] // 8 % LANES == 0:
            return grad_weight_tall(left, right, me, 8)
        tile = 384 if right.shape[1] % 384 == 0 else right.shape[1]
        return grad_weight_wide(left, right, me, 8, tile)

    def swap(self, value, bit):
        return lax.ppermute(value, "dp", [(i, i ^ bit) for i in range(8)])

    def reduce(self, halves):
        keep, send = halves
        total = added(keep, self.swap(send, 1))
        middle = total.shape[2] // 2
        first, second = total[:, :, :middle], total[:, :, middle:]
        first = added(first[0::2], self.swap(first[1::2], 2))
        second = added(second[0:2], self.swap(second[2:4], 4))
        first = added(first[0], self.swap(first[1], 4))
        second = added(second[0], self.swap(second[1], 2))
        total = jnp.concatenate([first, second], 1)
        total = added(total, lax.ppermute(total, "seq", [(0, 1), (3, 2)]))
        total = added(total, lax.ppermute(total, "seq", [(1, 2), (2, 1)]))
        ends = lax.ppermute(total, "seq", [(1, 0), (2, 3)])
        z = lax.axis_index("seq")
        return jnp.where((z == 1) | (z == 2), total, ends).astype(F32)

    def reduce_vectors(self, vectors):
        packed = jnp.concatenate(vectors)
        for bit in (1, 2, 4):
            packed = packed + self.swap(packed, bit)
        for bit in (1, 2):
            packed = packed + lax.ppermute(packed, "seq", [(i, i ^ bit) for i in range(4)])
        results, start = [], 0
        for vector in vectors:
            part = vector.shape[0] // 8
            results.append(
                lax.dynamic_slice(packed, (start + lax.axis_index("dp") * part,), (part,))
            )
            start += vector.shape[0]
        return results


class PlainPlan:
    def __init__(self, pieces):
        self.pieces = pieces

    def to_work(self, rows):
        return rows

    def to_home(self, rows):
        return rows

    def lengths(self, clip_lengths):
        return clip_lengths

    def gather(self, own):
        gathered = lax.all_gather(own, "seq", axis=0, tiled=False)
        return [gathered[i] for i in range(self.pieces)]

    def positions(self, rows):
        return jnp.arange(rows * self.pieces, dtype=jnp.int32)

    def own(self, gathered):
        rows = gathered.shape[0] // self.pieces
        return lax.dynamic_slice_in_dim(gathered, lax.axis_index("seq") * rows, rows, 0)

    def weight(self, left, right):
        return inner_rows(left, right)

    def reduce(self, total):
        return lax.psum(lax.psum_scatter(total, "dp", scatter_dimension=0, tiled=True), "seq")

    def reduce_vectors(self, vectors):
        return [self.reduce(vector) for vector in vectors]


def gelu_parts(pre_act):
    inside = 0.5 * (1.0 + lax.erf(pre_act * math.sqrt(0.5)))
    slope = inside + pre_act * jnp.exp(-0.5 * pre_act * pre_act) * (1.0 / math.sqrt(2.0 * math.pi))
    return pre_act * inside, slope


def body(
    plan,
    tokens,
    clip_lengths,
    ln1_gain,
    ln1_shift,
    w_qkv,
    bias_query,
    bias_value,
    w_out,
    bias_out,
    ln2_gain,
    ln2_shift,
    w_up,
    bias_up,
    w_down,
    bias_down,
    cotangent,
):
    rows, width = tokens.shape
    here = plan.to_work(tokens)
    lengths = plan.lengths(clip_lengths)
    grad_out = plan.to_work(cotangent)
    pieces = plan.gather(here)

    clip_ends = jnp.cumsum(lengths.reshape(-1))
    position = plan.positions(rows)
    segment = jnp.sum((position[:, None] >= clip_ends[None, :]).astype(jnp.int32), 1)
    lane = jnp.arange(LANES, dtype=jnp.int32)[None, :]
    same = lane == segment[:, None]
    mark_k = same.astype(BF16)
    mark_q = jnp.where(same | (lane >= clip_ends.shape[0]), 0.0, masked_score).astype(BF16)

    bias = jnp.concatenate([bias_query, jnp.zeros_like(bias_query), bias_value])

    def project(piece):
        hidden = layer_norm(piece.astype(F32), ln1_gain, ln1_shift)[0].astype(BF16)
        return hidden, (matmul(hidden, w_qkv) + bias).astype(BF16)

    own_hidden1, own = project(here)
    projected = [project(piece)[1] for piece in pieces]
    if isinstance(plan, PlanePlan):
        projected[0] = own

    attended, chances, log_totals = attend(own, projected, plan.own(mark_q), mark_k)
    log_totals = plan.gather(log_totals)

    inputs32 = here.astype(F32)
    middle = inputs32 + matmul(attended, w_out) + bias_out
    normed2_out, normed2, inverse2 = layer_norm(middle, ln2_gain, ln2_shift)
    hidden2 = normed2_out.astype(BF16)
    upper = matmul(hidden2, w_up) + bias_up
    activated, slope = gelu_parts(upper)
    activated = activated.astype(BF16)
    grad_upper = (inner_cols(grad_out, w_down) * slope).astype(BF16)
    grad_hidden2 = inner_cols(grad_upper, w_up)
    grad_norm2, grad_ln2_gain, grad_ln2_shift = norm_back(grad_hidden2, normed2, inverse2, ln2_gain)
    grad_middle = grad_out.astype(F32) + grad_norm2
    grad_branch = grad_middle.astype(BF16)
    grad_attended = inner_cols(grad_branch, w_out).astype(BF16)
    grads = plan.gather(grad_attended)

    block_out = (middle + matmul(activated, w_down) + bias_down).astype(BF16)
    block_out = plan.to_home(block_out)
    grad_w_down = plan.reduce(plan.weight(activated, grad_out))
    grad_w_up = plan.reduce(plan.weight(hidden2, grad_upper))
    grad_w_out = plan.reduce(plan.weight(attended, grad_branch))
    grad_bias_down = jnp.sum(grad_out.astype(F32), 0)
    grad_bias_up = jnp.sum(grad_upper.astype(F32), 0)
    grad_bias_out = jnp.sum(grad_branch.astype(F32), 0)
    grad_bias_down, grad_bias_up, grad_bias_out, grad_ln2_gain, grad_ln2_shift = (
        plan.reduce_vectors(
            [grad_bias_down, grad_bias_up, grad_bias_out, grad_ln2_gain, grad_ln2_shift]
        )
    )

    dq, deltas = grad_query(chances, grad_attended, attended, projected)
    deltas = plan.gather(deltas)
    dk, dv = grad_key_value(
        own, projected, grads, log_totals, deltas, plan.own(mark_k), mark_q
    )
    grad_projected = jnp.concatenate([dq, dk, dv], 1)
    grad_w_qkv = plan.reduce(plan.weight(own_hidden1, grad_projected))
    grad_bias_query = jnp.sum(dq.astype(F32), 0)
    grad_bias_value = jnp.sum(dv.astype(F32), 0)
    grad_hidden1 = inner_cols(grad_projected, w_qkv)
    _, normed1, inverse1 = layer_norm(inputs32, ln1_gain, ln1_shift)
    grad_norm1, grad_ln1_gain, grad_ln1_shift = norm_back(grad_hidden1, normed1, inverse1, ln1_gain)
    grad_tokens = plan.to_home((grad_middle + grad_norm1).astype(BF16))
    grad_bias_query, grad_bias_value, grad_ln1_gain, grad_ln1_shift = plan.reduce_vectors(
        [grad_bias_query, grad_bias_value, grad_ln1_gain, grad_ln1_shift]
    )
    return (
        block_out,
        grad_tokens,
        grad_ln1_gain,
        grad_ln1_shift,
        grad_w_qkv,
        grad_bias_query,
        grad_bias_value,
        grad_w_out,
        grad_bias_out,
        grad_ln2_gain,
        grad_ln2_shift,
        grad_w_up,
        grad_bias_up,
        grad_w_down,
        grad_bias_down,
    )


def solution(mesh):
    sizes = dict(mesh.shape)
    plan = PlanePlan() if sizes == {"dp": 8, "seq": 4} else PlainPlan(sizes["seq"])
    rows = P(("dp", "seq"), None)
    return jax.shard_map(
        functools.partial(body, plan),
        mesh=mesh,
        in_specs=(rows, P("dp", None)) + (P(),) * 13 + (rows,),
        out_specs=(
            rows,
            rows,
            P("dp"),
            P("dp"),
            P("dp", None),
            P("dp"),
            P("dp"),
            P("dp", None),
            P("dp"),
            P("dp"),
            P("dp"),
            P("dp", None),
            P("dp"),
            P("dp", None),
            P("dp"),
        ),
        check_vma=False,
    )
```

```python
import functools
import math

import jax
import jax.numpy as jnp
from jax import lax
from jax.experimental import pallas as pl
from jax.experimental.pallas import tpu as pltpu
from jax.sharding import PartitionSpec as P

HDIM = 64
LANES = 128
STATS = 16
F32 = jnp.float32
BF16 = jnp.bfloat16
VMEM_BYTES = 56 << 20
NT = (((1,), (1,)), ((), ()))
NN = (((1,), (0,)), ((), ()))

epsilon = 1e-06
masked_score = -1e30


def dot_as(left, right, dims):
    return lax.dot_general(left, right, dims, preferred_element_type=F32)


def matmul(left, right):
    return dot_as(left, right, NN)


def inner_rows(left, right):
    return dot_as(left, right, (((0,), (0,)), ((), ())))


def inner_cols(left, right):
    return dot_as(left, right, NT)


def layer_norm(values, gain, shift):
    center = values - jnp.mean(values, -1, keepdims=True)
    inverse = lax.rsqrt(jnp.mean(center * center, -1, keepdims=True) + epsilon)
    normed = center * inverse
    return (normed * gain + shift, normed, inverse)


def norm_back(grad_out, normed, inverse, gain):
    scaled = grad_out * gain
    grad_in = inverse * (
        scaled
        - jnp.mean(scaled, -1, keepdims=True)
        - normed * jnp.mean(scaled * normed, -1, keepdims=True)
    )
    return (grad_in, jnp.sum(grad_out * normed, 0), jnp.sum(grad_out, 0))


def pick(table, index):
    found = jnp.int32(table[0])
    for i, value in enumerate(table[1:], 1):
        found = jnp.where(index == i, jnp.int32(value), found)
    return found


def place_of_device():
    dp, z = lax.axis_index("dp"), lax.axis_index("seq")
    return lax.div(dp, jnp.int32(4)), lax.rem(dp, jnp.int32(4)), z


def greet(devices):
    barrier = pltpu.get_barrier_semaphore()
    for device in devices:
        pl.semaphore_signal(barrier, inc=1, device_id=device, device_id_type=pl.DeviceIdType.MESH)
    pl.semaphore_wait(barrier, len(devices))


def remote(source, target, sent, landed, device):
    return pltpu.make_async_remote_copy(
        src_ref=source,
        dst_ref=target,
        send_sem=sent,
        recv_sem=landed,
        device_id=device,
        device_id_type=pl.DeviceIdType.MESH,
    )


def routes(plane, place):
    y, j, z = place_of_device()
    targets = [(y * 4 + pick(place[h], z), pick(plane, j)) for h in range(2)]
    sources = [
        (
            y * 4 + pick([plane.index(p) for p in range(4)], z),
            pick([place[h].index(p) for p in range(4)], j),
        )
        for h in range(2)
    ]
    return targets, sources


def moves(source, target, sent, landed, devices):
    half = source.shape[0] // 2
    return [
        remote(
            source.at[pl.ds(h * half, half)],
            target.at[pl.ds(h * half, half)],
            sent.at[h],
            landed.at[h],
            devices[h],
        )
        for h in range(2)
    ]


def head_lanes(rows, head):
    lane = lax.broadcasted_iota(jnp.int32, (rows, LANES), 1)
    return (lane < HDIM) if head == 0 else (lane >= HDIM)


def place_stats(stat, rows, pair, values):
    lane = lax.broadcasted_iota(jnp.int32, (values[0].shape[0], LANES), 1)
    old = stat[rows, :]
    stat[rows, :] = jnp.where(
        lane == 2 * pair, values[0], jnp.where(lane == 2 * pair + 1, values[1], old)
    )


def attend_kernel(sub, ways, q_ref, k_ref, v_ref, mark_q, mark_k, *refs):
    pair = pl.program_id(0)
    if ways is None:
        out_ref, chance_ref, lse_ref, stat = refs
    else:
        home_ref, out_ref, chance_ref, lse_ref, here_ref, stat, sent, landed = refs
        targets, sources = routes(*ways)

        @pl.when(pair == 0)
        def _():
            greet(targets + sources)
            for copy in moves(home_ref, here_ref, sent, landed, targets):
                copy.start()

    keys = jnp.concatenate([k_ref[...], mark_k[...]], 1)
    values = v_ref[...]

    def step(i, carry):
        rows = pl.ds(pl.multiple_of(i * sub, sub), sub)
        query = q_ref[rows, :] * jnp.asarray(1.0 / math.sqrt(HDIM), BF16)
        outs, totals = [], []
        for head in range(2):
            own = jnp.where(head_lanes(sub, head), query, jnp.zeros_like(query))
            scores = dot_as(jnp.concatenate([own, mark_q[rows, :]], 1), keys, NT)
            highest = jnp.max(scores, -1, keepdims=True)
            powers = jnp.exp(scores - highest)
            total = jnp.sum(powers, -1, keepdims=True)
            chances = (powers * (1.0 / total)).astype(BF16)
            chance_ref[head, rows, :] = chances
            outs.append(dot_as(chances, values, NN))
            totals.append(highest + jnp.log(total))
        out_ref[rows, :] = jnp.where(head_lanes(sub, 0), outs[0], outs[1]).astype(BF16)
        place_stats(stat, rows, pair, totals)
        return carry

    lax.fori_loop(0, q_ref.shape[0] // sub, step, 0)

    @pl.when(pair == pl.num_programs(0) - 1)
    def _():
        lse_ref[...] = jnp.transpose(stat[...])[:STATS]
        if ways is not None:
            for copy in moves(home_ref, here_ref, sent, landed, targets):
                copy.wait()


def grad_query_kernel(
    sub, chance_ref, grad_ref, out_ref, k_ref, v_ref, dq_ref, delta_ref, stat
):
    pair = pl.program_id(0)
    keys, values = k_ref[...], v_ref[...]

    def step(i, carry):
        rows = pl.ds(pl.multiple_of(i * sub, sub), sub)
        grad = grad_ref[rows, :]
        product = grad.astype(F32) * out_ref[rows, :].astype(F32)
        outs, deltas = [], []
        for head in range(2):
            own = head_lanes(sub, head)
            delta = jnp.sum(jnp.where(own, product, 0.0), -1, keepdims=True)
            grad_chances = dot_as(jnp.where(own, grad, jnp.zeros_like(grad)), values, NT)
            scores = (chance_ref[head, rows, :].astype(F32) * (grad_chances - delta)).astype(BF16)
            outs.append(dot_as(scores, keys, NN))
            deltas.append(delta)
        both = jnp.where(head_lanes(sub, 0), outs[0], outs[1])
        dq_ref[rows, :] = (both * (1.0 / math.sqrt(HDIM))).astype(BF16)
        place_stats(stat, rows, pair, deltas)
        return carry

    lax.fori_loop(0, grad_ref.shape[0] // sub, step, 0)

    @pl.when(pair == pl.num_programs(0) - 1)
    def _():
        delta_ref[...] = jnp.transpose(stat[...])[:STATS]


def grad_key_kernel(sub, pieces, k_ref, v_ref, q_ref, *refs):
    g_refs = refs[:pieces]
    lse_refs, delta_refs = refs[pieces : 2 * pieces], refs[2 * pieces : 3 * pieces]
    mark_k, mark_q, dk_ref, dv_ref = refs[3 * pieces :]
    pair = pl.program_id(0)
    queries = q_ref[...]
    grads = jnp.concatenate([ref[...] for ref in g_refs], 0)
    scaled = jnp.concatenate(
        [queries * jnp.asarray(1.0 / math.sqrt(HDIM), BF16), mark_q[...]], 1
    )

    def stats(which, head):
        return jnp.concatenate([ref[pl.ds(2 * pair + head, 1), :] for ref in which], 1)

    log_totals = [stats(lse_refs, head) for head in range(2)]
    deltas = [stats(delta_refs, head) for head in range(2)]

    def step(i, carry):
        rows = pl.ds(pl.multiple_of(i * sub, sub), sub)
        key, value = k_ref[rows, :], v_ref[rows, :]
        dks, dvs = [], []
        for head in range(2):
            own = head_lanes(sub, head)
            key_own = jnp.where(own, key, jnp.zeros_like(key))
            value_own = jnp.where(own, value, jnp.zeros_like(value))
            scores = dot_as(jnp.concatenate([key_own, mark_k[rows, :]], 1), scaled, NT)
            chances = jnp.exp(scores - log_totals[head])
            grad_chances = dot_as(value_own, grads, NT)
            grad_scores = (chances * (grad_chances - deltas[head])).astype(BF16)
            dvs.append(dot_as(chances.astype(BF16), grads, NN))
            dks.append(dot_as(grad_scores, queries, NN))
        first = head_lanes(sub, 0)
        dk = jnp.where(first, dks[0], dks[1]) * (1.0 / math.sqrt(HDIM))
        dk_ref[rows, :] = dk.astype(BF16)
        dv_ref[rows, :] = jnp.where(first, dvs[0], dvs[1]).astype(BF16)
        return carry

    lax.fori_loop(0, k_ref.shape[0] // sub, step, 0)


def columns(rows, first):
    return pl.BlockSpec((rows, LANES), lambda t: (0, first + t))


def whole(array):
    return pl.BlockSpec(array.shape, lambda t: (0,) * array.ndim)


def kernel_call(kernel, name, grid, in_specs, out_specs, out_shape, scratch, flops, moved, **params):
    return pl.pallas_call(
        kernel,
        grid=grid,
        in_specs=in_specs,
        out_specs=out_specs,
        out_shape=out_shape,
        scratch_shapes=scratch,
        compiler_params=pltpu.CompilerParams(vmem_limit_bytes=VMEM_BYTES, **params),
        cost_estimate=pl.CostEstimate(flops=flops, bytes_accessed=moved, transcendentals=0),
        name=name,
    )


def attend(plan, own, projected, mark_q, mark_k, cotangent, sub=256):
    rows, width = mark_q.shape[0], own.shape[1] // 3
    length, pairs = projected.shape[0], width // LANES
    stats = jax.ShapeDtypeStruct((STATS, rows), F32)
    anywhere = pl.BlockSpec(memory_space=pl.ANY)
    ways = plan.ways
    moving = [] if ways is None else [cotangent]
    params = {} if ways is None else {"collective_id": 1, "has_side_effects": True}
    results = kernel_call(
        functools.partial(attend_kernel, sub, ways),
        "attend",
        (pairs,),
        [
            columns(rows, 0),
            columns(length, pairs),
            columns(length, 2 * pairs),
            whole(mark_q),
            whole(mark_k),
        ]
        + [anywhere] * len(moving),
        [
            columns(rows, 0),
            pl.BlockSpec((2, rows, length), lambda t: (t, 0, 0)),
            whole(stats),
        ]
        + [anywhere] * len(moving),
        [
            jax.ShapeDtypeStruct((rows, width), BF16),
            jax.ShapeDtypeStruct((2 * pairs, rows, length), BF16),
            stats,
        ]
        + [jax.ShapeDtypeStruct(array.shape, array.dtype) for array in moving],
        [pltpu.VMEM((rows, LANES), F32)] + [pltpu.SemaphoreType.DMA((2,))] * (2 * len(moving)),
        24 * rows * length * width,
        4 * pairs * rows * length,
        **params,
    )(own, projected, projected, mark_q, mark_k, *moving)
    return tuple(results) if moving else tuple(results) + (cotangent,)


def grad_query(chances, grad, attended, projected, sub=256):
    rows, width = grad.shape
    length, pairs = projected.shape[0], width // LANES
    stats = jax.ShapeDtypeStruct((STATS, rows), F32)
    return kernel_call(
        functools.partial(grad_query_kernel, sub),
        "grad_query",
        (pairs,),
        [
            pl.BlockSpec((2, rows, length), lambda t: (t, 0, 0)),
            columns(rows, 0),
            columns(rows, 0),
            columns(length, pairs),
            columns(length, 2 * pairs),
        ],
        [columns(rows, 0), whole(stats)],
        [jax.ShapeDtypeStruct((rows, width), BF16), stats],
        [pltpu.VMEM((rows, LANES), F32)],
        16 * rows * length * width,
        4 * pairs * rows * length,
    )(chances, grad, attended, projected, projected)


def grad_key_value(own, projected, grads, log_totals, deltas, mark_k, mark_q, sub=256):
    rows, width = grads[0].shape
    pieces, pairs = len(grads), width // LANES
    length = rows * pieces
    result = jax.ShapeDtypeStruct((rows, width), BF16)
    return kernel_call(
        functools.partial(grad_key_kernel, sub, pieces),
        "grad_key_value",
        (pairs,),
        [columns(rows, pairs), columns(rows, 2 * pairs), columns(length, 0)]
        + [columns(rows, 0)] * pieces
        + [whole(log_totals[0])] * (2 * pieces)
        + [whole(mark_k), whole(mark_q)],
        [columns(rows, 0)] * 2,
        [result] * 2,
        [],
        32 * rows * length * width,
        8 * length * width,
    )(own, own, projected, *grads, *log_totals, *deltas, mark_k, mark_q)


def grad_weight_kernel(parts, index_ref, left_ref, right_ref, keep_ref, send_ref, turned):
    @pl.when(pl.program_id(0) == 0)
    def _():
        turned[...] = jnp.transpose(left_ref[...])

    total = dot_as(turned[...], right_ref[...], NN)
    rows = total.shape[0] // parts
    me = index_ref[0]
    for part in range(parts):
        place = part ^ me
        block = total[part * rows : (part + 1) * rows].astype(BF16)

        @pl.when(place % 2 == 0)
        def _():
            keep_ref[place // 2] = block

        @pl.when(place % 2 == 1)
        def _():
            send_ref[place // 2] = block


def grad_weight_wide(left, right, me, parts, tile):
    length, height = left.shape
    width = right.shape[1]
    rows = height // parts
    half = jax.ShapeDtypeStruct((parts // 2, rows, width), BF16)
    out = pl.BlockSpec((parts // 2, rows, tile), lambda n, at: (0, 0, n))
    return pl.pallas_call(
        functools.partial(grad_weight_kernel, parts),
        grid_spec=pltpu.PrefetchScalarGridSpec(
            num_scalar_prefetch=1,
            grid=(width // tile,),
            in_specs=[
                pl.BlockSpec((length, height), lambda n, at: (0, 0)),
                pl.BlockSpec((length, tile), lambda n, at: (0, n)),
            ],
            out_specs=[out, out],
            scratch_shapes=[pltpu.VMEM((height, length), BF16)],
        ),
        out_shape=[half, half],
        compiler_params=pltpu.CompilerParams(vmem_limit_bytes=VMEM_BYTES),
        cost_estimate=pl.CostEstimate(
            flops=2 * length * height * width, bytes_accessed=2 * height * width, transcendentals=0
        ),
        name="grad_weight_wide",
    )(me, left, right)


def grad_weight_tall_kernel(index_ref, left_ref, right_ref, out_ref):
    out_ref[0] = inner_rows(left_ref[...], right_ref[...]).astype(BF16)


def grad_weight_tall(left, right, me, parts):
    length, height = left.shape
    width = right.shape[1]
    rows = height // parts

    def half(which):
        return pl.pallas_call(
            grad_weight_tall_kernel,
            grid_spec=pltpu.PrefetchScalarGridSpec(
                num_scalar_prefetch=1,
                grid=(parts // 2,),
                in_specs=[
                    pl.BlockSpec((length, rows), lambda b, at: (0, (2 * b + which) ^ at[0])),
                    pl.BlockSpec((length, width), lambda b, at: (0, 0)),
                ],
                out_specs=pl.BlockSpec((1, rows, width), lambda b, at: (b, 0, 0)),
            ),
            out_shape=jax.ShapeDtypeStruct((parts // 2, rows, width), BF16),
            compiler_params=pltpu.CompilerParams(vmem_limit_bytes=VMEM_BYTES),
            cost_estimate=pl.CostEstimate(
                flops=length * height * width, bytes_accessed=height * width, transcendentals=0
            ),
            name="grad_weight_tall",
        )(me, left, right)

    return half(0), half(1)


def start_kernel(
    plane,
    place,
    tokens_ref,
    lengths_ref,
    gain_ref,
    shift_ref,
    w_ref,
    bias_ref,
    projected_ref,
    hidden_ref,
    here_ref,
    found_ref,
    rows,
    staged,
    sent,
    landed,
    out_sem,
):
    y, j, z = place_of_device()
    dp = lax.axis_index("dp")
    half = tokens_ref.shape[0] // 2
    part = half // 2
    targets, sources = routes(plane, place)
    core, across = (dp + 1 - 2 * lax.rem(dp, jnp.int32(2)), z), (
        y * 4 + lax.rem(j + 2, jnp.int32(4)),
        z,
    )
    greet(targets + sources + [core, across])

    def span(i):
        return pl.ds(pl.multiple_of(lax.rem(i, 2) * half + lax.div(i, 2) * part, part), part)

    def moved(i, h):
        at = pl.ds(h * half + (i // 2) * part, part)
        return remote(
            tokens_ref.at[at], rows.at[0, at], sent.at[0, i], landed.at[0, i], targets[h]
        )

    def lengths():
        return remote(lengths_ref, found_ref, sent.at[4, 0], landed.at[4, 0], targets[0])

    def forward(i, origin, piece, device):
        at = span(i)
        return remote(
            rows.at[origin, at], rows.at[piece, at], sent.at[piece, i], landed.at[piece, i], device
        )

    def to_hbm(piece, i):
        at = pl.ds(pl.multiple_of(piece * 2 * half + span(i).start, part), part)
        return pltpu.make_async_copy(
            staged.at[at], projected_ref.at[at], out_sem.at[piece, i]
        )

    def project(piece, i):
        at = span(i)
        values = rows[piece, at, :].astype(F32)
        hidden = layer_norm(values, gain_ref[...], shift_ref[...])[0].astype(BF16)
        out = pl.ds(pl.multiple_of(piece * 2 * half + at.start, part), part)
        staged[out, :] = (dot_as(hidden, w_ref[...], NN) + bias_ref[...]).astype(BF16)
        to_hbm(piece, i).start()
        return hidden

    for i in range(4):
        moved(i, i % 2).start()
    lengths().start()

    def first(i, carry):
        at = span(i)
        remote(
            rows.at[0, at], rows.at[0, at], sent.at[0, i], landed.at[0, i], core
        ).wait_recv()
        forward(i, 0, 2, across).start()
        forward(i, 0, 1, core).start()
        hidden_ref[at, :] = project(0, i)
        here_ref[at, :] = rows[0, at, :]
        return carry

    lax.fori_loop(0, 4, first, 0)

    def second(i, carry):
        forward(i, 0, 1, core).wait_recv()
        project(1, i)
        forward(i, 0, 2, across).wait_recv()
        forward(i, 2, 3, core).start()
        project(2, i)
        return carry

    lax.fori_loop(0, 4, second, 0)

    def third(i, carry):
        forward(i, 2, 3, core).wait_recv()
        project(3, i)
        return carry

    lax.fori_loop(0, 4, third, 0)
    lengths().wait()
    for i in range(4):
        moved(i, i % 2).wait_send()

    def last(i, carry):
        forward(i, 0, 2, across).wait_send()
        forward(i, 0, 1, core).wait_send()
        forward(i, 2, 3, core).wait_send()
        for piece in range(4):
            to_hbm(piece, i).wait()
        return carry

    lax.fori_loop(0, 4, last, 0)


def start_work(plan, tokens, clip_lengths, gain, shift, weight, bias):
    rows, width = tokens.shape
    lengths = jnp.zeros((8, LANES), jnp.int32)
    lengths = lax.dynamic_update_slice(lengths, clip_lengths, (0, 0))
    vmem, anywhere = pl.BlockSpec(memory_space=pltpu.VMEM), pl.BlockSpec(memory_space=pl.ANY)
    projected, hidden, here, found = pl.pallas_call(
        functools.partial(start_kernel, plan.PLANE, plan.PLACE),
        in_specs=[anywhere] + [vmem] * 5,
        out_specs=[anywhere, vmem, vmem, vmem],
        out_shape=[
            jax.ShapeDtypeStruct((4 * rows, 3 * width), BF16),
            jax.ShapeDtypeStruct((rows, width), BF16),
            jax.ShapeDtypeStruct((rows, width), BF16),
            jax.ShapeDtypeStruct((8, LANES), jnp.int32),
        ],
        scratch_shapes=[
            pltpu.VMEM((4, rows, width), BF16),
            pltpu.VMEM((4 * rows, 3 * width), BF16),
            pltpu.SemaphoreType.DMA((5, 4)),
            pltpu.SemaphoreType.DMA((5, 4)),
            pltpu.SemaphoreType.DMA((4, 4)),
        ],
        compiler_params=pltpu.CompilerParams(
            vmem_limit_bytes=VMEM_BYTES, collective_id=0, has_side_effects=True
        ),
        cost_estimate=pl.CostEstimate(
            flops=24 * rows * width * width, bytes_accessed=32 * rows * width, transcendentals=0
        ),
        name="start_work",
    )(tokens, lengths, gain.reshape(1, -1), shift.reshape(1, -1), weight, bias.reshape(1, -1))
    return projected, hidden, here, found[:1, : clip_lengths.shape[1]]


def added(one, other):
    return (one.astype(F32) + other.astype(F32)).astype(BF16)


class PlanePlan:
    PLANE = (0, 3, 1, 2)
    PLACE = ((1, 3, 2, 0), (2, 0, 1, 3))
    pieces = 4
    ways = (PLANE, PLACE)

    def __init__(self):
        self.there = []
        for place in self.PLACE:
            self.there.append(
                [
                    ((y * 4 + j) * 4 + z, (y * 4 + place[z]) * 4 + self.PLANE[j])
                    for y in range(2)
                    for j in range(4)
                    for z in range(4)
                ]
            )
        self.back = [[(b, a) for a, b in pairs] for pairs in self.there]

    def move(self, rows, pairs):
        half = rows.shape[0] // 2
        return jnp.concatenate(
            [
                lax.ppermute(rows[:half], ("dp", "seq"), pairs[0]),
                lax.ppermute(rows[half:], ("dp", "seq"), pairs[1]),
            ]
        )

    def to_work(self, rows):
        return self.move(rows, self.there)

    def start(self, tokens, clip_lengths, gain, shift, weight, bias):
        projected, hidden, here, lengths = start_work(
            self, tokens, clip_lengths, gain, shift, weight, bias
        )
        return projected, projected, hidden, here, lengths

    def to_home(self, rows):
        return self.move(rows, self.back)

    def gather(self, own):
        core = lax.ppermute(own, "dp", [(i, i ^ 1) for i in range(8)])
        across = lax.ppermute(own, "dp", [(i, i ^ 2) for i in range(8)])
        corner = lax.ppermute(across, "dp", [(i, i ^ 1) for i in range(8)])
        return [own, core, across, corner]

    def positions(self, rows):
        j = lax.axis_index("dp") % 4
        half = rows // 2
        sources = jnp.asarray([[place.index(p) for place in self.PLACE] for p in range(4)], jnp.int32)
        found = []
        for piece in range(4):
            shards = sources[j ^ piece]
            for part in range(2):
                start = shards[part] * rows + part * half
                found.append(start + jnp.arange(half, dtype=jnp.int32))
        return jnp.concatenate(found)

    def own(self, gathered):
        return gathered[: gathered.shape[0] // 4]

    def weight(self, left, right):
        me = lax.axis_index("dp").astype(jnp.int32).reshape(1)
        if left.shape[1] // 8 % LANES == 0:
            return grad_weight_tall(left, right, me, 8)
        tile = 384 if right.shape[1] % 384 == 0 else right.shape[1]
        return grad_weight_wide(left, right, me, 8, tile)

    def swap(self, value, bit):
        return lax.ppermute(value, "dp", [(i, i ^ bit) for i in range(8)])

    def reduce(self, halves):
        keep, send = halves
        total = added(keep, self.swap(send, 1))
        middle = total.shape[2] // 2
        first, second = total[:, :, :middle], total[:, :, middle:]
        first = added(first[0::2], self.swap(first[1::2], 2))
        second = added(second[0:2], self.swap(second[2:4], 4))
        first = added(first[0], self.swap(first[1], 4))
        second = added(second[0], self.swap(second[1], 2))
        total = jnp.concatenate([first, second], 1)
        total = added(total, lax.ppermute(total, "seq", [(0, 1), (3, 2)]))
        total = added(total, lax.ppermute(total, "seq", [(1, 2), (2, 1)]))
        ends = lax.ppermute(total, "seq", [(1, 0), (2, 3)])
        z = lax.axis_index("seq")
        return jnp.where((z == 1) | (z == 2), total, ends).astype(F32)

    def reduce_vectors(self, vectors):
        packed = jnp.concatenate(vectors)
        for bit in (1, 2, 4):
            packed = packed + self.swap(packed, bit)
        for bit in (1, 2):
            packed = packed + lax.ppermute(packed, "seq", [(i, i ^ bit) for i in range(4)])
        results, start = [], 0
        for vector in vectors:
            part = vector.shape[0] // 8
            results.append(
                lax.dynamic_slice(packed, (start + lax.axis_index("dp") * part,), (part,))
            )
            start += vector.shape[0]
        return results


class PlainPlan:
    ways = None

    def __init__(self, pieces):
        self.pieces = pieces

    def to_work(self, rows):
        return rows

    def to_home(self, rows):
        return rows

    def start(self, tokens, clip_lengths, gain, shift, weight, bias):
        hidden = layer_norm(tokens.astype(F32), gain, shift)[0].astype(BF16)
        own = (matmul(hidden, weight) + bias).astype(BF16)
        projected = lax.all_gather(own, "seq", axis=0, tiled=True)
        return projected, own, hidden, tokens, clip_lengths

    def gather(self, own):
        gathered = lax.all_gather(own, "seq", axis=0, tiled=False)
        return [gathered[i] for i in range(self.pieces)]

    def positions(self, rows):
        return jnp.arange(rows * self.pieces, dtype=jnp.int32)

    def own(self, gathered):
        rows = gathered.shape[0] // self.pieces
        return lax.dynamic_slice_in_dim(gathered, lax.axis_index("seq") * rows, rows, 0)

    def weight(self, left, right):
        return inner_rows(left, right)

    def reduce(self, total):
        return lax.psum(lax.psum_scatter(total, "dp", scatter_dimension=0, tiled=True), "seq")

    def reduce_vectors(self, vectors):
        return [self.reduce(vector) for vector in vectors]


def gelu_parts(pre_act):
    inside = 0.5 * (1.0 + lax.erf(pre_act * math.sqrt(0.5)))
    slope = inside + pre_act * jnp.exp(-0.5 * pre_act * pre_act) * (1.0 / math.sqrt(2.0 * math.pi))
    return pre_act * inside, slope


def body(
    plan,
    tokens,
    clip_lengths,
    ln1_gain,
    ln1_shift,
    w_qkv,
    bias_query,
    bias_value,
    w_out,
    bias_out,
    ln2_gain,
    ln2_shift,
    w_up,
    bias_up,
    w_down,
    bias_down,
    cotangent,
):
    rows, width = tokens.shape
    bias = jnp.concatenate([bias_query, jnp.zeros_like(bias_query), bias_value])
    projected, own, hidden1, here, lengths = plan.start(
        tokens, clip_lengths, ln1_gain, ln1_shift, w_qkv, bias
    )

    clip_ends = jnp.cumsum(lengths.reshape(-1))
    position = plan.positions(rows)
    segment = jnp.sum((position[:, None] >= clip_ends[None, :]).astype(jnp.int32), 1)
    lane = jnp.arange(LANES, dtype=jnp.int32)[None, :]
    same = lane == segment[:, None]
    mark_k = same.astype(BF16)
    mark_q = jnp.where(same | (lane >= clip_ends.shape[0]), 0.0, masked_score).astype(BF16)

    attended, chances, log_totals, grad_out = attend(
        plan, own, projected, plan.own(mark_q), mark_k, cotangent
    )
    log_totals = plan.gather(log_totals)

    inputs32 = here.astype(F32)
    middle = inputs32 + matmul(attended, w_out) + bias_out
    normed2_out, normed2, inverse2 = layer_norm(middle, ln2_gain, ln2_shift)
    hidden2 = normed2_out.astype(BF16)
    upper = matmul(hidden2, w_up) + bias_up
    activated, slope = gelu_parts(upper)
    activated = activated.astype(BF16)
    grad_upper = (inner_cols(grad_out, w_down) * slope).astype(BF16)
    grad_hidden2 = inner_cols(grad_upper, w_up)
    grad_norm2, grad_ln2_gain, grad_ln2_shift = norm_back(grad_hidden2, normed2, inverse2, ln2_gain)
    grad_middle = grad_out.astype(F32) + grad_norm2
    grad_branch = grad_middle.astype(BF16)
    grad_attended = inner_cols(grad_branch, w_out).astype(BF16)
    grads = plan.gather(grad_attended)

    block_out = (middle + matmul(activated, w_down) + bias_down).astype(BF16)
    block_out = plan.to_home(block_out)
    grad_w_down = plan.reduce(plan.weight(activated, grad_out))
    grad_w_up = plan.reduce(plan.weight(hidden2, grad_upper))
    grad_w_out = plan.reduce(plan.weight(attended, grad_branch))
    grad_bias_down = jnp.sum(grad_out.astype(F32), 0)
    grad_bias_up = jnp.sum(grad_upper.astype(F32), 0)
    grad_bias_out = jnp.sum(grad_branch.astype(F32), 0)
    grad_bias_down, grad_bias_up, grad_bias_out, grad_ln2_gain, grad_ln2_shift = (
        plan.reduce_vectors(
            [grad_bias_down, grad_bias_up, grad_bias_out, grad_ln2_gain, grad_ln2_shift]
        )
    )

    dq, deltas = grad_query(chances, grad_attended, attended, projected)
    deltas = plan.gather(deltas)
    dk, dv = grad_key_value(
        own, projected, grads, log_totals, deltas, plan.own(mark_k), mark_q
    )
    grad_projected = jnp.concatenate([dq, dk, dv], 1)
    grad_w_qkv = plan.reduce(plan.weight(hidden1, grad_projected))
    grad_bias_query = jnp.sum(dq.astype(F32), 0)
    grad_bias_value = jnp.sum(dv.astype(F32), 0)
    grad_hidden1 = inner_cols(grad_projected, w_qkv)
    _, normed1, inverse1 = layer_norm(inputs32, ln1_gain, ln1_shift)
    grad_norm1, grad_ln1_gain, grad_ln1_shift = norm_back(grad_hidden1, normed1, inverse1, ln1_gain)
    grad_tokens = plan.to_home((grad_middle + grad_norm1).astype(BF16))
    grad_bias_query, grad_bias_value, grad_ln1_gain, grad_ln1_shift = plan.reduce_vectors(
        [grad_bias_query, grad_bias_value, grad_ln1_gain, grad_ln1_shift]
    )
    return (
        block_out,
        grad_tokens,
        grad_ln1_gain,
        grad_ln1_shift,
        grad_w_qkv,
        grad_bias_query,
        grad_bias_value,
        grad_w_out,
        grad_bias_out,
        grad_ln2_gain,
        grad_ln2_shift,
        grad_w_up,
        grad_bias_up,
        grad_w_down,
        grad_bias_down,
    )


def solution(mesh):
    sizes = dict(mesh.shape)
    plan = PlanePlan() if sizes == {"dp": 8, "seq": 4} else PlainPlan(sizes["seq"])
    rows = P(("dp", "seq"), None)
    return jax.shard_map(
        functools.partial(body, plan),
        mesh=mesh,
        in_specs=(rows, P("dp", None)) + (P(),) * 13 + (rows,),
        out_specs=(
            rows,
            rows,
            P("dp"),
            P("dp"),
            P("dp", None),
            P("dp"),
            P("dp"),
            P("dp", None),
            P("dp"),
            P("dp"),
            P("dp"),
            P("dp", None),
            P("dp"),
            P("dp", None),
            P("dp"),
        ),
        check_vma=False,
    )
```

```python
import functools
import math

import jax
import jax.numpy as jnp
from jax import lax
from jax.experimental import pallas as pl
from jax.experimental.pallas import tpu as pltpu
from jax.sharding import PartitionSpec as P

HDIM = 64
LANES = 128
STATS = 16
F32 = jnp.float32
BF16 = jnp.bfloat16
VMEM_BYTES = 56 << 20
NT = (((1,), (1,)), ((), ()))
NN = (((1,), (0,)), ((), ()))

epsilon = 1e-06
masked_score = -1e30


def dot_as(left, right, dims):
    return lax.dot_general(left, right, dims, preferred_element_type=F32)


def matmul(left, right):
    return dot_as(left, right, NN)


def inner_rows(left, right):
    return dot_as(left, right, (((0,), (0,)), ((), ())))


def inner_cols(left, right):
    return dot_as(left, right, NT)


def layer_norm(values, gain, shift):
    center = values - jnp.mean(values, -1, keepdims=True)
    inverse = lax.rsqrt(jnp.mean(center * center, -1, keepdims=True) + epsilon)
    normed = center * inverse
    return (normed * gain + shift, normed, inverse)


def norm_back(grad_out, normed, inverse, gain):
    scaled = grad_out * gain
    grad_in = inverse * (
        scaled
        - jnp.mean(scaled, -1, keepdims=True)
        - normed * jnp.mean(scaled * normed, -1, keepdims=True)
    )
    return (grad_in, jnp.sum(grad_out * normed, 0), jnp.sum(grad_out, 0))


def neighbours():
    dp, z = lax.axis_index("dp"), lax.axis_index("seq")
    other = dp + 1 - 2 * lax.rem(dp, jnp.int32(2))
    pair = z + 1 - 2 * lax.rem(z, jnp.int32(2))
    return (other, z), (dp, pair), (other, lax.rem(z + 2, jnp.int32(4)))


def stays():
    dp, z = lax.axis_index("dp"), lax.axis_index("seq")
    return lax.rem(dp, jnp.int32(2)) == lax.div(z, jnp.int32(2))


def greet(devices):
    barrier = pltpu.get_barrier_semaphore()
    for device in devices:
        pl.semaphore_signal(barrier, inc=1, device_id=device, device_id_type=pl.DeviceIdType.MESH)
    pl.semaphore_wait(barrier, len(devices))


def remote(source, target, sent, landed, device):
    return pltpu.make_async_remote_copy(
        src_ref=source,
        dst_ref=target,
        send_sem=sent,
        recv_sem=landed,
        device_id=device,
        device_id_type=pl.DeviceIdType.MESH,
    )


def move_start(source, target, sent, landed):
    swap = neighbours()[2]

    @pl.when(stays())
    def _():
        pltpu.make_async_copy(source, target, landed).start()

    @pl.when(jnp.logical_not(stays()))
    def _():
        remote(source, target, sent, landed, swap).start()


def move_landed(source, target, sent, landed):
    swap = neighbours()[2]

    @pl.when(stays())
    def _():
        pltpu.make_async_copy(source, target, landed).wait()

    @pl.when(jnp.logical_not(stays()))
    def _():
        remote(source, target, sent, landed, swap).wait_recv()


def move_sent(source, target, sent, landed):
    swap = neighbours()[2]

    @pl.when(jnp.logical_not(stays()))
    def _():
        remote(source, target, sent, landed, swap).wait_send()


def head_lanes(rows, head):
    lane = lax.broadcasted_iota(jnp.int32, (rows, LANES), 1)
    return (lane < HDIM) if head == 0 else (lane >= HDIM)


def place_stats(stat, rows, pair, values):
    lane = lax.broadcasted_iota(jnp.int32, (values[0].shape[0], LANES), 1)
    old = stat[rows, :]
    stat[rows, :] = jnp.where(
        lane == 2 * pair, values[0], jnp.where(lane == 2 * pair + 1, values[1], old)
    )


def attend_kernel(sub, ways, q_ref, k_ref, v_ref, mark_q, mark_k, *refs):
    pair = pl.program_id(0)
    if ways is None:
        out_ref, chance_ref, lse_ref, stat = refs
    else:
        home_ref, out_ref, chance_ref, lse_ref, here_ref, stat, sent, landed = refs
        move = (home_ref, here_ref, sent, landed)

        @pl.when(pair == 0)
        def _():
            greet([neighbours()[2]])
            move_start(*move)

    keys = jnp.concatenate([k_ref[...], mark_k[...]], 1)
    values = v_ref[...]

    def step(i, carry):
        rows = pl.ds(pl.multiple_of(i * sub, sub), sub)
        query = q_ref[rows, :] * jnp.asarray(1.0 / math.sqrt(HDIM), BF16)
        outs, totals = [], []
        for head in range(2):
            own = jnp.where(head_lanes(sub, head), query, jnp.zeros_like(query))
            scores = dot_as(jnp.concatenate([own, mark_q[rows, :]], 1), keys, NT)
            highest = jnp.max(scores, -1, keepdims=True)
            powers = jnp.exp(scores - highest)
            total = jnp.sum(powers, -1, keepdims=True)
            chances = (powers * (1.0 / total)).astype(BF16)
            chance_ref[head, rows, :] = chances
            outs.append(dot_as(chances, values, NN))
            totals.append(highest + jnp.log(total))
        out_ref[rows, :] = jnp.where(head_lanes(sub, 0), outs[0], outs[1]).astype(BF16)
        place_stats(stat, rows, pair, totals)
        return carry

    lax.fori_loop(0, q_ref.shape[0] // sub, step, 0)

    @pl.when(pair == pl.num_programs(0) - 1)
    def _():
        lse_ref[...] = jnp.transpose(stat[...])[:STATS]
        if ways is not None:
            move_landed(*move)
            move_sent(*move)


def grad_query_kernel(
    sub, chance_ref, grad_ref, out_ref, k_ref, v_ref, dq_ref, delta_ref, stat
):
    pair = pl.program_id(0)
    keys, values = k_ref[...], v_ref[...]

    def step(i, carry):
        rows = pl.ds(pl.multiple_of(i * sub, sub), sub)
        grad = grad_ref[rows, :]
        product = grad.astype(F32) * out_ref[rows, :].astype(F32)
        outs, deltas = [], []
        for head in range(2):
            own = head_lanes(sub, head)
            delta = jnp.sum(jnp.where(own, product, 0.0), -1, keepdims=True)
            grad_chances = dot_as(jnp.where(own, grad, jnp.zeros_like(grad)), values, NT)
            scores = (chance_ref[head, rows, :].astype(F32) * (grad_chances - delta)).astype(BF16)
            outs.append(dot_as(scores, keys, NN))
            deltas.append(delta)
        both = jnp.where(head_lanes(sub, 0), outs[0], outs[1])
        dq_ref[rows, :] = (both * (1.0 / math.sqrt(HDIM))).astype(BF16)
        place_stats(stat, rows, pair, deltas)
        return carry

    lax.fori_loop(0, grad_ref.shape[0] // sub, step, 0)

    @pl.when(pair == pl.num_programs(0) - 1)
    def _():
        delta_ref[...] = jnp.transpose(stat[...])[:STATS]


def grad_key_kernel(sub, pieces, k_ref, v_ref, q_ref, *refs):
    g_refs = refs[:pieces]
    lse_refs, delta_refs = refs[pieces : 2 * pieces], refs[2 * pieces : 3 * pieces]
    mark_k, mark_q, dk_ref, dv_ref = refs[3 * pieces :]
    pair = pl.program_id(0)
    queries = q_ref[...]
    grads = jnp.concatenate([ref[...] for ref in g_refs], 0)
    scaled = jnp.concatenate(
        [queries * jnp.asarray(1.0 / math.sqrt(HDIM), BF16), mark_q[...]], 1
    )

    def stats(which, head):
        return jnp.concatenate([ref[pl.ds(2 * pair + head, 1), :] for ref in which], 1)

    log_totals = [stats(lse_refs, head) for head in range(2)]
    deltas = [stats(delta_refs, head) for head in range(2)]

    def step(i, carry):
        rows = pl.ds(pl.multiple_of(i * sub, sub), sub)
        key, value = k_ref[rows, :], v_ref[rows, :]
        dks, dvs = [], []
        for head in range(2):
            own = head_lanes(sub, head)
            key_own = jnp.where(own, key, jnp.zeros_like(key))
            value_own = jnp.where(own, value, jnp.zeros_like(value))
            scores = dot_as(jnp.concatenate([key_own, mark_k[rows, :]], 1), scaled, NT)
            chances = jnp.exp(scores - log_totals[head])
            grad_chances = dot_as(value_own, grads, NT)
            grad_scores = (chances * (grad_chances - deltas[head])).astype(BF16)
            dvs.append(dot_as(chances.astype(BF16), grads, NN))
            dks.append(dot_as(grad_scores, queries, NN))
        first = head_lanes(sub, 0)
        dk = jnp.where(first, dks[0], dks[1]) * (1.0 / math.sqrt(HDIM))
        dk_ref[rows, :] = dk.astype(BF16)
        dv_ref[rows, :] = jnp.where(first, dvs[0], dvs[1]).astype(BF16)
        return carry

    lax.fori_loop(0, k_ref.shape[0] // sub, step, 0)


def columns(rows, first):
    return pl.BlockSpec((rows, LANES), lambda t: (0, first + t))


def whole(array):
    return pl.BlockSpec(array.shape, lambda t: (0,) * array.ndim)


def kernel_call(kernel, name, grid, in_specs, out_specs, out_shape, scratch, flops, moved, **params):
    return pl.pallas_call(
        kernel,
        grid=grid,
        in_specs=in_specs,
        out_specs=out_specs,
        out_shape=out_shape,
        scratch_shapes=scratch,
        compiler_params=pltpu.CompilerParams(vmem_limit_bytes=VMEM_BYTES, **params),
        cost_estimate=pl.CostEstimate(flops=flops, bytes_accessed=moved, transcendentals=0),
        name=name,
    )


def attend(plan, own, projected, mark_q, mark_k, cotangent, sub=256):
    rows, width = mark_q.shape[0], own.shape[1] // 3
    length, pairs = projected.shape[0], width // LANES
    stats = jax.ShapeDtypeStruct((STATS, rows), F32)
    anywhere = pl.BlockSpec(memory_space=pl.ANY)
    ways = plan.ways
    moving = [] if ways is None else [cotangent]
    params = {} if ways is None else {"collective_id": 1, "has_side_effects": True}
    results = kernel_call(
        functools.partial(attend_kernel, sub, ways),
        "attend",
        (pairs,),
        [
            columns(rows, 0),
            columns(length, pairs),
            columns(length, 2 * pairs),
            whole(mark_q),
            whole(mark_k),
        ]
        + [anywhere] * len(moving),
        [
            columns(rows, 0),
            pl.BlockSpec((2, rows, length), lambda t: (t, 0, 0)),
            whole(stats),
        ]
        + [anywhere] * len(moving),
        [
            jax.ShapeDtypeStruct((rows, width), BF16),
            jax.ShapeDtypeStruct((2 * pairs, rows, length), BF16),
            stats,
        ]
        + [jax.ShapeDtypeStruct(array.shape, array.dtype) for array in moving],
        [pltpu.VMEM((rows, LANES), F32)] + [pltpu.SemaphoreType.DMA] * (2 * len(moving)),
        24 * rows * length * width,
        4 * pairs * rows * length,
        **params,
    )(own, projected, projected, mark_q, mark_k, *moving)
    return tuple(results) if moving else tuple(results) + (cotangent,)


def grad_query(chances, grad, attended, projected, sub=256):
    rows, width = grad.shape
    length, pairs = projected.shape[0], width // LANES
    stats = jax.ShapeDtypeStruct((STATS, rows), F32)
    return kernel_call(
        functools.partial(grad_query_kernel, sub),
        "grad_query",
        (pairs,),
        [
            pl.BlockSpec((2, rows, length), lambda t: (t, 0, 0)),
            columns(rows, 0),
            columns(rows, 0),
            columns(length, pairs),
            columns(length, 2 * pairs),
        ],
        [columns(rows, 0), whole(stats)],
        [jax.ShapeDtypeStruct((rows, width), BF16), stats],
        [pltpu.VMEM((rows, LANES), F32)],
        16 * rows * length * width,
        4 * pairs * rows * length,
    )(chances, grad, attended, projected, projected)


def grad_key_value(own, projected, grads, log_totals, deltas, mark_k, mark_q, sub=256):
    rows, width = grads[0].shape
    pieces, pairs = len(grads), width // LANES
    length = rows * pieces
    result = jax.ShapeDtypeStruct((rows, width), BF16)
    return kernel_call(
        functools.partial(grad_key_kernel, sub, pieces),
        "grad_key_value",
        (pairs,),
        [columns(rows, pairs), columns(rows, 2 * pairs), columns(length, 0)]
        + [columns(rows, 0)] * pieces
        + [whole(log_totals[0])] * (2 * pieces)
        + [whole(mark_k), whole(mark_q)],
        [columns(rows, 0)] * 2,
        [result] * 2,
        [],
        32 * rows * length * width,
        8 * length * width,
    )(own, own, projected, *grads, *log_totals, *deltas, mark_k, mark_q)


class Chunk:
    def __init__(self, index, source, rows, columns, y_first):
        self.index, self.source, self.rows, self.columns = index, source, rows, columns
        self.shape = (rows[1], columns[1])
        self.blocks = ((2, 3), 1) if y_first else ((1, 3), 2)
        self.y_first = y_first

    def scratch(self):
        rows, columns = self.shape
        return [
            pltpu.VMEM((4, rows, columns), BF16),
            pltpu.VMEM((4, rows, columns), BF16),
            pltpu.VMEM((2, rows, columns), BF16),
            pltpu.VMEM((rows, columns), BF16),
            pltpu.VMEM((rows, columns), BF16),
            pltpu.VMEM((rows, columns), BF16),
            pltpu.VMEM((rows, columns), BF16),
            pltpu.SemaphoreType.DMA((8,)),
            pltpu.SemaphoreType.DMA((8,)),
        ]

    def bind(self, keep_refs, send_refs, out_refs, scratch, devices):
        at = (pl.ds(*self.rows), pl.ds(*self.columns))
        whole = (pl.ds(0, 4),) + at
        keep_hbm = keep_refs[self.source].at[whole]
        send_hbm = send_refs[self.source].at[whole]
        self.out = out_refs[self.source].at[at]
        (self.keep, core, first, second, self.z1, self.z2, self.z3, sent, landed) = scratch
        near, far = (devices["y"], devices["x"]) if self.y_first else (devices["x"], devices["y"])
        self.core, self.first, self.second = core, first, second
        sends, last = self.blocks
        self.load = pltpu.make_async_copy(keep_hbm, self.keep, landed.at[7])
        self.to_core = remote(send_hbm, core, sent.at[0], landed.at[0], devices["core"])
        self.to_near = [
            remote(self.keep.at[b], first.at[i], sent.at[1 + i], landed.at[1 + i], near)
            for i, b in enumerate(sends)
        ]
        self.to_far = remote(self.keep.at[last], second, sent.at[3], landed.at[3], far)
        self.inward = remote(self.keep.at[0], self.z1, sent.at[4], landed.at[4], devices["pair"])
        self.middle = remote(self.keep.at[0], self.z2, sent.at[5], landed.at[5], devices["mirror"])
        self.outward = remote(self.z1, self.z3, sent.at[6], landed.at[6], devices["pair"])

    def add(self, target, source):
        def step(i, carry):
            at = pl.ds(pl.multiple_of(i * 16, 16), 16)
            target[at, :] = added(target[at, :], source[at, :])
            return carry

        lax.fori_loop(0, self.shape[0] // 16, step, 0)

    def start(self):
        self.to_core.start()
        self.load.start()

    def near(self):
        self.load.wait()
        self.to_core.wait_recv()
        for block in range(4):
            self.add(self.keep.at[block], self.core.at[block])
        for copy in self.to_near:
            copy.start()

    def far(self):
        stay = [b for b in range(4) if b not in self.blocks[0]]
        for i, copy in enumerate(self.to_near):
            copy.wait_recv()
            self.add(self.keep.at[stay[i]], self.first.at[i])
        self.to_far.start()

    def along(self):
        self.to_far.wait_recv()
        self.add(self.keep.at[0], self.second)

        @pl.when(jnp.logical_not(inner()))
        def _():
            self.inward.start()

    def meet(self):
        @pl.when(inner())
        def _():
            self.inward.wait_recv()
            self.add(self.keep.at[0], self.z1)
            self.middle.start()

    def spread(self):
        @pl.when(inner())
        def _():
            self.middle.wait_recv()

            def step(i, carry):
                at = pl.ds(pl.multiple_of(i * 16, 16), 16)
                total = added(self.keep[0, at, :], self.z2[at, :])
                self.z1[at, :] = total
                self.out[at, :] = total.astype(F32)
                return carry

            lax.fori_loop(0, self.shape[0] // 16, step, 0)
            self.outward.start()

    def finish(self):
        @pl.when(jnp.logical_not(inner()))
        def _():
            self.outward.wait_recv()

            def step(i, carry):
                at = pl.ds(pl.multiple_of(i * 16, 16), 16)
                self.out[at, :] = self.z3[at, :].astype(F32)
                return carry

            lax.fori_loop(0, self.shape[0] // 16, step, 0)
            self.inward.wait_send()

        @pl.when(inner())
        def _():
            self.middle.wait_send()
            self.outward.wait_send()

        self.to_core.wait_send()
        for copy in self.to_near:
            copy.wait_send()
        self.to_far.wait_send()


def inner():
    z = lax.axis_index("seq")
    return jnp.logical_and(z > 0, z < 3)


def ring_devices():
    dp, z = lax.axis_index("dp"), lax.axis_index("seq")
    core, pair, swap = neighbours()
    x = dp + 2 - 4 * lax.rem(lax.div(dp, jnp.int32(2)), jnp.int32(2))
    y = dp + 4 - 8 * lax.div(dp, jnp.int32(4))
    return {
        "core": core,
        "pair": pair,
        "swap": swap,
        "x": (x, z),
        "y": (y, z),
        "mirror": (dp, 3 - z),
    }


def backward_chunks(shapes):
    found = []
    for source, y_first, count in ((0, True, 3), (1, False, 3), (2, True, 1)):
        _, rows, columns = shapes[source]
        for part in range(count):
            if source == 0:
                size = rows // count
                found.append((part, source, (part * size, size), (0, columns), y_first))
            else:
                size = columns // count
                found.append((part, source, (0, rows), (part * size, size), y_first))
    found.sort(key=lambda chunk: (chunk[0] if chunk[1] < 2 else 3, chunk[1]))
    return [Chunk(i, *chunk[1:]) for i, chunk in enumerate(found)]


def backward_kernel(
    shapes,
    pairs,
    chance_ref,
    grad_ref,
    attended_ref,
    k_ref,
    v_ref,
    q_ref,
    mark_k,
    mark_q,
    lse_ref,
    keep_down,
    send_down,
    keep_up,
    send_up,
    keep_out,
    send_out,
    block_ref,
    dq_ref,
    dk_ref,
    dv_ref,
    down_ref,
    up_ref,
    out_ref,
    home_ref,
    grads,
    stats,
    own_stats,
    sent,
    landed,
    *scratch,
):
    step = pl.program_id(0)
    rows, width = grad_ref.shape
    half = rows // 2
    devices = ring_devices()
    chunks = backward_chunks(shapes)
    per = len(scratch) // len(chunks)
    for chunk in chunks:
        chunk.bind(
            (keep_down, keep_up, keep_out),
            (send_down, send_up, send_out),
            (down_ref, up_ref, out_ref),
            scratch[chunk.index * per : (chunk.index + 1) * per],
            devices,
        )
    move = (block_ref, home_ref, sent.at[12], landed.at[12])

    def grad_copy(i, part, source, device):
        at = pl.ds(part * half, half)
        n = 2 * i + part
        return remote(source.at[at], grads.at[i, at], sent.at[n], landed.at[n], device)

    def to_core(part):
        return grad_copy(1, part, grad_ref, devices["core"])

    def to_pair(part):
        return grad_copy(2, part, grad_ref, devices["pair"])

    def to_corner(part):
        return grad_copy(3, part, grads.at[2], devices["core"])

    def stat_copy(i, source, device):
        return remote(source, stats.at[i], sent.at[8 + i], landed.at[8 + i], device)

    stat_core = stat_copy(1, own_stats, devices["core"])
    stat_pair = stat_copy(2, own_stats, devices["pair"])
    stat_corner = stat_copy(3, stats.at[2], devices["core"])

    def begin():
        greet(list(devices.values()))
        for part in range(2):
            to_pair(part).start()
        for part in range(2):
            to_core(part).start()
        product = grad_ref[...].astype(F32) * attended_ref[...].astype(F32)
        high = product.astype(BF16)
        low = (product - high.astype(F32)).astype(BF16)
        head = lax.broadcasted_iota(jnp.int32, (STATS, width), 0)
        column = lax.broadcasted_iota(jnp.int32, (STATS, width), 1)
        mine = jnp.where(
            jnp.logical_and(column >= head * HDIM, column < (head + 1) * HDIM), 1.0, 0.0
        ).astype(BF16)
        own_stats[0:STATS, :] = lse_ref[...]
        own_stats[STATS:, :] = dot_as(mine, high, NT) + dot_as(mine, low, NT)
        stats[0] = own_stats[...]
        grads[0] = grad_ref[...]
        stat_pair.start()
        stat_core.start()

    def corner_stats():
        stat_pair.wait_recv()
        stat_corner.start()

    def corner(part):
        def run():
            to_pair(part).wait_recv()
            to_corner(part).start()

        return run

    def all_grads():
        stat_core.wait_recv()
        stat_corner.wait_recv()
        for part in range(2):
            to_core(part).wait_recv()
            to_corner(part).wait_recv()

    events = {0: [begin], 2: [corner_stats], 4: [corner(0)], pairs: [corner(1), all_grads]}

    def plan(at, *methods):
        events.setdefault(at, []).extend(methods)

    plan(0, *[chunk.start for chunk in chunks])
    plan(pairs, lambda: move_start(*move))
    when = {
        0: (1, 5, 7, 9, 11, 13),
        1: (1, 5, 7, 9, 11, 13),
        2: (3, 8, 10, 12, 14, 16),
        3: (3, 8, 10, 12, 14, 16),
        4: (6, 12, 14, 16, 17, 18),
        5: (6, 12, 14, 16, 17, 18),
        6: (8, 13, 15, 17, 18, 18),
    }
    for number, stage in enumerate(("near", "far", "along", "meet", "spread", "finish")):
        for chunk in chunks:
            plan(when[chunk.index][number], getattr(chunk, stage))

    def end():
        move_landed(*move)
        move_sent(*move)
        stat_core.wait_send()
        stat_pair.wait_send()
        stat_corner.wait_send()
        for part in range(2):
            to_core(part).wait_send()
            to_pair(part).wait_send()
            to_corner(part).wait_send()

    steps = 3 * pairs
    plan(steps, end)
    for at in range(steps):
        if at in events:

            @pl.when(step == at)
            def _():
                for event in events[at]:
                    event()

    @pl.when(step < pairs)
    def _():
        query_grads(chance_ref, grad_ref, attended_ref, k_ref, v_ref, dq_ref, step)

    @pl.when(step >= pairs)
    def _():
        pair = lax.rem(step, jnp.int32(pairs))
        first = (lax.div(step, jnp.int32(pairs)) - 1) * half
        at = pl.ds(pl.multiple_of(first, half), half)
        tile = pl.ds(pl.multiple_of(pair * LANES, LANES), LANES)

        def stat(row):
            return jnp.concatenate([stats[i, pl.ds(row, 1), :] for i in range(4)], 1)

        dk, dv = key_grads(
            k_ref[at, :],
            v_ref[at, :],
            mark_k[at, :],
            q_ref[...],
            jnp.concatenate([grads[i, :, tile] for i in range(4)], 0),
            mark_q[...],
            [stat(2 * pair + head) for head in range(2)],
            [stat(STATS + 2 * pair + head) for head in range(2)],
        )
        dk_ref[...] = dk
        dv_ref[...] = dv

    @pl.when(step == steps - 1)
    def _():
        for event in events[steps]:
            event()


def query_grads(chance_ref, grad_ref, out_ref, k_ref, v_ref, dq_ref, pair, sub=256):
    keys, values = k_ref[...], v_ref[...]
    tile = pl.ds(pl.multiple_of(pair * LANES, LANES), LANES)

    def step(i, carry):
        rows = pl.ds(pl.multiple_of(i * sub, sub), sub)
        grad = grad_ref[rows, tile]
        product = grad.astype(F32) * out_ref[rows, tile].astype(F32)
        outs = []
        for head in range(2):
            own = head_lanes(sub, head)
            delta = jnp.sum(jnp.where(own, product, 0.0), -1, keepdims=True)
            grad_chances = dot_as(jnp.where(own, grad, jnp.zeros_like(grad)), values, NT)
            scores = (chance_ref[head, rows, :].astype(F32) * (grad_chances - delta)).astype(BF16)
            outs.append(dot_as(scores, keys, NN))
        both = jnp.where(head_lanes(sub, 0), outs[0], outs[1])
        dq_ref[rows, :] = (both * (1.0 / math.sqrt(HDIM))).astype(BF16)
        return carry

    lax.fori_loop(0, dq_ref.shape[0] // sub, step, 0)


def key_grads(key, value, mark_k, queries, grads, mark_q, log_totals, deltas):
    scaled = jnp.concatenate([queries * jnp.asarray(1.0 / math.sqrt(HDIM), BF16), mark_q], 1)
    dks, dvs = [], []
    for head in range(2):
        own = head_lanes(key.shape[0], head)
        key_own = jnp.where(own, key, jnp.zeros_like(key))
        value_own = jnp.where(own, value, jnp.zeros_like(value))
        scores = dot_as(jnp.concatenate([key_own, mark_k], 1), scaled, NT)
        chances = jnp.exp(scores - log_totals[head])
        grad_chances = dot_as(value_own, grads, NT)
        grad_scores = (chances * (grad_chances - deltas[head])).astype(BF16)
        dvs.append(dot_as(chances.astype(BF16), grads, NN))
        dks.append(dot_as(grad_scores, queries, NN))
    first = head_lanes(key.shape[0], 0)
    dk = jnp.where(first, dks[0], dks[1]) * (1.0 / math.sqrt(HDIM))
    return dk.astype(BF16), jnp.where(first, dvs[0], dvs[1]).astype(BF16)


def backward(chances, grad, attended, projected, mark_k, mark_q, log_totals, halves, block_out):
    rows, width = grad.shape
    length, pairs = projected.shape[0], width // LANES
    shapes = [keep.shape for keep, _ in halves]
    anywhere = pl.BlockSpec(memory_space=pl.ANY)
    result = jax.ShapeDtypeStruct((rows, width), BF16)
    reduced = [jax.ShapeDtypeStruct(shape[1:], F32) for shape in shapes]

    def once(array):
        return pl.BlockSpec(
            array.shape, lambda t: (0,) * array.ndim, pipeline_mode=pl.Buffered(1)
        )

    def tile(first):
        return pl.BlockSpec((length, LANES), lambda t: (0, first + lax.rem(t, pairs)))

    late = pl.BlockSpec(
        (rows // 2, LANES),
        lambda t: (jnp.maximum(lax.div(t, pairs) - 1, 0), jnp.maximum(t - pairs, 0) % pairs),
    )
    chunks = backward_chunks(shapes)
    stats = (2 * STATS, rows)
    return kernel_call(
        functools.partial(backward_kernel, shapes, pairs),
        "backward",
        (3 * pairs,),
        [
            pl.BlockSpec((2, rows, length), lambda t: (jnp.minimum(t, pairs - 1), 0, 0)),
            once(grad),
            once(attended),
            tile(pairs),
            tile(2 * pairs),
            pl.BlockSpec((length, LANES), lambda t: (0, jnp.maximum(t - pairs, 0) % pairs)),
            once(mark_k),
            once(mark_q),
            once(log_totals),
        ]
        + [anywhere] * (2 * len(halves) + 1),
        [pl.BlockSpec((rows, LANES), lambda t: (0, jnp.minimum(t, pairs - 1))), late, late]
        + [once(shape) for shape in reduced]
        + [anywhere],
        [result] * 3 + reduced + [result],
        [
            pltpu.VMEM((4, rows, width), BF16),
            pltpu.VMEM((4,) + stats, F32),
            pltpu.VMEM(stats, F32),
            pltpu.SemaphoreType.DMA((13,)),
            pltpu.SemaphoreType.DMA((13,)),
        ]
        + [entry for chunk in chunks for entry in chunk.scratch()],
        48 * rows * length * width,
        4 * pairs * rows * length,
        collective_id=2,
        has_side_effects=True,
    )(
        chances,
        grad,
        attended,
        projected,
        projected,
        projected,
        mark_k,
        mark_q,
        log_totals,
        *[array for pair in halves for array in pair],
        block_out,
    )


def grad_weight_kernel(parts, index_ref, left_ref, right_ref, keep_ref, send_ref, turned):
    @pl.when(pl.program_id(0) == 0)
    def _():
        turned[...] = jnp.transpose(left_ref[...])

    total = dot_as(turned[...], right_ref[...], NN)
    rows = total.shape[0] // parts
    me = index_ref[0]
    for part in range(parts):
        place = part ^ me
        block = total[part * rows : (part + 1) * rows].astype(BF16)

        @pl.when(place % 2 == 0)
        def _():
            keep_ref[place // 2] = block

        @pl.when(place % 2 == 1)
        def _():
            send_ref[place // 2] = block


def grad_weight_wide(left, right, me, parts, tile):
    length, height = left.shape
    width = right.shape[1]
    rows = height // parts
    half = jax.ShapeDtypeStruct((parts // 2, rows, width), BF16)
    out = pl.BlockSpec((parts // 2, rows, tile), lambda n, at: (0, 0, n))
    return pl.pallas_call(
        functools.partial(grad_weight_kernel, parts),
        grid_spec=pltpu.PrefetchScalarGridSpec(
            num_scalar_prefetch=1,
            grid=(width // tile,),
            in_specs=[
                pl.BlockSpec((length, height), lambda n, at: (0, 0)),
                pl.BlockSpec((length, tile), lambda n, at: (0, n)),
            ],
            out_specs=[out, out],
            scratch_shapes=[pltpu.VMEM((height, length), BF16)],
        ),
        out_shape=[half, half],
        compiler_params=pltpu.CompilerParams(vmem_limit_bytes=VMEM_BYTES),
        cost_estimate=pl.CostEstimate(
            flops=2 * length * height * width, bytes_accessed=2 * height * width, transcendentals=0
        ),
        name="grad_weight_wide",
    )(me, left, right)


def grad_weight_tall_kernel(index_ref, left_ref, right_ref, out_ref):
    out_ref[0] = inner_rows(left_ref[...], right_ref[...]).astype(BF16)


def grad_weight_tall(left, right, me, parts):
    length, height = left.shape
    width = right.shape[1]
    rows = height // parts

    def half(which):
        return pl.pallas_call(
            grad_weight_tall_kernel,
            grid_spec=pltpu.PrefetchScalarGridSpec(
                num_scalar_prefetch=1,
                grid=(parts // 2,),
                in_specs=[
                    pl.BlockSpec((length, rows), lambda b, at: (0, (2 * b + which) ^ at[0])),
                    pl.BlockSpec((length, width), lambda b, at: (0, 0)),
                ],
                out_specs=pl.BlockSpec((1, rows, width), lambda b, at: (b, 0, 0)),
            ),
            out_shape=jax.ShapeDtypeStruct((parts // 2, rows, width), BF16),
            compiler_params=pltpu.CompilerParams(vmem_limit_bytes=VMEM_BYTES),
            cost_estimate=pl.CostEstimate(
                flops=length * height * width, bytes_accessed=height * width, transcendentals=0
            ),
            name="grad_weight_tall",
        )(me, left, right)

    return half(0), half(1)


def start_kernel(
    tokens_ref,
    lengths_ref,
    gain_ref,
    shift_ref,
    w_ref,
    bias_ref,
    projected_ref,
    hidden_ref,
    here_ref,
    found_ref,
    rows,
    staged,
    sent,
    landed,
    out_sem,
):
    core, across, swap = neighbours()
    parts = sent.shape[1]
    height = tokens_ref.shape[0]
    part = height // parts
    greet([core, across, swap])

    def span(i):
        return pl.ds(pl.multiple_of(i * part, part), part)

    def moved(i):
        return (tokens_ref.at[span(i)], rows.at[0, span(i)], sent.at[0, i], landed.at[0, i])

    def lengths():
        return remote(lengths_ref, found_ref, sent.at[4, 0], landed.at[4, 0], core)

    def forward(i, origin, piece, device):
        return remote(
            rows.at[origin, span(i)],
            rows.at[piece, span(i)],
            sent.at[piece, i],
            landed.at[piece, i],
            device,
        )

    def out_span(piece, i):
        return pl.ds(pl.multiple_of(piece * height + i * part, part), part)

    def to_hbm(piece, i):
        at = out_span(piece, i)
        return pltpu.make_async_copy(staged.at[at], projected_ref.at[at], out_sem.at[piece, i])

    def project(piece, i):
        values = rows[piece, span(i), :].astype(F32)
        hidden = layer_norm(values, gain_ref[...], shift_ref[...])[0].astype(BF16)
        staged[out_span(piece, i), :] = (
            dot_as(hidden, w_ref[...], NN) + bias_ref[...]
        ).astype(BF16)
        to_hbm(piece, i).start()
        return hidden

    for i in range(parts):
        move_start(*moved(i))
    lengths().start()

    def first(i, carry):
        move_landed(*moved(i))
        forward(i, 0, 2, across).start()
        forward(i, 0, 1, core).start()
        hidden_ref[span(i), :] = project(0, i)
        here_ref[span(i), :] = rows[0, span(i), :]
        return carry

    lax.fori_loop(0, parts, first, 0)

    def second(i, carry):
        forward(i, 0, 1, core).wait_recv()
        project(1, i)
        forward(i, 0, 2, across).wait_recv()
        forward(i, 2, 3, core).start()
        project(2, i)
        return carry

    lax.fori_loop(0, parts, second, 0)

    def third(i, carry):
        forward(i, 2, 3, core).wait_recv()
        project(3, i)
        return carry

    lax.fori_loop(0, parts, third, 0)
    lengths().wait()

    def last(i, carry):
        move_sent(*moved(i))
        forward(i, 0, 2, across).wait_send()
        forward(i, 0, 1, core).wait_send()
        forward(i, 2, 3, core).wait_send()
        for piece in range(4):
            to_hbm(piece, i).wait()
        return carry

    lax.fori_loop(0, parts, last, 0)


def start_work(tokens, clip_lengths, gain, shift, weight, bias):
    rows, width = tokens.shape
    vmem, anywhere = pl.BlockSpec(memory_space=pltpu.VMEM), pl.BlockSpec(memory_space=pl.ANY)
    projected, hidden, here, found = pl.pallas_call(
        start_kernel,
        in_specs=[anywhere] + [vmem] * 5,
        out_specs=[anywhere, vmem, vmem, vmem],
        out_shape=[
            jax.ShapeDtypeStruct((4 * rows, 3 * width), BF16),
            jax.ShapeDtypeStruct((rows, width), BF16),
            jax.ShapeDtypeStruct((rows, width), BF16),
            jax.ShapeDtypeStruct(clip_lengths.shape, jnp.int32),
        ],
        scratch_shapes=[
            pltpu.VMEM((4, rows, width), BF16),
            pltpu.VMEM((4 * rows, 3 * width), BF16),
            pltpu.SemaphoreType.DMA((5, 4)),
            pltpu.SemaphoreType.DMA((5, 4)),
            pltpu.SemaphoreType.DMA((4, 4)),
        ],
        compiler_params=pltpu.CompilerParams(
            vmem_limit_bytes=VMEM_BYTES, collective_id=0, has_side_effects=True
        ),
        cost_estimate=pl.CostEstimate(
            flops=24 * rows * width * width, bytes_accessed=32 * rows * width, transcendentals=0
        ),
        name="start_work",
    )(tokens, clip_lengths, gain.reshape(1, -1), shift.reshape(1, -1), weight, bias.reshape(1, -1))
    return projected, hidden, here, jnp.where(stays(), clip_lengths, found)


def added(one, other):
    return (one.astype(F32) + other.astype(F32)).astype(BF16)


class PairPlan:
    ways = True

    def start(self, tokens, clip_lengths, gain, shift, weight, bias):
        projected, hidden, here, lengths = start_work(
            tokens, clip_lengths, gain, shift, weight, bias
        )
        return projected, projected, hidden, here, lengths

    def to_home(self, rows):
        pairs = [
            (dp * 4 + z, (dp ^ 1) * 4 + (z ^ 2))
            for dp in range(8)
            for z in range(4)
            if dp % 2 != z // 2
        ]
        return jnp.where(stays(), rows, lax.ppermute(rows, ("dp", "seq"), pairs))

    def gather(self, own):
        core = self.swap(own, 1)
        across = lax.ppermute(own, "seq", [(i, i ^ 1) for i in range(4)])
        return [own, core, across, self.swap(across, 1)]

    def positions(self, rows):
        core, z = lax.axis_index("dp") % 2, lax.axis_index("seq")
        found = []
        for piece in range(4):
            c, plane = core ^ (piece % 2), z ^ (piece // 2)
            shard = jnp.where(c == plane // 2, plane, plane ^ 2)
            found.append(shard * rows + jnp.arange(rows, dtype=jnp.int32))
        return jnp.concatenate(found)

    def own(self, gathered):
        return gathered[: gathered.shape[0] // 4]

    def backward(
        self, chances, grad, attended, projected, own, mark_k, mark_q, log_totals, halves, block_out
    ):
        dq, dk, dv, down, up, out, home = backward(
            chances,
            grad,
            attended,
            projected,
            self.own(mark_k),
            mark_q,
            log_totals,
            halves,
            block_out,
        )
        return dq, dk, dv, (down, up, out), home

    def weight(self, left, right):
        me = lax.axis_index("dp").astype(jnp.int32).reshape(1)
        if left.shape[1] // 8 % LANES == 0:
            return grad_weight_tall(left, right, me, 8)
        tile = 384 if right.shape[1] % 384 == 0 else right.shape[1]
        return grad_weight_wide(left, right, me, 8, tile)

    def swap(self, value, bit):
        return lax.ppermute(value, "dp", [(i, i ^ bit) for i in range(8)])

    def reduce(self, halves):
        keep, send = halves
        total = added(keep, self.swap(send, 1))
        middle = total.shape[2] // 2
        first, second = total[:, :, :middle], total[:, :, middle:]
        first = added(first[0::2], self.swap(first[1::2], 2))
        second = added(second[0:2], self.swap(second[2:4], 4))
        first = added(first[0], self.swap(first[1], 4))
        second = added(second[0], self.swap(second[1], 2))
        total = jnp.concatenate([first, second], 1)
        total = added(total, lax.ppermute(total, "seq", [(0, 1), (3, 2)]))
        total = added(total, lax.ppermute(total, "seq", [(1, 2), (2, 1)]))
        ends = lax.ppermute(total, "seq", [(1, 0), (2, 3)])
        z = lax.axis_index("seq")
        return jnp.where((z == 1) | (z == 2), total, ends).astype(F32)

    def reduce_vectors(self, vectors):
        packed = jnp.concatenate(vectors)
        for bit in (1, 2, 4):
            packed = packed + self.swap(packed, bit)
        for bit in (1, 2):
            packed = packed + lax.ppermute(packed, "seq", [(i, i ^ bit) for i in range(4)])
        results, start = [], 0
        for vector in vectors:
            part = vector.shape[0] // 8
            results.append(
                lax.dynamic_slice(packed, (start + lax.axis_index("dp") * part,), (part,))
            )
            start += vector.shape[0]
        return results


class PlainPlan:
    ways = None

    def __init__(self, pieces):
        self.pieces = pieces

    def to_home(self, rows):
        return rows

    def start(self, tokens, clip_lengths, gain, shift, weight, bias):
        hidden = layer_norm(tokens.astype(F32), gain, shift)[0].astype(BF16)
        own = (matmul(hidden, weight) + bias).astype(BF16)
        projected = lax.all_gather(own, "seq", axis=0, tiled=True)
        return projected, own, hidden, tokens, clip_lengths

    def gather(self, own):
        gathered = lax.all_gather(own, "seq", axis=0, tiled=False)
        return [gathered[i] for i in range(self.pieces)]

    def positions(self, rows):
        return jnp.arange(rows * self.pieces, dtype=jnp.int32)

    def own(self, gathered):
        rows = gathered.shape[0] // self.pieces
        return lax.dynamic_slice_in_dim(gathered, lax.axis_index("seq") * rows, rows, 0)

    def backward(
        self, chances, grad, attended, projected, own, mark_k, mark_q, log_totals, halves, block_out
    ):
        dq, deltas = grad_query(chances, grad, attended, projected)
        dk, dv = grad_key_value(
            own,
            projected,
            self.gather(grad),
            self.gather(log_totals),
            self.gather(deltas),
            self.own(mark_k),
            mark_q,
        )
        return dq, dk, dv, [self.reduce(total) for total in halves], block_out

    def weight(self, left, right):
        return inner_rows(left, right)

    def reduce(self, total):
        return lax.psum(lax.psum_scatter(total, "dp", scatter_dimension=0, tiled=True), "seq")

    def reduce_vectors(self, vectors):
        return [self.reduce(vector) for vector in vectors]


def gelu_parts(pre_act):
    inside = 0.5 * (1.0 + lax.erf(pre_act * math.sqrt(0.5)))
    slope = inside + pre_act * jnp.exp(-0.5 * pre_act * pre_act) * (1.0 / math.sqrt(2.0 * math.pi))
    return pre_act * inside, slope


def body(
    plan,
    tokens,
    clip_lengths,
    ln1_gain,
    ln1_shift,
    w_qkv,
    bias_query,
    bias_value,
    w_out,
    bias_out,
    ln2_gain,
    ln2_shift,
    w_up,
    bias_up,
    w_down,
    bias_down,
    cotangent,
):
    rows, width = tokens.shape
    bias = jnp.concatenate([bias_query, jnp.zeros_like(bias_query), bias_value])
    projected, own, hidden1, here, lengths = plan.start(
        tokens, clip_lengths, ln1_gain, ln1_shift, w_qkv, bias
    )

    clip_ends = jnp.cumsum(lengths.reshape(-1))
    position = plan.positions(rows)
    segment = jnp.sum((position[:, None] >= clip_ends[None, :]).astype(jnp.int32), 1)
    lane = jnp.arange(LANES, dtype=jnp.int32)[None, :]
    same = lane == segment[:, None]
    mark_k = same.astype(BF16)
    mark_q = jnp.where(same | (lane >= clip_ends.shape[0]), 0.0, masked_score).astype(BF16)

    attended, chances, log_totals, grad_out = attend(
        plan, own, projected, plan.own(mark_q), mark_k, cotangent
    )

    inputs32 = here.astype(F32)
    middle = inputs32 + matmul(attended, w_out) + bias_out
    normed2_out, normed2, inverse2 = layer_norm(middle, ln2_gain, ln2_shift)
    hidden2 = normed2_out.astype(BF16)
    upper = matmul(hidden2, w_up) + bias_up
    activated, slope = gelu_parts(upper)
    activated = activated.astype(BF16)
    grad_upper = (inner_cols(grad_out, w_down) * slope).astype(BF16)
    grad_hidden2 = inner_cols(grad_upper, w_up)
    grad_norm2, grad_ln2_gain, grad_ln2_shift = norm_back(grad_hidden2, normed2, inverse2, ln2_gain)
    grad_middle = grad_out.astype(F32) + grad_norm2
    grad_branch = grad_middle.astype(BF16)
    grad_attended = inner_cols(grad_branch, w_out).astype(BF16)

    block_out = (middle + matmul(activated, w_down) + bias_down).astype(BF16)
    halves = [
        plan.weight(activated, grad_out),
        plan.weight(hidden2, grad_upper),
        plan.weight(attended, grad_branch),
    ]
    grad_bias_down = jnp.sum(grad_out.astype(F32), 0)
    grad_bias_up = jnp.sum(grad_upper.astype(F32), 0)
    grad_bias_out = jnp.sum(grad_branch.astype(F32), 0)
    grad_bias_down, grad_bias_up, grad_bias_out, grad_ln2_gain, grad_ln2_shift = (
        plan.reduce_vectors(
            [grad_bias_down, grad_bias_up, grad_bias_out, grad_ln2_gain, grad_ln2_shift]
        )
    )

    dq, dk, dv, (grad_w_down, grad_w_up, grad_w_out), block_out = plan.backward(
        chances,
        grad_attended,
        attended,
        projected,
        own,
        mark_k,
        mark_q,
        log_totals,
        halves,
        block_out,
    )
    grad_projected = jnp.concatenate([dq, dk, dv], 1)
    grad_w_qkv = plan.reduce(plan.weight(hidden1, grad_projected))
    grad_bias_query = jnp.sum(dq.astype(F32), 0)
    grad_bias_value = jnp.sum(dv.astype(F32), 0)
    grad_hidden1 = inner_cols(grad_projected, w_qkv)
    _, normed1, inverse1 = layer_norm(inputs32, ln1_gain, ln1_shift)
    grad_norm1, grad_ln1_gain, grad_ln1_shift = norm_back(grad_hidden1, normed1, inverse1, ln1_gain)
    grad_tokens = plan.to_home((grad_middle + grad_norm1).astype(BF16))
    grad_bias_query, grad_bias_value, grad_ln1_gain, grad_ln1_shift = plan.reduce_vectors(
        [grad_bias_query, grad_bias_value, grad_ln1_gain, grad_ln1_shift]
    )
    return (
        block_out,
        grad_tokens,
        grad_ln1_gain,
        grad_ln1_shift,
        grad_w_qkv,
        grad_bias_query,
        grad_bias_value,
        grad_w_out,
        grad_bias_out,
        grad_ln2_gain,
        grad_ln2_shift,
        grad_w_up,
        grad_bias_up,
        grad_w_down,
        grad_bias_down,
    )


def solution(mesh):
    sizes = dict(mesh.shape)
    plan = PairPlan() if sizes == {"dp": 8, "seq": 4} else PlainPlan(sizes["seq"])
    rows = P(("dp", "seq"), None)
    return jax.shard_map(
        functools.partial(body, plan),
        mesh=mesh,
        in_specs=(rows, P("dp", None)) + (P(),) * 13 + (rows,),
        out_specs=(
            rows,
            rows,
            P("dp"),
            P("dp"),
            P("dp", None),
            P("dp"),
            P("dp"),
            P("dp", None),
            P("dp"),
            P("dp"),
            P("dp"),
            P("dp", None),
            P("dp"),
            P("dp", None),
            P("dp"),
        ),
        check_vma=False,
    )
```

```python
import functools
import math

import jax
import jax.numpy as jnp
from jax import lax
from jax.experimental import pallas as pl
from jax.experimental.pallas import tpu as pltpu
from jax.sharding import PartitionSpec as P

HDIM = 64
LANES = 128
STATS = 16
F32 = jnp.float32
BF16 = jnp.bfloat16
VMEM_BYTES = 56 << 20
NT = (((1,), (1,)), ((), ()))
NN = (((1,), (0,)), ((), ()))

epsilon = 1e-06
masked_score = -1e30


def dot_as(left, right, dims):
    return lax.dot_general(left, right, dims, preferred_element_type=F32)


def matmul(left, right):
    return dot_as(left, right, NN)


def inner_rows(left, right):
    return dot_as(left, right, (((0,), (0,)), ((), ())))


def inner_cols(left, right):
    return dot_as(left, right, NT)


def layer_norm(values, gain, shift):
    center = values - jnp.mean(values, -1, keepdims=True)
    inverse = lax.rsqrt(jnp.mean(center * center, -1, keepdims=True) + epsilon)
    normed = center * inverse
    return (normed * gain + shift, normed, inverse)


def norm_back(grad_out, normed, inverse, gain):
    scaled = grad_out * gain
    grad_in = inverse * (
        scaled
        - jnp.mean(scaled, -1, keepdims=True)
        - normed * jnp.mean(scaled * normed, -1, keepdims=True)
    )
    return (grad_in, jnp.sum(grad_out * normed, 0), jnp.sum(grad_out, 0))


def neighbours():
    dp, z = lax.axis_index("dp"), lax.axis_index("seq")
    other = dp + 1 - 2 * lax.rem(dp, jnp.int32(2))
    pair = z + 1 - 2 * lax.rem(z, jnp.int32(2))
    return (other, z), (dp, pair), (other, lax.rem(z + 2, jnp.int32(4)))


def stays():
    dp, z = lax.axis_index("dp"), lax.axis_index("seq")
    return lax.rem(dp, jnp.int32(2)) == lax.div(z, jnp.int32(2))


def greet(devices):
    barrier = pltpu.get_barrier_semaphore()
    for device in devices:
        pl.semaphore_signal(barrier, inc=1, device_id=device, device_id_type=pl.DeviceIdType.MESH)
    pl.semaphore_wait(barrier, len(devices))


def remote(source, target, sent, landed, device):
    return pltpu.make_async_remote_copy(
        src_ref=source,
        dst_ref=target,
        send_sem=sent,
        recv_sem=landed,
        device_id=device,
        device_id_type=pl.DeviceIdType.MESH,
    )


def move_start(source, target, sent, landed):
    swap = neighbours()[2]

    @pl.when(stays())
    def _():
        pltpu.make_async_copy(source, target, landed).start()

    @pl.when(jnp.logical_not(stays()))
    def _():
        remote(source, target, sent, landed, swap).start()


def move_landed(source, target, sent, landed):
    swap = neighbours()[2]

    @pl.when(stays())
    def _():
        pltpu.make_async_copy(source, target, landed).wait()

    @pl.when(jnp.logical_not(stays()))
    def _():
        remote(source, target, sent, landed, swap).wait_recv()


def move_sent(source, target, sent, landed):
    swap = neighbours()[2]

    @pl.when(jnp.logical_not(stays()))
    def _():
        remote(source, target, sent, landed, swap).wait_send()


def head_lanes(rows, head):
    lane = lax.broadcasted_iota(jnp.int32, (rows, LANES), 1)
    return (lane < HDIM) if head == 0 else (lane >= HDIM)


def place_stats(stat, rows, pair, values):
    lane = lax.broadcasted_iota(jnp.int32, (values[0].shape[0], LANES), 1)
    old = stat[rows, :]
    stat[rows, :] = jnp.where(
        lane == 2 * pair, values[0], jnp.where(lane == 2 * pair + 1, values[1], old)
    )


def attend_kernel(sub, ways, q_ref, k_ref, v_ref, mark_q, mark_k, *refs):
    pair = pl.program_id(0)
    if ways is None:
        out_ref, chance_ref, lse_ref, stat = refs
    else:
        home_ref, out_ref, chance_ref, lse_ref, here_ref, stat, sent, landed = refs
        move = (home_ref, here_ref, sent, landed)

        @pl.when(pair == 0)
        def _():
            greet([neighbours()[2]])
            move_start(*move)

    keys = jnp.concatenate([k_ref[...], mark_k[...]], 1)
    values = v_ref[...]

    def step(i, carry):
        rows = pl.ds(pl.multiple_of(i * sub, sub), sub)
        query = q_ref[rows, :] * jnp.asarray(1.0 / math.sqrt(HDIM), BF16)
        outs, totals = [], []
        for head in range(2):
            own = jnp.where(head_lanes(sub, head), query, jnp.zeros_like(query))
            scores = dot_as(jnp.concatenate([own, mark_q[rows, :]], 1), keys, NT)
            highest = jnp.max(scores, -1, keepdims=True)
            powers = jnp.exp(scores - highest)
            total = jnp.sum(powers, -1, keepdims=True)
            chances = (powers * (1.0 / total)).astype(BF16)
            chance_ref[head, rows, :] = chances
            outs.append(dot_as(chances, values, NN))
            totals.append(highest + jnp.log(total))
        out_ref[rows, :] = jnp.where(head_lanes(sub, 0), outs[0], outs[1]).astype(BF16)
        place_stats(stat, rows, pair, totals)
        return carry

    lax.fori_loop(0, q_ref.shape[0] // sub, step, 0)

    @pl.when(pair == pl.num_programs(0) - 1)
    def _():
        lse_ref[...] = jnp.transpose(stat[...])[:STATS]
        if ways is not None:
            move_landed(*move)
            move_sent(*move)


def grad_query_kernel(
    sub, chance_ref, grad_ref, out_ref, k_ref, v_ref, dq_ref, delta_ref, stat
):
    pair = pl.program_id(0)
    keys, values = k_ref[...], v_ref[...]

    def step(i, carry):
        rows = pl.ds(pl.multiple_of(i * sub, sub), sub)
        grad = grad_ref[rows, :]
        product = grad.astype(F32) * out_ref[rows, :].astype(F32)
        outs, deltas = [], []
        for head in range(2):
            own = head_lanes(sub, head)
            delta = jnp.sum(jnp.where(own, product, 0.0), -1, keepdims=True)
            grad_chances = dot_as(jnp.where(own, grad, jnp.zeros_like(grad)), values, NT)
            scores = (chance_ref[head, rows, :].astype(F32) * (grad_chances - delta)).astype(BF16)
            outs.append(dot_as(scores, keys, NN))
            deltas.append(delta)
        both = jnp.where(head_lanes(sub, 0), outs[0], outs[1])
        dq_ref[rows, :] = (both * (1.0 / math.sqrt(HDIM))).astype(BF16)
        place_stats(stat, rows, pair, deltas)
        return carry

    lax.fori_loop(0, grad_ref.shape[0] // sub, step, 0)

    @pl.when(pair == pl.num_programs(0) - 1)
    def _():
        delta_ref[...] = jnp.transpose(stat[...])[:STATS]


def grad_key_kernel(sub, pieces, k_ref, v_ref, q_ref, *refs):
    g_refs = refs[:pieces]
    lse_refs, delta_refs = refs[pieces : 2 * pieces], refs[2 * pieces : 3 * pieces]
    mark_k, mark_q, dk_ref, dv_ref = refs[3 * pieces :]
    pair = pl.program_id(0)
    queries = q_ref[...]
    grads = jnp.concatenate([ref[...] for ref in g_refs], 0)
    scaled = jnp.concatenate(
        [queries * jnp.asarray(1.0 / math.sqrt(HDIM), BF16), mark_q[...]], 1
    )

    def stats(which, head):
        return jnp.concatenate([ref[pl.ds(2 * pair + head, 1), :] for ref in which], 1)

    log_totals = [stats(lse_refs, head) for head in range(2)]
    deltas = [stats(delta_refs, head) for head in range(2)]

    def step(i, carry):
        rows = pl.ds(pl.multiple_of(i * sub, sub), sub)
        key, value = k_ref[rows, :], v_ref[rows, :]
        dks, dvs = [], []
        for head in range(2):
            own = head_lanes(sub, head)
            key_own = jnp.where(own, key, jnp.zeros_like(key))
            value_own = jnp.where(own, value, jnp.zeros_like(value))
            scores = dot_as(jnp.concatenate([key_own, mark_k[rows, :]], 1), scaled, NT)
            chances = jnp.exp(scores - log_totals[head])
            grad_chances = dot_as(value_own, grads, NT)
            grad_scores = (chances * (grad_chances - deltas[head])).astype(BF16)
            dvs.append(dot_as(chances.astype(BF16), grads, NN))
            dks.append(dot_as(grad_scores, queries, NN))
        first = head_lanes(sub, 0)
        dk = jnp.where(first, dks[0], dks[1]) * (1.0 / math.sqrt(HDIM))
        dk_ref[rows, :] = dk.astype(BF16)
        dv_ref[rows, :] = jnp.where(first, dvs[0], dvs[1]).astype(BF16)
        return carry

    lax.fori_loop(0, k_ref.shape[0] // sub, step, 0)


def columns(rows, first):
    return pl.BlockSpec((rows, LANES), lambda t: (0, first + t))


def whole(array):
    return pl.BlockSpec(array.shape, lambda t: (0,) * array.ndim)


def kernel_call(kernel, name, grid, in_specs, out_specs, out_shape, scratch, flops, moved, **params):
    return pl.pallas_call(
        kernel,
        grid=grid,
        in_specs=in_specs,
        out_specs=out_specs,
        out_shape=out_shape,
        scratch_shapes=scratch,
        compiler_params=pltpu.CompilerParams(vmem_limit_bytes=VMEM_BYTES, **params),
        cost_estimate=pl.CostEstimate(flops=flops, bytes_accessed=moved, transcendentals=0),
        name=name,
    )


def attend(plan, own, projected, mark_q, mark_k, cotangent, sub=256):
    rows, width = mark_q.shape[0], own.shape[1] // 3
    length, pairs = projected.shape[0], width // LANES
    stats = jax.ShapeDtypeStruct((STATS, rows), F32)
    anywhere = pl.BlockSpec(memory_space=pl.ANY)
    ways = plan.ways
    moving = [] if ways is None else [cotangent]
    params = {} if ways is None else {"collective_id": 1, "has_side_effects": True}
    results = kernel_call(
        functools.partial(attend_kernel, sub, ways),
        "attend",
        (pairs,),
        [
            columns(rows, 0),
            columns(length, pairs),
            columns(length, 2 * pairs),
            whole(mark_q),
            whole(mark_k),
        ]
        + [anywhere] * len(moving),
        [
            columns(rows, 0),
            pl.BlockSpec((2, rows, length), lambda t: (t, 0, 0)),
            whole(stats),
        ]
        + [anywhere] * len(moving),
        [
            jax.ShapeDtypeStruct((rows, width), BF16),
            jax.ShapeDtypeStruct((2 * pairs, rows, length), BF16),
            stats,
        ]
        + [jax.ShapeDtypeStruct(array.shape, array.dtype) for array in moving],
        [pltpu.VMEM((rows, LANES), F32)] + [pltpu.SemaphoreType.DMA] * (2 * len(moving)),
        24 * rows * length * width,
        4 * pairs * rows * length,
        **params,
    )(own, projected, projected, mark_q, mark_k, *moving)
    return tuple(results) if moving else tuple(results) + (cotangent,)


def grad_query(chances, grad, attended, projected, sub=256):
    rows, width = grad.shape
    length, pairs = projected.shape[0], width // LANES
    stats = jax.ShapeDtypeStruct((STATS, rows), F32)
    return kernel_call(
        functools.partial(grad_query_kernel, sub),
        "grad_query",
        (pairs,),
        [
            pl.BlockSpec((2, rows, length), lambda t: (t, 0, 0)),
            columns(rows, 0),
            columns(rows, 0),
            columns(length, pairs),
            columns(length, 2 * pairs),
        ],
        [columns(rows, 0), whole(stats)],
        [jax.ShapeDtypeStruct((rows, width), BF16), stats],
        [pltpu.VMEM((rows, LANES), F32)],
        16 * rows * length * width,
        4 * pairs * rows * length,
    )(chances, grad, attended, projected, projected)


def grad_key_value(own, projected, grads, log_totals, deltas, mark_k, mark_q, sub=256):
    rows, width = grads[0].shape
    pieces, pairs = len(grads), width // LANES
    length = rows * pieces
    result = jax.ShapeDtypeStruct((rows, width), BF16)
    return kernel_call(
        functools.partial(grad_key_kernel, sub, pieces),
        "grad_key_value",
        (pairs,),
        [columns(rows, pairs), columns(rows, 2 * pairs), columns(length, 0)]
        + [columns(rows, 0)] * pieces
        + [whole(log_totals[0])] * (2 * pieces)
        + [whole(mark_k), whole(mark_q)],
        [columns(rows, 0)] * 2,
        [result] * 2,
        [],
        32 * rows * length * width,
        8 * length * width,
    )(own, own, projected, *grads, *log_totals, *deltas, mark_k, mark_q)


class Chunk:
    def __init__(self, index, source, rows, columns, y_first):
        self.index, self.source, self.rows, self.columns = index, source, rows, columns
        self.shape = (rows[1], columns[1])
        self.blocks = ((2, 3), 1) if y_first else ((1, 3), 2)
        self.y_first = y_first

    def scratch(self):
        rows, columns = self.shape
        return [
            pltpu.VMEM((4, rows, columns), BF16),
            pltpu.VMEM((4, rows, columns), BF16),
            pltpu.VMEM((2, rows, columns), BF16),
            pltpu.VMEM((rows, columns), BF16),
            pltpu.VMEM((rows, columns), BF16),
            pltpu.VMEM((rows, columns), BF16),
            pltpu.VMEM((rows, columns), BF16),
            pltpu.SemaphoreType.DMA((8,)),
            pltpu.SemaphoreType.DMA((8,)),
        ]

    def bind(self, refs, out_refs, scratch, devices):
        at = (pl.ds(*self.rows), pl.ds(*self.columns))
        keep_hbm = refs[self.source].at[(pl.ds(0, 4),) + at]
        send_hbm = refs[self.source].at[(pl.ds(4, 4),) + at]
        self.out = out_refs[self.source].at[at]
        (self.keep, core, first, second, self.z1, self.z2, self.z3, sent, landed) = scratch
        near, far = (devices["y"], devices["x"]) if self.y_first else (devices["x"], devices["y"])
        self.core, self.first, self.second = core, first, second
        sends, last = self.blocks
        self.load = pltpu.make_async_copy(keep_hbm, self.keep, landed.at[7])
        self.to_core = remote(send_hbm, core, sent.at[0], landed.at[0], devices["core"])
        self.to_near = [
            remote(self.keep.at[b], first.at[i], sent.at[1 + i], landed.at[1 + i], near)
            for i, b in enumerate(sends)
        ]
        self.to_far = remote(self.keep.at[last], second, sent.at[3], landed.at[3], far)
        self.inward = remote(self.keep.at[0], self.z1, sent.at[4], landed.at[4], devices["pair"])
        self.middle = remote(self.keep.at[0], self.z2, sent.at[5], landed.at[5], devices["mirror"])
        self.outward = remote(self.z1, self.z3, sent.at[6], landed.at[6], devices["pair"])

    def add(self, target, source):
        def step(i, carry):
            at = pl.ds(pl.multiple_of(i * 16, 16), 16)
            target[at, :] = added(target[at, :], source[at, :])
            return carry

        lax.fori_loop(0, self.shape[0] // 16, step, 0)

    def start(self):
        self.to_core.start()
        self.load.start()

    def near(self):
        self.load.wait()
        self.to_core.wait_recv()
        for block in range(4):
            self.add(self.keep.at[block], self.core.at[block])
        for copy in self.to_near:
            copy.start()

    def far(self):
        stay = [b for b in range(4) if b not in self.blocks[0]]
        for i, copy in enumerate(self.to_near):
            copy.wait_recv()
            self.add(self.keep.at[stay[i]], self.first.at[i])
        self.to_far.start()

    def along(self):
        self.to_far.wait_recv()
        self.add(self.keep.at[0], self.second)

        @pl.when(jnp.logical_not(inner()))
        def _():
            self.inward.start()

    def meet(self):
        @pl.when(inner())
        def _():
            self.inward.wait_recv()
            self.add(self.keep.at[0], self.z1)
            self.middle.start()

    def spread(self):
        @pl.when(inner())
        def _():
            self.middle.wait_recv()

            def step(i, carry):
                at = pl.ds(pl.multiple_of(i * 16, 16), 16)
                total = added(self.keep[0, at, :], self.z2[at, :])
                self.z1[at, :] = total
                self.out[at, :] = total.astype(F32)
                return carry

            lax.fori_loop(0, self.shape[0] // 16, step, 0)
            self.outward.start()

    def finish(self):
        @pl.when(jnp.logical_not(inner()))
        def _():
            self.outward.wait_recv()

            def step(i, carry):
                at = pl.ds(pl.multiple_of(i * 16, 16), 16)
                self.out[at, :] = self.z3[at, :].astype(F32)
                return carry

            lax.fori_loop(0, self.shape[0] // 16, step, 0)
            self.inward.wait_send()

        @pl.when(inner())
        def _():
            self.middle.wait_send()
            self.outward.wait_send()

        self.to_core.wait_send()
        for copy in self.to_near:
            copy.wait_send()
        self.to_far.wait_send()


def inner():
    z = lax.axis_index("seq")
    return jnp.logical_and(z > 0, z < 3)


def ring_devices():
    dp, z = lax.axis_index("dp"), lax.axis_index("seq")
    core, pair, swap = neighbours()
    x = dp + 2 - 4 * lax.rem(lax.div(dp, jnp.int32(2)), jnp.int32(2))
    y = dp + 4 - 8 * lax.div(dp, jnp.int32(4))
    return {
        "core": core,
        "pair": pair,
        "swap": swap,
        "x": (x, z),
        "y": (y, z),
        "mirror": (dp, 3 - z),
    }


def backward_chunks(shapes):
    found = []
    for source, y_first, count in ((0, True, 3), (1, False, 3), (2, True, 1)):
        _, rows, columns = shapes[source]
        for part in range(count):
            if source == 0:
                size = rows // count
                found.append((part, source, (part * size, size), (0, columns), y_first))
            else:
                size = columns // count
                found.append((part, source, (0, rows), (part * size, size), y_first))
    found.sort(key=lambda chunk: (chunk[0] if chunk[1] < 2 else 3, chunk[1]))
    return [Chunk(i, *chunk[1:]) for i, chunk in enumerate(found)]


def backward_kernel(
    shapes,
    pairs,
    chance_ref,
    grad_ref,
    attended_ref,
    k_ref,
    v_ref,
    q_ref,
    mark_k,
    mark_q,
    lse_ref,
    grad_down,
    grad_up,
    grad_out,
    block_ref,
    dq_ref,
    dk_ref,
    dv_ref,
    down_ref,
    up_ref,
    out_ref,
    home_ref,
    grads,
    stats,
    own_stats,
    sent,
    landed,
    *scratch,
):
    step = pl.program_id(0)
    rows, width = grad_ref.shape
    half = rows // 2
    devices = ring_devices()
    chunks = backward_chunks(shapes)
    per = len(scratch) // len(chunks)
    for chunk in chunks:
        chunk.bind(
            (grad_down, grad_up, grad_out),
            (down_ref, up_ref, out_ref),
            scratch[chunk.index * per : (chunk.index + 1) * per],
            devices,
        )
    move = (block_ref, home_ref, sent.at[12], landed.at[12])

    def grad_copy(i, part, source, device):
        at = pl.ds(part * half, half)
        n = 2 * i + part
        return remote(source.at[at], grads.at[i, at], sent.at[n], landed.at[n], device)

    def to_core(part):
        return grad_copy(1, part, grad_ref, devices["core"])

    def to_pair(part):
        return grad_copy(2, part, grad_ref, devices["pair"])

    def to_corner(part):
        return grad_copy(3, part, grads.at[2], devices["core"])

    def stat_copy(i, source, device):
        return remote(source, stats.at[i], sent.at[8 + i], landed.at[8 + i], device)

    stat_core = stat_copy(1, own_stats, devices["core"])
    stat_pair = stat_copy(2, own_stats, devices["pair"])
    stat_corner = stat_copy(3, stats.at[2], devices["core"])

    def begin():
        greet(list(devices.values()))
        for part in range(2):
            to_pair(part).start()
        for part in range(2):
            to_core(part).start()
        product = grad_ref[...].astype(F32) * attended_ref[...].astype(F32)
        high = product.astype(BF16)
        low = (product - high.astype(F32)).astype(BF16)
        head = lax.broadcasted_iota(jnp.int32, (STATS, width), 0)
        column = lax.broadcasted_iota(jnp.int32, (STATS, width), 1)
        mine = jnp.where(
            jnp.logical_and(column >= head * HDIM, column < (head + 1) * HDIM), 1.0, 0.0
        ).astype(BF16)
        own_stats[0:STATS, :] = lse_ref[...]
        own_stats[STATS:, :] = dot_as(mine, high, NT) + dot_as(mine, low, NT)
        stats[0] = own_stats[...]
        grads[0] = grad_ref[...]
        stat_pair.start()
        stat_core.start()

    def corner_stats():
        stat_pair.wait_recv()
        stat_corner.start()

    def corner(part):
        def run():
            to_pair(part).wait_recv()
            to_corner(part).start()

        return run

    def all_grads():
        stat_core.wait_recv()
        stat_corner.wait_recv()
        for part in range(2):
            to_core(part).wait_recv()
            to_corner(part).wait_recv()

    events = {0: [begin], 2: [corner_stats], 4: [corner(0)], pairs: [corner(1), all_grads]}

    def plan(at, *methods):
        events.setdefault(at, []).extend(methods)

    plan(0, *[chunk.start for chunk in chunks])
    plan(pairs, lambda: move_start(*move))
    when = {
        0: (1, 5, 7, 9, 11, 13),
        1: (1, 5, 7, 9, 11, 13),
        2: (3, 8, 10, 12, 14, 16),
        3: (3, 8, 10, 12, 14, 16),
        4: (6, 12, 14, 16, 17, 18),
        5: (6, 12, 14, 16, 17, 18),
        6: (8, 13, 15, 17, 18, 18),
    }
    for number, stage in enumerate(("near", "far", "along", "meet", "spread", "finish")):
        for chunk in chunks:
            plan(when[chunk.index][number], getattr(chunk, stage))

    def end():
        move_landed(*move)
        move_sent(*move)
        stat_core.wait_send()
        stat_pair.wait_send()
        stat_corner.wait_send()
        for part in range(2):
            to_core(part).wait_send()
            to_pair(part).wait_send()
            to_corner(part).wait_send()

    steps = 3 * pairs
    plan(steps, end)
    for at in range(steps):
        if at in events:

            @pl.when(step == at)
            def _():
                for event in events[at]:
                    event()

    @pl.when(step < pairs)
    def _():
        query_grads(chance_ref, grad_ref, attended_ref, k_ref, v_ref, dq_ref, step)

    @pl.when(step >= pairs)
    def _():
        pair = lax.rem(step, jnp.int32(pairs))
        first = (lax.div(step, jnp.int32(pairs)) - 1) * half
        at = pl.ds(pl.multiple_of(first, half), half)
        tile = pl.ds(pl.multiple_of(pair * LANES, LANES), LANES)

        def stat(row):
            return jnp.concatenate([stats[i, pl.ds(row, 1), :] for i in range(4)], 1)

        dk, dv = key_grads(
            k_ref[at, :],
            v_ref[at, :],
            mark_k[at, :],
            q_ref[...],
            jnp.concatenate([grads[i, :, tile] for i in range(4)], 0),
            mark_q[...],
            [stat(2 * pair + head) for head in range(2)],
            [stat(STATS + 2 * pair + head) for head in range(2)],
        )
        dk_ref[...] = dk
        dv_ref[...] = dv

    @pl.when(step == steps - 1)
    def _():
        for event in events[steps]:
            event()


def query_grads(chance_ref, grad_ref, out_ref, k_ref, v_ref, dq_ref, pair, sub=256):
    keys, values = k_ref[...], v_ref[...]
    tile = pl.ds(pl.multiple_of(pair * LANES, LANES), LANES)

    def step(i, carry):
        rows = pl.ds(pl.multiple_of(i * sub, sub), sub)
        grad = grad_ref[rows, tile]
        product = grad.astype(F32) * out_ref[rows, tile].astype(F32)
        outs = []
        for head in range(2):
            own = head_lanes(sub, head)
            delta = jnp.sum(jnp.where(own, product, 0.0), -1, keepdims=True)
            grad_chances = dot_as(jnp.where(own, grad, jnp.zeros_like(grad)), values, NT)
            scores = (chance_ref[head, rows, :].astype(F32) * (grad_chances - delta)).astype(BF16)
            outs.append(dot_as(scores, keys, NN))
        both = jnp.where(head_lanes(sub, 0), outs[0], outs[1])
        dq_ref[rows, :] = (both * (1.0 / math.sqrt(HDIM))).astype(BF16)
        return carry

    lax.fori_loop(0, dq_ref.shape[0] // sub, step, 0)


def key_grads(key, value, mark_k, queries, grads, mark_q, log_totals, deltas):
    scaled = jnp.concatenate([queries * jnp.asarray(1.0 / math.sqrt(HDIM), BF16), mark_q], 1)
    dks, dvs = [], []
    for head in range(2):
        own = head_lanes(key.shape[0], head)
        key_own = jnp.where(own, key, jnp.zeros_like(key))
        value_own = jnp.where(own, value, jnp.zeros_like(value))
        scores = dot_as(jnp.concatenate([key_own, mark_k], 1), scaled, NT)
        chances = jnp.exp(scores - log_totals[head])
        grad_chances = dot_as(value_own, grads, NT)
        grad_scores = (chances * (grad_chances - deltas[head])).astype(BF16)
        dvs.append(dot_as(chances.astype(BF16), grads, NN))
        dks.append(dot_as(grad_scores, queries, NN))
    first = head_lanes(key.shape[0], 0)
    dk = jnp.where(first, dks[0], dks[1]) * (1.0 / math.sqrt(HDIM))
    return dk.astype(BF16), jnp.where(first, dvs[0], dvs[1]).astype(BF16)


def backward(chances, grad, attended, projected, mark_k, mark_q, log_totals, totals, block_out):
    rows, width = grad.shape
    length, pairs = projected.shape[0], width // LANES
    shapes = [total.shape for total in totals]
    anywhere = pl.BlockSpec(memory_space=pl.ANY)
    result = jax.ShapeDtypeStruct((rows, width), BF16)
    reduced = [jax.ShapeDtypeStruct(shape[1:], F32) for shape in shapes]

    def once(array):
        return pl.BlockSpec(
            array.shape, lambda t: (0,) * array.ndim, pipeline_mode=pl.Buffered(1)
        )

    def tile(first):
        return pl.BlockSpec((length, LANES), lambda t: (0, first + lax.rem(t, pairs)))

    late = pl.BlockSpec(
        (rows // 2, LANES),
        lambda t: (jnp.maximum(lax.div(t, pairs) - 1, 0), jnp.maximum(t - pairs, 0) % pairs),
    )
    chunks = backward_chunks(shapes)
    stats = (2 * STATS, rows)
    return kernel_call(
        functools.partial(backward_kernel, shapes, pairs),
        "backward",
        (3 * pairs,),
        [
            pl.BlockSpec((2, rows, length), lambda t: (jnp.minimum(t, pairs - 1), 0, 0)),
            once(grad),
            once(attended),
            tile(pairs),
            tile(2 * pairs),
            pl.BlockSpec((length, LANES), lambda t: (0, jnp.maximum(t - pairs, 0) % pairs)),
            once(mark_k),
            once(mark_q),
            once(log_totals),
        ]
        + [anywhere] * (len(totals) + 1),
        [pl.BlockSpec((rows, LANES), lambda t: (0, jnp.minimum(t, pairs - 1))), late, late]
        + [once(shape) for shape in reduced]
        + [anywhere],
        [result] * 3 + reduced + [result],
        [
            pltpu.VMEM((4, rows, width), BF16),
            pltpu.VMEM((4,) + stats, F32),
            pltpu.VMEM(stats, F32),
            pltpu.SemaphoreType.DMA((13,)),
            pltpu.SemaphoreType.DMA((13,)),
        ]
        + [entry for chunk in chunks for entry in chunk.scratch()],
        48 * rows * length * width,
        4 * pairs * rows * length,
        collective_id=2,
        has_side_effects=True,
    )(
        chances,
        grad,
        attended,
        projected,
        projected,
        projected,
        mark_k,
        mark_q,
        log_totals,
        *totals,
        block_out,
    )


def gelu_parts(pre_act):
    inside = 0.5 * (1.0 + lax.erf(pre_act * math.sqrt(0.5)))
    slope = inside + pre_act * jnp.exp(-0.5 * pre_act * pre_act) * (1.0 / math.sqrt(2.0 * math.pi))
    return pre_act * inside, slope


def relative(block, me):
    turned = block ^ me
    return (turned % 2) * 4 + turned // 2


def feed_kernel(
    sub,
    index_ref,
    here_ref,
    attended_ref,
    grad_ref,
    w_out_ref,
    bias_out_ref,
    gain_ref,
    shift_ref,
    w_up_ref,
    bias_up_ref,
    w_down_ref,
    bias_down_ref,
    block_ref,
    grad_attended_ref,
    grad_middle_ref,
    down_ref,
    up_ref,
    out_ref,
    sum_up_ref,
    sums_ref,
    middle,
    normed,
    inverse,
    hidden,
    turned,
    total,
    grad_hidden,
    activated,
    grad_upper,
):
    step, last = pl.program_id(0), pl.num_programs(0) - 1
    me = index_ref[0]
    rows, width = here_ref.shape
    blocks = rows // sub

    def span(i):
        return pl.ds(pl.multiple_of(i * sub, sub), sub)

    @pl.when(step == 0)
    def _():
        def norm(i, carry):
            at = span(i)
            values = (
                here_ref[at, :].astype(F32)
                + dot_as(attended_ref[at, :], w_out_ref[...], NN)
                + bias_out_ref[...]
            )
            out, unit, root = layer_norm(values, gain_ref[...], shift_ref[...])
            middle[at, :] = values
            normed[at, :] = unit
            inverse[at, :] = jnp.broadcast_to(root, (sub, LANES))
            hidden[at, :] = out.astype(BF16)
            total[at, :] = values + bias_down_ref[...]
            grad_hidden[at, :] = jnp.zeros((sub, width), F32)
            return carry

        lax.fori_loop(0, blocks, norm, 0)
        turned[...] = jnp.transpose(hidden[...])

    def tile(i, carry):
        at = span(i)
        upper = dot_as(hidden[at, :], w_up_ref[...], NN) + bias_up_ref[...]
        grad_activated = dot_as(grad_ref[at, :], w_down_ref[...], NT)
        active, slope = gelu_parts(upper)
        active = active.astype(BF16)
        grad_in = (grad_activated * slope).astype(BF16)
        activated[at, :] = active
        grad_upper[at, :] = grad_in
        total[at, :] += dot_as(active, w_down_ref[...], NN)
        grad_hidden[at, :] += dot_as(grad_in, w_up_ref[...], NT)
        return carry + jnp.sum(grad_in.astype(F32), 0, keepdims=True)

    sum_up_ref[...] = lax.fori_loop(0, blocks, tile, jnp.zeros(sum_up_ref.shape, F32))

    grad_up = dot_as(turned[...], grad_upper[...], NN)
    part = width // 8
    for block in range(8):
        up_ref[relative(block, me)] = grad_up[block * part : (block + 1) * part].astype(BF16)
    grad_down = inner_rows(activated[...], grad_ref[...])
    part = down_ref.shape[2]
    for i in range(2):
        down_ref[(i ^ me) % 2, 0] = grad_down[i * part : (i + 1) * part].astype(BF16)

    @pl.when(step == last)
    def _():
        def norm(i, carry):
            at = span(i)
            block_ref[at, :] = total[at, :].astype(BF16)
            grad, unit = grad_hidden[at, :], normed[at, :]
            scaled = grad * gain_ref[...]
            grad_in = inverse[at, 0:1] * (
                scaled
                - jnp.mean(scaled, -1, keepdims=True)
                - unit * jnp.mean(scaled * unit, -1, keepdims=True)
            )
            before = grad_ref[at, :].astype(F32)
            grad_in = before + grad_in
            branch = grad_in.astype(BF16)
            grad_middle_ref[at, :] = grad_in
            hidden[at, :] = branch
            grad_attended_ref[at, :] = dot_as(branch, w_out_ref[...], NT).astype(BF16)
            sums = [grad * unit, grad, branch.astype(F32), before]
            return tuple(
                old + jnp.sum(value, 0, keepdims=True) for old, value in zip(carry, sums)
            )

        zero = jnp.zeros((1, width), F32)
        sums = lax.fori_loop(0, blocks, norm, (zero,) * 4)
        sums_ref[...] = jnp.concatenate(list(sums) + [zero] * 4, 0)
        grad_out = inner_rows(attended_ref[...], hidden[...])
        part = width // 8
        for block in range(8):
            out_ref[relative(block, me)] = grad_out[block * part : (block + 1) * part].astype(BF16)


def feed(
    here, attended, grad, w_out, bias_out, gain, shift, w_up, bias_up, w_down, bias_down, me, sub=256
):
    rows, width = here.shape
    wide = w_up.shape[1]
    steps = 4
    tile = wide // steps
    part = width // 8

    def row(vector):
        return vector.reshape(1, -1)

    def once(*shape):
        return pl.BlockSpec(shape, lambda f, at: (0,) * len(shape), pipeline_mode=pl.Buffered(1))

    act = once(rows, width)
    line = once(1, width)
    outs = [
        jax.ShapeDtypeStruct((rows, width), BF16),
        jax.ShapeDtypeStruct((rows, width), BF16),
        jax.ShapeDtypeStruct((rows, width), F32),
        jax.ShapeDtypeStruct((2, 4, wide // 8, width), BF16),
        jax.ShapeDtypeStruct((8, part, wide), BF16),
        jax.ShapeDtypeStruct((8, part, width), BF16),
        jax.ShapeDtypeStruct((1, wide), F32),
        jax.ShapeDtypeStruct((8, width), F32),
    ]
    return pl.pallas_call(
        functools.partial(feed_kernel, sub),
        grid_spec=pltpu.PrefetchScalarGridSpec(
            num_scalar_prefetch=1,
            grid=(steps,),
            in_specs=[
                act,
                act,
                act,
                once(width, width),
                line,
                line,
                line,
                pl.BlockSpec((width, tile), lambda f, at: (0, f)),
                pl.BlockSpec((1, tile), lambda f, at: (0, f)),
                pl.BlockSpec((tile, width), lambda f, at: (f, 0)),
                line,
            ],
            out_specs=[
                act,
                act,
                act,
                pl.BlockSpec((2, 1, wide // 8, width), lambda f, at: (0, f ^ (at[0] // 2), 0, 0)),
                pl.BlockSpec((8, part, tile), lambda f, at: (0, 0, f)),
                once(8, part, width),
                pl.BlockSpec((1, tile), lambda f, at: (0, f)),
                once(8, width),
            ],
            scratch_shapes=[
                pltpu.VMEM((rows, width), F32),
                pltpu.VMEM((rows, width), F32),
                pltpu.VMEM((rows, LANES), F32),
                pltpu.VMEM((rows, width), BF16),
                pltpu.VMEM((width, rows), BF16),
                pltpu.VMEM((rows, width), F32),
                pltpu.VMEM((rows, width), F32),
                pltpu.VMEM((rows, tile), BF16),
                pltpu.VMEM((rows, tile), BF16),
            ],
        ),
        out_shape=outs,
        compiler_params=pltpu.CompilerParams(vmem_limit_bytes=VMEM_BYTES),
        cost_estimate=pl.CostEstimate(
            flops=12 * rows * width * wide, bytes_accessed=8 * width * wide, transcendentals=0
        ),
        name="feed",
    )(
        me,
        here,
        attended,
        grad,
        w_out,
        row(bias_out),
        row(gain),
        row(shift),
        w_up,
        row(bias_up),
        w_down,
        row(bias_down),
    )


def grad_weight_kernel(parts, index_ref, left_ref, right_ref, keep_ref, send_ref, turned):
    @pl.when(pl.program_id(0) == 0)
    def _():
        turned[...] = jnp.transpose(left_ref[...])

    total = dot_as(turned[...], right_ref[...], NN)
    rows = total.shape[0] // parts
    me = index_ref[0]
    for part in range(parts):
        place = part ^ me
        block = total[part * rows : (part + 1) * rows].astype(BF16)

        @pl.when(place % 2 == 0)
        def _():
            keep_ref[place // 2] = block

        @pl.when(place % 2 == 1)
        def _():
            send_ref[place // 2] = block


def grad_weight_wide(left, right, me, parts, tile):
    length, height = left.shape
    width = right.shape[1]
    rows = height // parts
    half = jax.ShapeDtypeStruct((parts // 2, rows, width), BF16)
    out = pl.BlockSpec((parts // 2, rows, tile), lambda n, at: (0, 0, n))
    return pl.pallas_call(
        functools.partial(grad_weight_kernel, parts),
        grid_spec=pltpu.PrefetchScalarGridSpec(
            num_scalar_prefetch=1,
            grid=(width // tile,),
            in_specs=[
                pl.BlockSpec((length, height), lambda n, at: (0, 0)),
                pl.BlockSpec((length, tile), lambda n, at: (0, n)),
            ],
            out_specs=[out, out],
            scratch_shapes=[pltpu.VMEM((height, length), BF16)],
        ),
        out_shape=[half, half],
        compiler_params=pltpu.CompilerParams(vmem_limit_bytes=VMEM_BYTES),
        cost_estimate=pl.CostEstimate(
            flops=2 * length * height * width, bytes_accessed=2 * height * width, transcendentals=0
        ),
        name="grad_weight_wide",
    )(me, left, right)


def grad_weight_tall_kernel(index_ref, left_ref, right_ref, out_ref):
    out_ref[0] = inner_rows(left_ref[...], right_ref[...]).astype(BF16)


def grad_weight_tall(left, right, me, parts):
    length, height = left.shape
    width = right.shape[1]
    rows = height // parts

    def half(which):
        return pl.pallas_call(
            grad_weight_tall_kernel,
            grid_spec=pltpu.PrefetchScalarGridSpec(
                num_scalar_prefetch=1,
                grid=(parts // 2,),
                in_specs=[
                    pl.BlockSpec((length, rows), lambda b, at: (0, (2 * b + which) ^ at[0])),
                    pl.BlockSpec((length, width), lambda b, at: (0, 0)),
                ],
                out_specs=pl.BlockSpec((1, rows, width), lambda b, at: (b, 0, 0)),
            ),
            out_shape=jax.ShapeDtypeStruct((parts // 2, rows, width), BF16),
            compiler_params=pltpu.CompilerParams(vmem_limit_bytes=VMEM_BYTES),
            cost_estimate=pl.CostEstimate(
                flops=length * height * width, bytes_accessed=height * width, transcendentals=0
            ),
            name="grad_weight_tall",
        )(me, left, right)

    return half(0), half(1)


def start_kernel(
    tokens_ref,
    lengths_ref,
    gain_ref,
    shift_ref,
    w_ref,
    bias_ref,
    projected_ref,
    hidden_ref,
    here_ref,
    found_ref,
    rows,
    staged,
    sent,
    landed,
    out_sem,
):
    core, across, swap = neighbours()
    parts = sent.shape[1]
    height = tokens_ref.shape[0]
    part = height // parts
    greet([core, across, swap])

    def span(i):
        return pl.ds(pl.multiple_of(i * part, part), part)

    def moved(i):
        return (tokens_ref.at[span(i)], rows.at[0, span(i)], sent.at[0, i], landed.at[0, i])

    def lengths():
        return remote(lengths_ref, found_ref, sent.at[4, 0], landed.at[4, 0], core)

    def forward(i, origin, piece, device):
        return remote(
            rows.at[origin, span(i)],
            rows.at[piece, span(i)],
            sent.at[piece, i],
            landed.at[piece, i],
            device,
        )

    def out_span(piece, i):
        return pl.ds(pl.multiple_of(piece * height + i * part, part), part)

    def to_hbm(piece, i):
        at = out_span(piece, i)
        return pltpu.make_async_copy(staged.at[at], projected_ref.at[at], out_sem.at[piece, i])

    def project(piece, i):
        values = rows[piece, span(i), :].astype(F32)
        hidden = layer_norm(values, gain_ref[...], shift_ref[...])[0].astype(BF16)
        staged[out_span(piece, i), :] = (
            dot_as(hidden, w_ref[...], NN) + bias_ref[...]
        ).astype(BF16)
        to_hbm(piece, i).start()
        return hidden

    for i in range(parts):
        move_start(*moved(i))
    lengths().start()

    def first(i, carry):
        move_landed(*moved(i))
        forward(i, 0, 2, across).start()
        forward(i, 0, 1, core).start()
        hidden_ref[span(i), :] = project(0, i)
        here_ref[span(i), :] = rows[0, span(i), :]
        return carry

    lax.fori_loop(0, parts, first, 0)

    def second(i, carry):
        forward(i, 0, 1, core).wait_recv()
        project(1, i)
        forward(i, 0, 2, across).wait_recv()
        forward(i, 2, 3, core).start()
        project(2, i)
        return carry

    lax.fori_loop(0, parts, second, 0)

    def third(i, carry):
        forward(i, 2, 3, core).wait_recv()
        project(3, i)
        return carry

    lax.fori_loop(0, parts, third, 0)
    lengths().wait()

    def last(i, carry):
        move_sent(*moved(i))
        forward(i, 0, 2, across).wait_send()
        forward(i, 0, 1, core).wait_send()
        forward(i, 2, 3, core).wait_send()
        for piece in range(4):
            to_hbm(piece, i).wait()
        return carry

    lax.fori_loop(0, parts, last, 0)


def start_work(tokens, clip_lengths, gain, shift, weight, bias):
    rows, width = tokens.shape
    vmem, anywhere = pl.BlockSpec(memory_space=pltpu.VMEM), pl.BlockSpec(memory_space=pl.ANY)
    projected, hidden, here, found = pl.pallas_call(
        start_kernel,
        in_specs=[anywhere] + [vmem] * 5,
        out_specs=[anywhere, vmem, vmem, vmem],
        out_shape=[
            jax.ShapeDtypeStruct((4 * rows, 3 * width), BF16),
            jax.ShapeDtypeStruct((rows, width), BF16),
            jax.ShapeDtypeStruct((rows, width), BF16),
            jax.ShapeDtypeStruct(clip_lengths.shape, jnp.int32),
        ],
        scratch_shapes=[
            pltpu.VMEM((4, rows, width), BF16),
            pltpu.VMEM((4 * rows, 3 * width), BF16),
            pltpu.SemaphoreType.DMA((5, 4)),
            pltpu.SemaphoreType.DMA((5, 4)),
            pltpu.SemaphoreType.DMA((4, 4)),
        ],
        compiler_params=pltpu.CompilerParams(
            vmem_limit_bytes=VMEM_BYTES, collective_id=0, has_side_effects=True
        ),
        cost_estimate=pl.CostEstimate(
            flops=24 * rows * width * width, bytes_accessed=32 * rows * width, transcendentals=0
        ),
        name="start_work",
    )(tokens, clip_lengths, gain.reshape(1, -1), shift.reshape(1, -1), weight, bias.reshape(1, -1))
    return projected, hidden, here, jnp.where(stays(), clip_lengths, found)


def added(one, other):
    return (one.astype(F32) + other.astype(F32)).astype(BF16)


class PairPlan:
    ways = True

    def start(self, tokens, clip_lengths, gain, shift, weight, bias):
        projected, hidden, here, lengths = start_work(
            tokens, clip_lengths, gain, shift, weight, bias
        )
        return projected, projected, hidden, here, lengths

    def to_home(self, rows):
        pairs = [
            (dp * 4 + z, (dp ^ 1) * 4 + (z ^ 2))
            for dp in range(8)
            for z in range(4)
            if dp % 2 != z // 2
        ]
        return jnp.where(stays(), rows, lax.ppermute(rows, ("dp", "seq"), pairs))

    def gather(self, own):
        core = self.swap(own, 1)
        across = lax.ppermute(own, "seq", [(i, i ^ 1) for i in range(4)])
        return [own, core, across, self.swap(across, 1)]

    def positions(self, rows):
        core, z = lax.axis_index("dp") % 2, lax.axis_index("seq")
        found = []
        for piece in range(4):
            c, plane = core ^ (piece % 2), z ^ (piece // 2)
            shard = jnp.where(c == plane // 2, plane, plane ^ 2)
            found.append(shard * rows + jnp.arange(rows, dtype=jnp.int32))
        return jnp.concatenate(found)

    def own(self, gathered):
        return gathered[: gathered.shape[0] // 4]

    def feed(self, *args):
        me = lax.axis_index("dp").astype(jnp.int32).reshape(1)
        block_out, grad_attended, grad_middle, down, up, out, sum_up, sums = feed(*args, me)
        totals = [down.reshape((8,) + down.shape[2:]), up, out]
        return block_out, grad_attended, grad_middle, totals, [*sums[:4], sum_up[0]]

    def backward(
        self, chances, grad, attended, projected, own, mark_k, mark_q, log_totals, totals, block_out
    ):
        dq, dk, dv, down, up, out, home = backward(
            chances,
            grad,
            attended,
            projected,
            self.own(mark_k),
            mark_q,
            log_totals,
            totals,
            block_out,
        )
        return dq, dk, dv, (down, up, out), home

    def weight(self, left, right):
        me = lax.axis_index("dp").astype(jnp.int32).reshape(1)
        if left.shape[1] // 8 % LANES == 0:
            return grad_weight_tall(left, right, me, 8)
        tile = 384 if right.shape[1] % 384 == 0 else right.shape[1]
        return grad_weight_wide(left, right, me, 8, tile)

    def swap(self, value, bit):
        return lax.ppermute(value, "dp", [(i, i ^ bit) for i in range(8)])

    def reduce(self, halves):
        keep, send = halves
        total = added(keep, self.swap(send, 1))
        middle = total.shape[2] // 2
        first, second = total[:, :, :middle], total[:, :, middle:]
        first = added(first[0::2], self.swap(first[1::2], 2))
        second = added(second[0:2], self.swap(second[2:4], 4))
        first = added(first[0], self.swap(first[1], 4))
        second = added(second[0], self.swap(second[1], 2))
        total = jnp.concatenate([first, second], 1)
        total = added(total, lax.ppermute(total, "seq", [(0, 1), (3, 2)]))
        total = added(total, lax.ppermute(total, "seq", [(1, 2), (2, 1)]))
        ends = lax.ppermute(total, "seq", [(1, 0), (2, 3)])
        z = lax.axis_index("seq")
        return jnp.where((z == 1) | (z == 2), total, ends).astype(F32)

    def reduce_vectors(self, vectors):
        packed = jnp.concatenate(vectors)
        for bit in (1, 2, 4):
            packed = packed + self.swap(packed, bit)
        for bit in (1, 2):
            packed = packed + lax.ppermute(packed, "seq", [(i, i ^ bit) for i in range(4)])
        results, start = [], 0
        for vector in vectors:
            part = vector.shape[0] // 8
            results.append(
                lax.dynamic_slice(packed, (start + lax.axis_index("dp") * part,), (part,))
            )
            start += vector.shape[0]
        return results


class PlainPlan:
    ways = None

    def __init__(self, pieces):
        self.pieces = pieces

    def to_home(self, rows):
        return rows

    def start(self, tokens, clip_lengths, gain, shift, weight, bias):
        hidden = layer_norm(tokens.astype(F32), gain, shift)[0].astype(BF16)
        own = (matmul(hidden, weight) + bias).astype(BF16)
        projected = lax.all_gather(own, "seq", axis=0, tiled=True)
        return projected, own, hidden, tokens, clip_lengths

    def gather(self, own):
        gathered = lax.all_gather(own, "seq", axis=0, tiled=False)
        return [gathered[i] for i in range(self.pieces)]

    def positions(self, rows):
        return jnp.arange(rows * self.pieces, dtype=jnp.int32)

    def own(self, gathered):
        rows = gathered.shape[0] // self.pieces
        return lax.dynamic_slice_in_dim(gathered, lax.axis_index("seq") * rows, rows, 0)

    def backward(
        self, chances, grad, attended, projected, own, mark_k, mark_q, log_totals, totals, block_out
    ):
        dq, deltas = grad_query(chances, grad, attended, projected)
        dk, dv = grad_key_value(
            own,
            projected,
            self.gather(grad),
            self.gather(log_totals),
            self.gather(deltas),
            self.own(mark_k),
            mark_q,
        )
        return dq, dk, dv, [self.reduce(total) for total in totals], block_out

    def feed(
        self,
        here,
        attended,
        grad_out,
        w_out,
        bias_out,
        gain,
        shift,
        w_up,
        bias_up,
        w_down,
        bias_down,
    ):
        middle = here.astype(F32) + matmul(attended, w_out) + bias_out
        normed_out, normed, inverse = layer_norm(middle, gain, shift)
        hidden = normed_out.astype(BF16)
        activated, slope = gelu_parts(matmul(hidden, w_up) + bias_up)
        activated = activated.astype(BF16)
        grad_upper = (inner_cols(grad_out, w_down) * slope).astype(BF16)
        grad_hidden = inner_cols(grad_upper, w_up)
        grad_norm, grad_gain, grad_shift = norm_back(grad_hidden, normed, inverse, gain)
        grad_middle = grad_out.astype(F32) + grad_norm
        grad_branch = grad_middle.astype(BF16)
        grad_attended = inner_cols(grad_branch, w_out).astype(BF16)
        block_out = (middle + matmul(activated, w_down) + bias_down).astype(BF16)
        totals = [
            inner_rows(activated, grad_out),
            inner_rows(hidden, grad_upper),
            inner_rows(attended, grad_branch),
        ]
        vectors = [grad_gain, grad_shift] + [
            jnp.sum(value.astype(F32), 0) for value in (grad_branch, grad_out, grad_upper)
        ]
        return block_out, grad_attended, grad_middle, totals, vectors

    def weight(self, left, right):
        return inner_rows(left, right)

    def reduce(self, total):
        return lax.psum(lax.psum_scatter(total, "dp", scatter_dimension=0, tiled=True), "seq")

    def reduce_vectors(self, vectors):
        return [self.reduce(vector) for vector in vectors]


def body(
    plan,
    tokens,
    clip_lengths,
    ln1_gain,
    ln1_shift,
    w_qkv,
    bias_query,
    bias_value,
    w_out,
    bias_out,
    ln2_gain,
    ln2_shift,
    w_up,
    bias_up,
    w_down,
    bias_down,
    cotangent,
):
    rows, width = tokens.shape
    bias = jnp.concatenate([bias_query, jnp.zeros_like(bias_query), bias_value])
    projected, own, hidden1, here, lengths = plan.start(
        tokens, clip_lengths, ln1_gain, ln1_shift, w_qkv, bias
    )

    clip_ends = jnp.cumsum(lengths.reshape(-1))
    position = plan.positions(rows)
    segment = jnp.sum((position[:, None] >= clip_ends[None, :]).astype(jnp.int32), 1)
    lane = jnp.arange(LANES, dtype=jnp.int32)[None, :]
    same = lane == segment[:, None]
    mark_k = same.astype(BF16)
    mark_q = jnp.where(same | (lane >= clip_ends.shape[0]), 0.0, masked_score).astype(BF16)

    attended, chances, log_totals, grad_out = attend(
        plan, own, projected, plan.own(mark_q), mark_k, cotangent
    )

    block_out, grad_attended, grad_middle, totals, vectors = plan.feed(
        here,
        attended,
        grad_out,
        w_out,
        bias_out,
        ln2_gain,
        ln2_shift,
        w_up,
        bias_up,
        w_down,
        bias_down,
    )
    grad_ln2_gain, grad_ln2_shift, grad_bias_out, grad_bias_down, grad_bias_up = (
        plan.reduce_vectors(vectors)
    )

    dq, dk, dv, (grad_w_down, grad_w_up, grad_w_out), block_out = plan.backward(
        chances,
        grad_attended,
        attended,
        projected,
        own,
        mark_k,
        mark_q,
        log_totals,
        totals,
        block_out,
    )
    grad_projected = jnp.concatenate([dq, dk, dv], 1)
    grad_w_qkv = plan.reduce(plan.weight(hidden1, grad_projected))
    grad_bias_query = jnp.sum(dq.astype(F32), 0)
    grad_bias_value = jnp.sum(dv.astype(F32), 0)
    grad_hidden1 = inner_cols(grad_projected, w_qkv)
    _, normed1, inverse1 = layer_norm(here.astype(F32), ln1_gain, ln1_shift)
    grad_norm1, grad_ln1_gain, grad_ln1_shift = norm_back(grad_hidden1, normed1, inverse1, ln1_gain)
    grad_tokens = plan.to_home((grad_middle + grad_norm1).astype(BF16))
    grad_bias_query, grad_bias_value, grad_ln1_gain, grad_ln1_shift = plan.reduce_vectors(
        [grad_bias_query, grad_bias_value, grad_ln1_gain, grad_ln1_shift]
    )
    return (
        block_out,
        grad_tokens,
        grad_ln1_gain,
        grad_ln1_shift,
        grad_w_qkv,
        grad_bias_query,
        grad_bias_value,
        grad_w_out,
        grad_bias_out,
        grad_ln2_gain,
        grad_ln2_shift,
        grad_w_up,
        grad_bias_up,
        grad_w_down,
        grad_bias_down,
    )


def solution(mesh):
    sizes = dict(mesh.shape)
    plan = PairPlan() if sizes == {"dp": 8, "seq": 4} else PlainPlan(sizes["seq"])
    rows = P(("dp", "seq"), None)
    return jax.shard_map(
        functools.partial(body, plan),
        mesh=mesh,
        in_specs=(rows, P("dp", None)) + (P(),) * 13 + (rows,),
        out_specs=(
            rows,
            rows,
            P("dp"),
            P("dp"),
            P("dp", None),
            P("dp"),
            P("dp"),
            P("dp", None),
            P("dp"),
            P("dp"),
            P("dp"),
            P("dp", None),
            P("dp"),
            P("dp", None),
            P("dp"),
        ),
        check_vma=False,
    )
```

```python
import functools
import math

import jax
import jax.numpy as jnp
from jax import lax
from jax.experimental import pallas as pl
from jax.experimental.pallas import tpu as pltpu
from jax.sharding import PartitionSpec as P

HDIM = 64
LANES = 128
STATS = 16
F32 = jnp.float32
BF16 = jnp.bfloat16
VMEM_BYTES = 56 << 20
NT = (((1,), (1,)), ((), ()))
NN = (((1,), (0,)), ((), ()))

epsilon = 1e-06
masked_score = -1e30


def dot_as(left, right, dims):
    return lax.dot_general(left, right, dims, preferred_element_type=F32)


def matmul(left, right):
    return dot_as(left, right, NN)


def inner_rows(left, right):
    return dot_as(left, right, (((0,), (0,)), ((), ())))


def inner_cols(left, right):
    return dot_as(left, right, NT)


def layer_norm(values, gain, shift):
    center = values - jnp.mean(values, -1, keepdims=True)
    inverse = lax.rsqrt(jnp.mean(center * center, -1, keepdims=True) + epsilon)
    normed = center * inverse
    return (normed * gain + shift, normed, inverse)


def row_of(ref):
    return ref[...].reshape(1, -1)


def norm_back(grad_out, normed, inverse, gain):
    scaled = grad_out * gain
    grad_in = inverse * (
        scaled
        - jnp.mean(scaled, -1, keepdims=True)
        - normed * jnp.mean(scaled * normed, -1, keepdims=True)
    )
    return (grad_in, jnp.sum(grad_out * normed, 0), jnp.sum(grad_out, 0))


def neighbours():
    dp, z = lax.axis_index("dp"), lax.axis_index("seq")
    other = dp + 1 - 2 * lax.rem(dp, jnp.int32(2))
    pair = z + 1 - 2 * lax.rem(z, jnp.int32(2))
    return (other, z), (dp, pair), (other, lax.rem(z + 2, jnp.int32(4)))


def stays():
    dp, z = lax.axis_index("dp"), lax.axis_index("seq")
    return lax.rem(dp, jnp.int32(2)) == lax.div(z, jnp.int32(2))


def greet(devices):
    barrier = pltpu.get_barrier_semaphore()
    for device in devices:
        pl.semaphore_signal(barrier, inc=1, device_id=device, device_id_type=pl.DeviceIdType.MESH)
    pl.semaphore_wait(barrier, len(devices))


def remote(source, target, sent, landed, device):
    return pltpu.make_async_remote_copy(
        src_ref=source,
        dst_ref=target,
        send_sem=sent,
        recv_sem=landed,
        device_id=device,
        device_id_type=pl.DeviceIdType.MESH,
    )


def move_start(source, target, sent, landed):
    swap = neighbours()[2]

    @pl.when(stays())
    def _():
        pltpu.make_async_copy(source, target, landed).start()

    @pl.when(jnp.logical_not(stays()))
    def _():
        remote(source, target, sent, landed, swap).start()


def move_landed(source, target, sent, landed):
    swap = neighbours()[2]

    @pl.when(stays())
    def _():
        pltpu.make_async_copy(source, target, landed).wait()

    @pl.when(jnp.logical_not(stays()))
    def _():
        remote(source, target, sent, landed, swap).wait_recv()


def move_sent(source, target, sent, landed):
    swap = neighbours()[2]

    @pl.when(jnp.logical_not(stays()))
    def _():
        remote(source, target, sent, landed, swap).wait_send()


def two_heads(values):
    lane = lax.broadcasted_iota(jnp.int32, values.shape, 1)
    zero = jnp.zeros_like(values)
    return jnp.concatenate(
        [jnp.where(lane < HDIM, values, zero), jnp.where(lane < HDIM, zero, values)], 0
    )


def own_columns(values):
    rows = values.shape[0] // 2
    lane = lax.broadcasted_iota(jnp.int32, (rows, LANES), 1)
    return jnp.where(lane < HDIM, values[:rows], values[rows:])


def own_rows(values):
    count = values.shape[1] // 2
    return jnp.transpose(jnp.concatenate([values[:HDIM, :count], values[HDIM:, count:]], 0))


def scaled_down(values):
    return values * jnp.asarray(1.0 / math.sqrt(HDIM), values.dtype)


def attend_kernel(ways, q_ref, k_ref, v_ref, mark_q, mark_k, *refs):
    pair = pl.program_id(0)
    if ways is None:
        out_ref, chance_ref, lse_ref = refs
    else:
        home_ref, out_ref, chance_ref, lse_ref, here_ref, sent, landed = refs
        move = (home_ref, here_ref, sent, landed)

        @pl.when(pair == 0)
        def _():
            greet([neighbours()[2]])
            move_start(*move)

    rows = q_ref.shape[0]
    marks = mark_q[...]
    queries = jnp.concatenate(
        [two_heads(scaled_down(q_ref[...])), jnp.concatenate([marks, marks], 0)], 1
    )
    scores = dot_as(jnp.concatenate([k_ref[...], mark_k[...]], 1), queries, NT)
    highest = jnp.max(scores, 0, keepdims=True)
    powers = jnp.exp(scores - highest)
    total = jnp.sum(powers, 0, keepdims=True)
    chances = (powers * (1.0 / total)).astype(BF16)
    chance_ref[0] = chances[:, :rows]
    chance_ref[1] = chances[:, rows:]
    out_ref[...] = own_rows(dot_as(jnp.transpose(v_ref[...]), chances, NN)).astype(BF16)
    log_total = highest + jnp.log(total)
    lse_ref[pl.ds(2 * pair, 1), :] = log_total[:, :rows]
    lse_ref[pl.ds(2 * pair + 1, 1), :] = log_total[:, rows:]

    if ways is not None:

        @pl.when(pair == pl.num_programs(0) - 1)
        def _():
            move_landed(*move)
            move_sent(*move)


def query_grads(chance_ref, grad, keys, values, deltas, sub=1024):
    turned, grads = jnp.transpose(keys), two_heads(grad)
    delta = jnp.concatenate(deltas, 1)
    total = jnp.zeros((LANES, grads.shape[0]), F32)
    for first in range(0, keys.shape[0], sub):
        at = slice(first, first + sub)
        grad_chances = dot_as(values[at], grads, NT)
        chances = jnp.concatenate([chance_ref[0, at, :], chance_ref[1, at, :]], 1)
        scores = (chances.astype(F32) * (grad_chances - delta)).astype(BF16)
        total += dot_as(turned[:, at], scores, NN)
    return scaled_down(own_rows(total)).astype(BF16)


def key_grads(key, value, mark_k, parts):
    rows = key.shape[0]
    keys = jnp.concatenate([two_heads(key), jnp.concatenate([mark_k, mark_k], 0)], 1)
    values = two_heads(value)
    dk = dv = jnp.zeros((2 * rows, LANES), F32)
    for queries, grads, marks, log_totals, deltas in parts:
        scores = dot_as(keys, jnp.concatenate([scaled_down(queries), marks], 1), NT)
        grad_chances = dot_as(values, grads, NT)
        chances, grad_scores = [], []
        for head in range(2):
            at = slice(head * rows, (head + 1) * rows)
            powers = jnp.exp(scores[at] - log_totals[head])
            chances.append(powers.astype(BF16))
            grad_scores.append((powers * (grad_chances[at] - deltas[head])).astype(BF16))
        dv += dot_as(jnp.concatenate(chances, 0), grads, NN)
        dk += dot_as(jnp.concatenate(grad_scores, 0), queries, NN)
    return scaled_down(own_columns(dk)).astype(BF16), own_columns(dv).astype(BF16)


def grad_query_kernel(chance_ref, grad_ref, k_ref, v_ref, delta_ref, dq_ref):
    pair = pl.program_id(0)
    deltas = [delta_ref[pl.ds(2 * pair + head, 1), :] for head in range(2)]
    dq_ref[...] = query_grads(chance_ref, grad_ref[...], k_ref[...], v_ref[...], deltas)


def grad_key_kernel(pieces, k_ref, v_ref, q_ref, *refs):
    g_refs = refs[:pieces]
    lse_refs, delta_refs = refs[pieces : 2 * pieces], refs[2 * pieces : 3 * pieces]
    mark_k, mark_q, dk_ref, dv_ref = refs[3 * pieces :]
    pair = pl.program_id(0)
    rows = g_refs[0].shape[0]
    parts = []
    for i in range(pieces):
        at = pl.ds(i * rows, rows)
        stats = [
            [ref[i][pl.ds(2 * pair + head, 1), :] for head in range(2)]
            for ref in (lse_refs, delta_refs)
        ]
        parts.append((q_ref[at, :], g_refs[i][...], mark_q[at, :], *stats))
    dk_ref[...], dv_ref[...] = key_grads(k_ref[...], v_ref[...], mark_k[...], parts)


def columns(rows, first):
    return pl.BlockSpec((rows, LANES), lambda t: (0, first + t))


def whole(array):
    return pl.BlockSpec(array.shape, lambda t: (0,) * array.ndim)


def kernel_call(kernel, name, grid, in_specs, out_specs, out_shape, scratch, flops, moved, **params):
    return pl.pallas_call(
        kernel,
        grid=grid,
        in_specs=in_specs,
        out_specs=out_specs,
        out_shape=out_shape,
        scratch_shapes=scratch,
        compiler_params=pltpu.CompilerParams(vmem_limit_bytes=VMEM_BYTES, **params),
        cost_estimate=pl.CostEstimate(flops=flops, bytes_accessed=moved, transcendentals=0),
        name=name,
    )


def attend(plan, own, projected, mark_q, mark_k, cotangent):
    rows, width = mark_q.shape[0], own.shape[1] // 3
    length, pairs = projected.shape[0], width // LANES
    stats = jax.ShapeDtypeStruct((STATS, rows), F32)
    anywhere = pl.BlockSpec(memory_space=pl.ANY)
    ways = plan.ways
    moving = [] if ways is None else [cotangent]
    params = {} if ways is None else {"collective_id": 1, "has_side_effects": True}
    results = kernel_call(
        functools.partial(attend_kernel, ways),
        "attend",
        (pairs,),
        [
            columns(rows, 0),
            columns(length, pairs),
            columns(length, 2 * pairs),
            whole(mark_q),
            whole(mark_k),
        ]
        + [anywhere] * len(moving),
        [
            columns(rows, 0),
            pl.BlockSpec((2, length, rows), lambda t: (t, 0, 0)),
            whole(stats),
        ]
        + [anywhere] * len(moving),
        [
            jax.ShapeDtypeStruct((rows, width), BF16),
            jax.ShapeDtypeStruct((2 * pairs, length, rows), BF16),
            stats,
        ]
        + [jax.ShapeDtypeStruct(array.shape, array.dtype) for array in moving],
        [pltpu.SemaphoreType.DMA] * (2 * len(moving)),
        24 * rows * length * width,
        4 * pairs * rows * length,
        **params,
    )(own, projected, projected, mark_q, mark_k, *moving)
    return tuple(results) if moving else tuple(results) + (cotangent,)


def grad_query(chances, grad, projected, deltas):
    rows, width = grad.shape
    length, pairs = projected.shape[0], width // LANES
    return kernel_call(
        grad_query_kernel,
        "grad_query",
        (pairs,),
        [
            pl.BlockSpec((2, length, rows), lambda t: (t, 0, 0)),
            columns(rows, 0),
            columns(length, pairs),
            columns(length, 2 * pairs),
            whole(deltas),
        ],
        columns(rows, 0),
        jax.ShapeDtypeStruct((rows, width), BF16),
        [],
        16 * rows * length * width,
        4 * pairs * rows * length,
    )(chances, grad, projected, projected, deltas)


def grad_key_value(own, projected, grads, log_totals, deltas, mark_k, mark_q):
    rows, width = grads[0].shape
    pieces, pairs = len(grads), width // LANES
    length = rows * pieces
    result = jax.ShapeDtypeStruct((rows, width), BF16)
    return kernel_call(
        functools.partial(grad_key_kernel, pieces),
        "grad_key_value",
        (pairs,),
        [columns(rows, pairs), columns(rows, 2 * pairs), columns(length, 0)]
        + [columns(rows, 0)] * pieces
        + [whole(log_totals[0])] * (2 * pieces)
        + [whole(mark_k), whole(mark_q)],
        [columns(rows, 0)] * 2,
        [result] * 2,
        [],
        32 * rows * length * width,
        8 * length * width,
    )(own, own, projected, *grads, *log_totals, *deltas, mark_k, mark_q)


class Chunk:
    stages = ("start", "near", "far", "along", "meet", "spread", "finish")

    def __init__(self, source, rows, columns, y_first, when, held=False, dtype=BF16):
        self.source, self.rows, self.columns = source, rows, columns
        self.shape = (rows[1], columns[1])
        self.blocks = ((2, 3), 1) if y_first else ((1, 3), 2)
        self.y_first, self.when, self.held, self.dtype = y_first, when, held, dtype

    def scratch(self):
        rows, columns = self.shape
        lead = [(4,), (2,), (), (), ()] if self.held else [(4,), (2,), (), (), (), (4,)]
        return [pltpu.VMEM(first + (rows, columns), self.dtype) for first in lead] + [
            pltpu.SemaphoreType.DMA((7,)),
            pltpu.SemaphoreType.DMA((8,)),
        ]

    def bind(self, source, out, scratch, devices):
        at = (pl.ds(*self.rows), pl.ds(*self.columns))
        kept = source.at[(pl.ds(0, 4),) + at]
        self.out = out.at[at]
        core, first, second, z1, z2, *rest = scratch
        *rest, sent, landed = rest
        self.keep = kept if self.held else rest[0]
        self.core, self.first, self.second, self.z1, self.z2 = core, first, second, z1, z2
        near, far = (devices["y"], devices["x"]) if self.y_first else (devices["x"], devices["y"])
        sends, last = self.blocks
        self.load = pltpu.make_async_copy(kept, self.keep, landed.at[7])
        self.to_core = remote(
            source.at[(pl.ds(4, 4),) + at], core, sent.at[0], landed.at[0], devices["core"]
        )
        self.to_near = [
            remote(self.keep.at[b], first.at[i], sent.at[1 + i], landed.at[1 + i], near)
            for i, b in enumerate(sends)
        ]
        self.to_far = remote(self.keep.at[last], second, sent.at[3], landed.at[3], far)
        self.inward = remote(self.keep.at[0], z1, sent.at[4], landed.at[4], devices["pair"])
        self.middle = remote(self.keep.at[0], z2, sent.at[5], landed.at[5], devices["mirror"])
        self.outward = remote(z1, self.out, sent.at[6], landed.at[6], devices["pair"])
        self.store = pltpu.make_async_copy(z1, self.out, landed.at[6])

    def add(self, target, one, other):
        size = 32 if self.shape[0] % 32 == 0 else 16

        def step(i, carry):
            at = pl.ds(pl.multiple_of(i * size, size), size)
            target[at, :] = one[at, :] + other[at, :]
            return carry

        lax.fori_loop(0, self.shape[0] // size, step, 0)

    def start(self):
        self.to_core.start()
        if not self.held:
            self.load.start()

    def near(self):
        if not self.held:
            self.load.wait()
        self.to_core.wait_recv()
        sends = self.blocks[0]
        for block in sends:
            self.add(self.keep.at[block], self.keep.at[block], self.core.at[block])
        for copy in self.to_near:
            copy.start()
        for block in range(4):
            if block not in sends:
                self.add(self.keep.at[block], self.keep.at[block], self.core.at[block])

    def far(self):
        stay = [b for b in range(4) if b not in self.blocks[0]]
        for i in (1, 0):
            self.to_near[i].wait_recv()
            self.add(self.keep.at[stay[i]], self.keep.at[stay[i]], self.first.at[i])
            if stay[i] == self.blocks[1]:
                self.to_far.start()

    def along(self):
        self.to_far.wait_recv()
        self.add(self.keep.at[0], self.keep.at[0], self.second)

        @pl.when(jnp.logical_not(inner()))
        def _():
            self.inward.start()

    def meet(self):
        @pl.when(inner())
        def _():
            self.inward.wait_recv()
            self.add(self.keep.at[0], self.keep.at[0], self.z1)
            self.middle.start()

    def spread(self):
        @pl.when(inner())
        def _():
            self.middle.wait_recv()
            self.add(self.z1, self.keep.at[0], self.z2)
            self.outward.start()
            self.store.start()

    def finish(self):
        @pl.when(jnp.logical_not(inner()))
        def _():
            self.outward.wait_recv()
            self.inward.wait_send()

        @pl.when(inner())
        def _():
            self.store.wait()
            self.middle.wait_send()
            self.outward.wait_send()

        self.to_core.wait_send()
        for copy in self.to_near:
            copy.wait_send()
        self.to_far.wait_send()


def inner():
    z = lax.axis_index("seq")
    return jnp.logical_and(z > 0, z < 3)


def ring_devices():
    dp, z = lax.axis_index("dp"), lax.axis_index("seq")
    core, pair, swap = neighbours()
    x = dp + 2 - 4 * lax.rem(lax.div(dp, jnp.int32(2)), jnp.int32(2))
    y = dp + 4 - 8 * lax.div(dp, jnp.int32(4))
    return {
        "core": core,
        "pair": pair,
        "swap": swap,
        "x": (x, z),
        "y": (y, z),
        "mirror": (dp, 3 - z),
    }


def relative_place(block):
    dp = lax.axis_index("dp")
    bits = [lax.rem(lax.div(dp, jnp.int32(1 << k)) + (block >> k) % 2, jnp.int32(2)) for k in range(3)]
    return bits[0] * 4 + bits[1] + bits[2] * 2


def store_blocks(target, columns, total):
    part = total.shape[0] // 8
    for block in range(8):
        target[relative_place(block), :, columns] = total[block * part : (block + 1) * part].astype(BF16)


VECTORS = 16


def backward_chunks(shapes, width, pairs):
    down, up, out = shapes
    third, share = down[1] // 3, up[2] // 3
    part = width // 8
    end = 4 * pairs

    def when(*steps):
        return tuple(at if isinstance(at, tuple) else (at, 0) for at in steps)

    tile = 2 * LANES
    ends = [tuple((end, i) for i in range(n)) for n in range(8)]
    return [
        Chunk("down", (0, third), (0, width), True, when(0, 2, 8, 14, 16, 18)),
        Chunk("down", (third, third), (0, width), False, when(0, 2, 8, 14, 16, 18)),
        Chunk("up", (0, part), (0, share), True, when(1, 4, 12, 17, 19, 21)),
        Chunk("up", (0, part), (share, share), False, when(1, 4, 12, 17, 19, 21)),
        Chunk("down", (2 * third, third), (0, width), True, when(3, 10, 16, 20, 21, 23)),
        Chunk("up", (0, part), (2 * share, share), False, when(3, 10, 16, 20, 21, 23)),
        Chunk("out", (0, part), (0, width), True, when(6, 13, 19, 22, 23, (end, 1))),
        Chunk("query", (0, part), (0, width), False, when(12, 13, 19, 22, 23, (end, 1)), True),
        Chunk("pair", (0, part), (0, 2 * tile), True, when(20, 21, 23, *ends[4][1:]), True),
        Chunk("pair", (0, part), (2 * tile, 2 * tile), False, when(22, 23, *ends[5][1:]), True),
        Chunk("pair", (0, part), (4 * tile, tile), True, when(23, *ends[6][1:]), True),
        Chunk("pair", (0, part), (5 * tile, tile), False, when((end, 0), *ends[7][2:]), True),
        Chunk(
            "vector",
            (0, VECTORS),
            (0, LANES),
            True,
            when((end, 0), *ends[7][2:]),
            True,
            F32,
        ),
    ]


def backward_kernel(
    shapes,
    pairs,
    chance_ref,
    grad_ref,
    attended_ref,
    k_ref,
    v_ref,
    q_ref,
    mark_k,
    mark_q,
    lse_ref,
    gain_ref,
    sums_ref,
    sum_up_ref,
    w_hbm,
    hidden_hbm,
    here_hbm,
    middle_hbm,
    grad_down,
    grad_up,
    grad_out,
    block_ref,
    home_ref,
    tokens_ref,
    down_ref,
    up_ref,
    out_ref,
    query_ref,
    pair_ref,
    vector_ref,
    grads,
    stats,
    own_stats,
    turned,
    dq,
    dkv,
    grad_hidden,
    query_grad,
    pair_grad,
    vector,
    late,
    tokens,
    weights,
    hidden_ref,
    here_ref,
    middle_ref,
    sent,
    landed,
    loaded,
    *scratch,
):
    step = pl.program_id(0)
    rows, width = grad_ref.shape
    held = ((hidden_hbm, hidden_ref), (w_hbm, weights), (here_hbm, here_ref), (middle_hbm, middle_ref))
    loads = [
        pltpu.make_async_copy(source, target, loaded.at[i])
        for i, (source, target) in enumerate(held)
    ]
    half = rows // 2
    first, steps = 2 * pairs, 4 * pairs
    devices = ring_devices()
    chunks = backward_chunks(shapes, width, pairs)
    sources = {
        "down": (grad_down, down_ref),
        "up": (grad_up, up_ref),
        "out": (grad_out, out_ref),
        "query": (query_grad, query_ref),
        "pair": (pair_grad, pair_ref),
        "vector": (vector, vector_ref),
    }
    scratch = list(scratch)
    for chunk in chunks:
        count = len(chunk.scratch())
        chunk.bind(*sources[chunk.source], scratch[:count], devices)
        del scratch[:count]
    block_move = (block_ref, home_ref, sent.at[12], landed.at[12])

    def token_move(part):
        at = pl.ds(part * half, half)
        return (tokens.at[at], tokens_ref.at[at], sent.at[13 + part], landed.at[13 + part])

    def grad_copy(i, part, source, device):
        at = pl.ds(part * half, half)
        n = 2 * i + part
        return remote(source.at[at], grads.at[i, at], sent.at[n], landed.at[n], device)

    def to_core(part):
        return grad_copy(1, part, grad_ref, devices["core"])

    def to_pair(part):
        return grad_copy(2, part, grad_ref, devices["pair"])

    def to_corner(part):
        return grad_copy(3, part, grads.at[2], devices["core"])

    def stat_copy(i, source, device):
        return remote(source, stats.at[i], sent.at[8 + i], landed.at[8 + i], device)

    stat_core = stat_copy(1, own_stats, devices["core"])
    stat_pair = stat_copy(2, own_stats, devices["pair"])
    stat_corner = stat_copy(3, stats.at[2], devices["core"])

    def begin():
        greet(list(devices.values()))
        for part in range(2):
            to_pair(part).start()
        for part in range(2):
            to_core(part).start()
        for load in loads:
            load.start()

    def begin_stats():
        product = grad_ref[...].astype(F32) * attended_ref[...].astype(F32)
        high = product.astype(BF16)
        low = (product - high.astype(F32)).astype(BF16)
        head = lax.broadcasted_iota(jnp.int32, (STATS, width), 0)
        column = lax.broadcasted_iota(jnp.int32, (STATS, width), 1)
        mine = jnp.where(
            jnp.logical_and(column >= head * HDIM, column < (head + 1) * HDIM), 1.0, 0.0
        ).astype(BF16)
        own_stats[0:STATS, :] = lse_ref[...]
        own_stats[STATS:, :] = dot_as(mine, high, NT) + dot_as(mine, low, NT)
        stats[0] = own_stats[...]
        grads[0] = grad_ref[...]
        stat_pair.start()
        stat_core.start()
        late[...] = jnp.zeros_like(late)

    def corner_stats():
        stat_pair.wait_recv()
        stat_corner.start()

    def corner(part):
        def run():
            to_pair(part).wait_recv()
            to_corner(part).start()

        return run

    def all_grads():
        stat_core.wait_recv()
        stat_corner.wait_recv()
        for part in range(2):
            to_core(part).wait_recv()
            to_corner(part).wait_recv()

    def query_done():
        for load in loads:
            load.wait()
        turned[...] = jnp.transpose(hidden_ref[...])
        store_blocks(query_grad, pl.ds(0, width), dot_as(turned[...], dq[...], NN))
        grad_hidden[...] = dot_as(dq[...], weights[:, 0:width], NT)
        late[0:1, :] = jnp.sum(dq[...].astype(F32), 0, keepdims=True)

    def first_norm(part):
        def run():
            at = pl.ds(part * half, half)
            _, unit, root = layer_norm(here_ref[at, :].astype(F32), 0.0, 0.0)
            grad = grad_hidden[at, :]
            scaled = grad * row_of(gain_ref)
            grad_in = root * (
                scaled
                - jnp.mean(scaled, -1, keepdims=True)
                - unit * jnp.mean(scaled * unit, -1, keepdims=True)
            )
            tokens[at, :] = (middle_ref[at, :] + grad_in).astype(BF16)
            move_start(*token_move(part))
            late[2:3, :] += jnp.sum(grad * unit, 0, keepdims=True)
            late[3:4, :] += jnp.sum(grad, 0, keepdims=True)

        return run

    def early_vectors():
        share = width // 8
        vector[...] = jnp.zeros_like(vector)
        for block in range(8):
            place = relative_place(block)
            vector[place, 0:4, 0:share] = sums_ref[0:4, block * share : (block + 1) * share]
            for i in range(4):
                first = (block * 4 + i) * share
                vector[place, 8 + i : 9 + i, 0:share] = sum_up_ref[0:1, first : first + share]

    def late_vectors():
        share = width // 8
        for block in range(8):
            vector[relative_place(block), 4:8, 0:share] = late[
                0:4, block * share : (block + 1) * share
            ]

    def finish_moves():
        for move in (block_move, token_move(0), token_move(1)):
            move_landed(*move)
            move_sent(*move)
        for copy in (stat_core, stat_pair, stat_corner):
            copy.wait_send()
        for part in range(2):
            to_core(part).wait_send()
            to_pair(part).wait_send()
            to_corner(part).wait_send()

    events = [
        ((0, -2), begin),
        ((0, 1), begin_stats),
        ((4, -1), corner_stats),
        ((4, 2), early_vectors),
        ((8, -1), corner(0)),
        ((first, -2), corner(1)),
        ((first, -1), query_done),
        ((first, 3), lambda: move_start(*block_move)),
        ((first, 4), all_grads),
        ((first + pairs, -1), first_norm(0)),
        ((steps, -2), first_norm(1)),
        ((steps, -1), late_vectors),
        ((steps, 9), finish_moves),
    ]
    for order in (2, 1, 0, 3, 4, 5, 6):
        for chunk in chunks:
            at = chunk.when[order] if order < 6 else (steps, 8)
            events.append((at, getattr(chunk, Chunk.stages[order])))
    events.sort(key=lambda event: event[0])

    def run(at):
        for (when, _), event in events:
            if when == at:
                event()

    for at in range(steps):
        if any(when == at for (when, _), _ in events):

            @pl.when(step == at)
            def _():
                run(at)

    @pl.when(step < first)
    def _():
        pair = lax.div(step, jnp.int32(2))
        at = pl.ds(pl.multiple_of(lax.rem(step, jnp.int32(2)) * half, half), half)
        tile = pl.ds(pl.multiple_of(pair * LANES, LANES), LANES)
        deltas = [own_stats[pl.ds(STATS + 2 * pair + head, 1), at] for head in range(2)]
        dq[at, tile] = query_grads(chance_ref, grad_ref[at, tile], k_ref[...], v_ref[...], deltas)

    @pl.when(step >= first)
    def _():
        pair = lax.rem(step, jnp.int32(pairs))
        at = pl.ds(pl.multiple_of((lax.div(step, jnp.int32(pairs)) - 2) * half, half), half)
        tile = pl.ds(pl.multiple_of(pair * LANES, LANES), LANES)
        double = pl.ds(pl.multiple_of(pair * (2 * LANES), 2 * LANES), 2 * LANES)

        def weight(part):
            return weights[:, pl.ds(pl.multiple_of(part * width + pair * LANES, LANES), LANES)]

        parts = []
        for i in range(4):
            span = pl.ds(i * rows, rows)
            rows_of = [
                [stats[i, pl.ds(start + 2 * pair + head, 1), :] for head in range(2)]
                for start in (0, STATS)
            ]
            parts.append((q_ref[span, :], grads[i, :, tile], mark_q[span, :], *rows_of))
        dk, dv = key_grads(k_ref[at, :], v_ref[at, :], mark_k[at, :], parts)
        both = jnp.concatenate([dk, dv], 1)
        dkv[at, double] = both
        grad_hidden[at, :] += dot_as(both, jnp.concatenate([weight(1), weight(2)], 1), NT)
        late[1:2, tile] += jnp.sum(dv.astype(F32), 0, keepdims=True)

        @pl.when(step >= first + pairs)
        def _():
            store_blocks(pair_grad, double, dot_as(turned[...], dkv[:, double], NN))

    @pl.when(step == steps - 1)
    def _():
        run(steps)


def once(array):
    return pl.BlockSpec(array.shape, lambda *t: (0,) * array.ndim, pipeline_mode=pl.Buffered(1))


def backward(
    chances,
    grad,
    attended,
    projected,
    mark_k,
    mark_q,
    log_totals,
    weight,
    hidden,
    here,
    grad_middle,
    gain,
    sums,
    sum_up,
    totals,
    block_out,
):
    rows, width = grad.shape
    length, pairs = projected.shape[0], width // LANES
    shapes = [total.shape for total in totals]
    part = width // 8
    anywhere = pl.BlockSpec(memory_space=pl.ANY)
    result = jax.ShapeDtypeStruct((rows, width), BF16)
    outs = [result, result] + [
        jax.ShapeDtypeStruct(shape, BF16)
        for shape in [shape[1:] for shape in shapes] + [(part, width), (part, 2 * width)]
    ]
    outs.append(jax.ShapeDtypeStruct((VECTORS, LANES), F32))

    def pair_at(t):
        return jnp.where(t < 2 * pairs, lax.div(t, 2), lax.rem(t, pairs))

    def tile(first):
        return pl.BlockSpec((length, LANES), lambda t: (0, first + pair_at(t)))

    def chance_at(t):
        t = jnp.minimum(t, 2 * pairs - 1)
        return lax.div(t, 2), 0, lax.rem(t, 2)

    fixed = [mark_k, mark_q, log_totals, gain, sums, sum_up]
    held = [weight, hidden, here, grad_middle]
    chunks = backward_chunks(shapes, width, pairs)
    stats = (2 * STATS, rows)
    return kernel_call(
        functools.partial(backward_kernel, shapes, pairs),
        "backward",
        (4 * pairs,),
        [
            pl.BlockSpec((2, length, rows // 2), chance_at),
            once(grad),
            once(attended),
            tile(pairs),
            tile(2 * pairs),
            pl.BlockSpec((length, LANES), lambda t: (0, lax.rem(jnp.maximum(t - 2 * pairs, 0), pairs))),
        ]
        + [once(array) for array in fixed]
        + [anywhere] * (len(held) + len(totals) + 1),
        [anywhere] * len(outs),
        outs,
        [
            pltpu.VMEM((4, rows, width), BF16),
            pltpu.VMEM((4,) + stats, F32),
            pltpu.VMEM(stats, F32),
            pltpu.VMEM((width, rows), BF16),
            pltpu.VMEM((rows, width), BF16),
            pltpu.VMEM((rows, 2 * width), BF16),
            pltpu.VMEM((rows, width), F32),
            pltpu.VMEM((8, part, width), BF16),
            pltpu.VMEM((8, part, 2 * width), BF16),
            pltpu.VMEM((8, VECTORS, LANES), F32),
            pltpu.VMEM((8, width), F32),
            pltpu.VMEM((rows, width), BF16),
        ]
        + [pltpu.VMEM(array.shape, array.dtype) for array in held]
        + [
            pltpu.SemaphoreType.DMA((15,)),
            pltpu.SemaphoreType.DMA((15,)),
            pltpu.SemaphoreType.DMA((len(held),)),
        ]
        + [entry for chunk in chunks for entry in chunk.scratch()],
        48 * rows * length * width,
        4 * pairs * rows * length,
        collective_id=2,
        has_side_effects=True,
    )(chances, grad, attended, projected, projected, projected, *fixed, *held, *totals, block_out)


def results_kernel(block, tokens, down, up, out, query, pair, vector, *outs):
    (
        block_ref,
        tokens_ref,
        ln1_gain,
        ln1_shift,
        w_qkv,
        bias_query,
        bias_value,
        w_out,
        bias_out,
        ln2_gain,
        ln2_shift,
        w_up,
        bias_up,
        w_down,
        bias_down,
    ) = outs
    block_ref[...] = block[...]
    tokens_ref[...] = tokens[...]
    width = query.shape[1]
    w_qkv[:, 0:width] = query[...].astype(F32)
    for i in range(width // LANES):
        for j in range(2):
            first = (2 * i + j) * LANES
            to = (1 + j) * width + i * LANES
            w_qkv[:, to : to + LANES] = pair[:, first : first + LANES].astype(F32)
    w_up[...] = up[...].astype(F32)
    w_down[...] = down[...].astype(F32)
    w_out[...] = out[...].astype(F32)
    share = width // 8
    order = (ln2_gain, ln2_shift, bias_out, bias_down, bias_query, bias_value, ln1_gain, ln1_shift)
    for i, ref in enumerate(order):
        ref[...] = vector[i, 0:share]
    bias_up[...] = jnp.concatenate([vector[8 + i : 9 + i, 0:share] for i in range(4)], 1)[0]


def results(block, tokens, down, up, out, query, pair, vector):
    part, width = query.shape
    vmem = pl.BlockSpec(memory_space=pltpu.VMEM)

    def line(size=part):
        return jax.ShapeDtypeStruct((size,), F32)

    def like(array):
        return jax.ShapeDtypeStruct(array.shape, F32)

    return pl.pallas_call(
        results_kernel,
        in_specs=[vmem] * 8,
        out_specs=[vmem] * 15,
        out_shape=[
            jax.ShapeDtypeStruct(block.shape, BF16),
            jax.ShapeDtypeStruct(tokens.shape, BF16),
            line(),
            line(),
            jax.ShapeDtypeStruct((part, 3 * width), F32),
            line(),
            line(),
            like(out),
            line(),
            line(),
            line(),
            like(up),
            line(4 * part),
            like(down),
            line(),
        ],
        compiler_params=pltpu.CompilerParams(vmem_limit_bytes=VMEM_BYTES),
        name="results",
    )(block, tokens, down, up, out, query, pair, vector)


def gelu_parts(pre_act):
    inside = 0.5 * (1.0 + lax.erf(pre_act * math.sqrt(0.5)))
    slope = inside + pre_act * jnp.exp(-0.5 * pre_act * pre_act) * (1.0 / math.sqrt(2.0 * math.pi))
    return pre_act * inside, slope


def relative(block, me):
    turned = block ^ me
    return (turned % 2) * 4 + turned // 2


def feed_kernel(
    sub,
    index_ref,
    here_ref,
    attended_ref,
    grad_ref,
    w_out_ref,
    bias_out_ref,
    gain_ref,
    shift_ref,
    w_up_ref,
    bias_up_ref,
    w_down_ref,
    bias_down_ref,
    block_ref,
    grad_attended_ref,
    grad_middle_ref,
    down_ref,
    up_ref,
    out_ref,
    sum_up_ref,
    sums_ref,
    middle,
    normed,
    inverse,
    hidden,
    turned,
    total,
    grad_hidden,
    activated,
    grad_upper,
):
    step, last = pl.program_id(0), pl.num_programs(0) - 1
    me = index_ref[0]
    rows, width = here_ref.shape
    blocks = rows // sub

    def span(i):
        return pl.ds(pl.multiple_of(i * sub, sub), sub)

    @pl.when(step == 0)
    def _():
        def norm(i, carry):
            at = span(i)
            values = (
                here_ref[at, :].astype(F32)
                + dot_as(attended_ref[at, :], w_out_ref[...], NN)
                + row_of(bias_out_ref)
            )
            out, unit, root = layer_norm(values, row_of(gain_ref), row_of(shift_ref))
            middle[at, :] = values
            normed[at, :] = unit
            inverse[at, :] = jnp.broadcast_to(root, (sub, LANES))
            hidden[at, :] = out.astype(BF16)
            total[at, :] = values + row_of(bias_down_ref)
            grad_hidden[at, :] = jnp.zeros((sub, width), F32)
            return carry

        lax.fori_loop(0, blocks, norm, 0)
        turned[...] = jnp.transpose(hidden[...])

    def tile(i, carry):
        at = span(i)
        upper = dot_as(hidden[at, :], w_up_ref[...], NN) + bias_up_ref[...]
        grad_activated = dot_as(grad_ref[at, :], w_down_ref[...], NT)
        active, slope = gelu_parts(upper)
        active = active.astype(BF16)
        grad_in = (grad_activated * slope).astype(BF16)
        activated[at, :] = active
        grad_upper[at, :] = grad_in
        total[at, :] += dot_as(active, w_down_ref[...], NN)
        grad_hidden[at, :] += dot_as(grad_in, w_up_ref[...], NT)
        return carry + jnp.sum(grad_in.astype(F32), 0, keepdims=True)

    sum_up_ref[...] = lax.fori_loop(0, blocks, tile, jnp.zeros(sum_up_ref.shape, F32))

    grad_up = dot_as(turned[...], grad_upper[...], NN)
    part = width // 8
    for block in range(8):
        up_ref[relative(block, me)] = grad_up[block * part : (block + 1) * part].astype(BF16)
    grad_down = inner_rows(activated[...], grad_ref[...])
    part = down_ref.shape[2]
    for i in range(2):
        down_ref[(i ^ me) % 2, 0] = grad_down[i * part : (i + 1) * part].astype(BF16)

    @pl.when(step == last)
    def _():
        def norm(i, carry):
            at = span(i)
            block_ref[at, :] = total[at, :].astype(BF16)
            grad, unit = grad_hidden[at, :], normed[at, :]
            scaled = grad * row_of(gain_ref)
            grad_in = inverse[at, 0:1] * (
                scaled
                - jnp.mean(scaled, -1, keepdims=True)
                - unit * jnp.mean(scaled * unit, -1, keepdims=True)
            )
            before = grad_ref[at, :].astype(F32)
            grad_in = before + grad_in
            branch = grad_in.astype(BF16)
            grad_middle_ref[at, :] = grad_in
            hidden[at, :] = branch
            grad_attended_ref[at, :] = dot_as(branch, w_out_ref[...], NT).astype(BF16)
            sums = [grad * unit, grad, branch.astype(F32), before]
            return tuple(
                old + jnp.sum(value, 0, keepdims=True) for old, value in zip(carry, sums)
            )

        zero = jnp.zeros((1, width), F32)
        sums = lax.fori_loop(0, blocks, norm, (zero,) * 4)
        sums_ref[...] = jnp.concatenate(list(sums) + [zero] * 4, 0)
        grad_out = inner_rows(attended_ref[...], hidden[...])
        part = width // 8
        for block in range(8):
            out_ref[relative(block, me)] = grad_out[block * part : (block + 1) * part].astype(BF16)


def feed(
    here, attended, grad, w_out, bias_out, gain, shift, w_up, bias_up, w_down, bias_down, me, sub=256
):
    rows, width = here.shape
    wide = w_up.shape[1]
    steps = 4
    tile = wide // steps
    part = width // 8

    def once(*shape):
        return pl.BlockSpec(shape, lambda f, at: (0,) * len(shape), pipeline_mode=pl.Buffered(1))

    act = once(rows, width)
    line = once(width)
    outs = [
        jax.ShapeDtypeStruct((rows, width), BF16),
        jax.ShapeDtypeStruct((rows, width), BF16),
        jax.ShapeDtypeStruct((rows, width), F32),
        jax.ShapeDtypeStruct((2, 4, wide // 8, width), BF16),
        jax.ShapeDtypeStruct((8, part, wide), BF16),
        jax.ShapeDtypeStruct((8, part, width), BF16),
        jax.ShapeDtypeStruct((1, wide), F32),
        jax.ShapeDtypeStruct((8, width), F32),
    ]
    return pl.pallas_call(
        functools.partial(feed_kernel, sub),
        grid_spec=pltpu.PrefetchScalarGridSpec(
            num_scalar_prefetch=1,
            grid=(steps,),
            in_specs=[
                act,
                act,
                act,
                once(width, width),
                line,
                line,
                line,
                pl.BlockSpec((width, tile), lambda f, at: (0, f)),
                pl.BlockSpec((1, tile), lambda f, at: (0, f)),
                pl.BlockSpec((tile, width), lambda f, at: (f, 0)),
                line,
            ],
            out_specs=[
                act,
                act,
                act,
                pl.BlockSpec((2, 1, wide // 8, width), lambda f, at: (0, f ^ (at[0] // 2), 0, 0)),
                pl.BlockSpec((8, part, tile), lambda f, at: (0, 0, f)),
                once(8, part, width),
                pl.BlockSpec((1, tile), lambda f, at: (0, f)),
                once(8, width),
            ],
            scratch_shapes=[
                pltpu.VMEM((rows, width), F32),
                pltpu.VMEM((rows, width), F32),
                pltpu.VMEM((rows, LANES), F32),
                pltpu.VMEM((rows, width), BF16),
                pltpu.VMEM((width, rows), BF16),
                pltpu.VMEM((rows, width), F32),
                pltpu.VMEM((rows, width), F32),
                pltpu.VMEM((rows, tile), BF16),
                pltpu.VMEM((rows, tile), BF16),
            ],
        ),
        out_shape=outs,
        compiler_params=pltpu.CompilerParams(vmem_limit_bytes=VMEM_BYTES),
        cost_estimate=pl.CostEstimate(
            flops=12 * rows * width * wide, bytes_accessed=8 * width * wide, transcendentals=0
        ),
        name="feed",
    )(
        me,
        here,
        attended,
        grad,
        w_out,
        bias_out,
        gain,
        shift,
        w_up,
        bias_up.reshape(1, -1),
        w_down,
        bias_down,
    )


def start_kernel(
    tokens_ref,
    lengths_ref,
    gain_ref,
    shift_ref,
    w_ref,
    bias_ref,
    projected_ref,
    hidden_ref,
    here_ref,
    found_ref,
    rows,
    staged,
    sent,
    landed,
    out_sem,
):
    core, across, swap = neighbours()
    parts = sent.shape[1]
    height = tokens_ref.shape[0]
    part = height // parts
    greet([core, across, swap])

    def span(i):
        return pl.ds(pl.multiple_of(i * part, part), part)

    def moved(i):
        return (tokens_ref.at[span(i)], rows.at[0, span(i)], sent.at[0, i], landed.at[0, i])

    def lengths():
        return remote(lengths_ref, found_ref, sent.at[4, 0], landed.at[4, 0], core)

    def forward(i, origin, piece, device):
        return remote(
            rows.at[origin, span(i)],
            rows.at[piece, span(i)],
            sent.at[piece, i],
            landed.at[piece, i],
            device,
        )

    def out_span(piece, i):
        return pl.ds(pl.multiple_of(piece * height + i * part, part), part)

    def to_hbm(piece, i):
        at = out_span(piece, i)
        return pltpu.make_async_copy(staged.at[at], projected_ref.at[at], out_sem.at[piece, i])

    def project(piece, i):
        values = rows[piece, span(i), :].astype(F32)
        hidden = layer_norm(values, row_of(gain_ref), row_of(shift_ref))[0].astype(BF16)
        staged[out_span(piece, i), :] = (
            dot_as(hidden, w_ref[...], NN) + row_of(bias_ref)
        ).astype(BF16)
        to_hbm(piece, i).start()
        return hidden

    for i in range(parts):
        move_start(*moved(i))
    lengths().start()

    def first(i, carry):
        move_landed(*moved(i))
        forward(i, 0, 2, across).start()
        forward(i, 0, 1, core).start()
        hidden_ref[span(i), :] = project(0, i)
        here_ref[span(i), :] = rows[0, span(i), :]
        return carry

    lax.fori_loop(0, parts, first, 0)

    def second(i, carry):
        forward(i, 0, 1, core).wait_recv()
        project(1, i)
        forward(i, 0, 2, across).wait_recv()
        forward(i, 2, 3, core).start()
        project(2, i)
        return carry

    lax.fori_loop(0, parts, second, 0)

    def third(i, carry):
        forward(i, 2, 3, core).wait_recv()
        project(3, i)
        return carry

    lax.fori_loop(0, parts, third, 0)
    lengths().wait()

    def last(i, carry):
        move_sent(*moved(i))
        forward(i, 0, 2, across).wait_send()
        forward(i, 0, 1, core).wait_send()
        forward(i, 2, 3, core).wait_send()
        for piece in range(4):
            to_hbm(piece, i).wait()
        return carry

    lax.fori_loop(0, parts, last, 0)


def start_work(tokens, clip_lengths, gain, shift, weight, bias):
    rows, width = tokens.shape
    vmem, anywhere = pl.BlockSpec(memory_space=pltpu.VMEM), pl.BlockSpec(memory_space=pl.ANY)
    projected, hidden, here, found = pl.pallas_call(
        start_kernel,
        in_specs=[anywhere] + [vmem] * 5,
        out_specs=[anywhere, vmem, vmem, vmem],
        out_shape=[
            jax.ShapeDtypeStruct((4 * rows, 3 * width), BF16),
            jax.ShapeDtypeStruct((rows, width), BF16),
            jax.ShapeDtypeStruct((rows, width), BF16),
            jax.ShapeDtypeStruct(clip_lengths.shape, jnp.int32),
        ],
        scratch_shapes=[
            pltpu.VMEM((4, rows, width), BF16),
            pltpu.VMEM((4 * rows, 3 * width), BF16),
            pltpu.SemaphoreType.DMA((5, 4)),
            pltpu.SemaphoreType.DMA((5, 4)),
            pltpu.SemaphoreType.DMA((4, 4)),
        ],
        compiler_params=pltpu.CompilerParams(
            vmem_limit_bytes=VMEM_BYTES, collective_id=0, has_side_effects=True
        ),
        cost_estimate=pl.CostEstimate(
            flops=24 * rows * width * width, bytes_accessed=32 * rows * width, transcendentals=0
        ),
        name="start_work",
    )(tokens, clip_lengths, gain, shift, weight, bias)
    return projected, hidden, here, jnp.where(stays(), clip_lengths, found)


class PairPlan:
    ways = True

    def start(self, tokens, clip_lengths, gain, shift, weight, bias):
        projected, hidden, here, lengths = start_work(
            tokens, clip_lengths, gain, shift, weight, bias
        )
        return projected, projected, hidden, here, lengths

    def positions(self, rows):
        core, z = lax.axis_index("dp") % 2, lax.axis_index("seq")
        found = []
        for piece in range(4):
            c, plane = core ^ (piece % 2), z ^ (piece // 2)
            shard = jnp.where(c == plane // 2, plane, plane ^ 2)
            found.append(shard * rows + jnp.arange(rows, dtype=jnp.int32))
        return jnp.concatenate(found)

    def own(self, gathered):
        return gathered[: gathered.shape[0] // 4]

    def backward(self, work, weights, attention):
        here, hidden1, grad_out, projected, own, mark_k, mark_q = work
        chances, attended, log_totals = attention
        me = lax.axis_index("dp").astype(jnp.int32).reshape(1)
        block_out, grad, grad_middle, down, up, out, sum_up, sums = feed(
            here, attended, grad_out, *weights[2:], me
        )
        return results(
            *backward(
                chances,
                grad,
                attended,
                projected,
                self.own(mark_k),
                mark_q,
                log_totals,
                weights[0],
                hidden1,
                here,
                grad_middle,
                weights[1],
                sums,
                sum_up,
                [down.reshape((8,) + down.shape[2:]), up, out],
                block_out,
            )
        )


class PlainPlan:
    ways = None

    def __init__(self, pieces):
        self.pieces = pieces

    def start(self, tokens, clip_lengths, gain, shift, weight, bias):
        hidden = layer_norm(tokens.astype(F32), gain, shift)[0].astype(BF16)
        own = (matmul(hidden, weight) + bias).astype(BF16)
        projected = lax.all_gather(own, "seq", axis=0, tiled=True)
        return projected, own, hidden, tokens, clip_lengths

    def gather(self, own):
        gathered = lax.all_gather(own, "seq", axis=0, tiled=False)
        return [gathered[i] for i in range(self.pieces)]

    def positions(self, rows):
        return jnp.arange(rows * self.pieces, dtype=jnp.int32)

    def own(self, gathered):
        rows = gathered.shape[0] // self.pieces
        return lax.dynamic_slice_in_dim(gathered, lax.axis_index("seq") * rows, rows, 0)

    def backward(self, work, weights, attention):
        here, hidden1, grad_out, projected, own, mark_k, mark_q = work
        chances, attended, log_totals = attention
        w_qkv, ln1_gain, w_out, bias_out, gain, shift, w_up, bias_up, w_down, bias_down = weights
        middle = here.astype(F32) + matmul(attended, w_out) + bias_out
        normed_out, normed, inverse = layer_norm(middle, gain, shift)
        hidden = normed_out.astype(BF16)
        activated, slope = gelu_parts(matmul(hidden, w_up) + bias_up)
        activated = activated.astype(BF16)
        grad_upper = (inner_cols(grad_out, w_down) * slope).astype(BF16)
        grad_hidden = inner_cols(grad_upper, w_up)
        grad_norm, grad_gain, grad_shift = norm_back(grad_hidden, normed, inverse, gain)
        grad_middle = grad_out.astype(F32) + grad_norm
        grad_branch = grad_middle.astype(BF16)
        grad = inner_cols(grad_branch, w_out).astype(BF16)
        block_out = (middle + matmul(activated, w_down) + bias_down).astype(BF16)

        product = (grad.astype(F32) * attended.astype(F32)).reshape(grad.shape[0], -1, HDIM)
        deltas = jnp.sum(product, -1).T
        deltas = jnp.pad(deltas, ((0, STATS - deltas.shape[0]), (0, 0)))
        dq = grad_query(chances, grad, projected, deltas)
        dk, dv = grad_key_value(
            own,
            projected,
            self.gather(grad),
            self.gather(log_totals),
            self.gather(deltas),
            self.own(mark_k),
            mark_q,
        )
        grad_projected = jnp.concatenate([dq, dk, dv], 1)
        grad_hidden1 = inner_cols(grad_projected, w_qkv)
        _, normed1, inverse1 = layer_norm(here.astype(F32), 0.0, 0.0)
        grad_norm1, grad_ln1_gain, grad_ln1_shift = norm_back(
            grad_hidden1, normed1, inverse1, ln1_gain
        )

        def total(values):
            return jnp.sum(values.astype(F32), 0)

        return (block_out, (grad_middle + grad_norm1).astype(BF16)) + tuple(
            self.reduce(value)
            for value in (
                grad_ln1_gain,
                grad_ln1_shift,
                inner_rows(hidden1, grad_projected),
                total(dq),
                total(dv),
                inner_rows(attended, grad_branch),
                total(grad_branch),
                grad_gain,
                grad_shift,
                inner_rows(hidden, grad_upper),
                total(grad_upper),
                inner_rows(activated, grad_out),
                total(grad_out),
            )
        )

    def reduce(self, total):
        return lax.psum(lax.psum_scatter(total, "dp", scatter_dimension=0, tiled=True), "seq")


def body(
    plan,
    tokens,
    clip_lengths,
    ln1_gain,
    ln1_shift,
    w_qkv,
    bias_query,
    bias_value,
    w_out,
    bias_out,
    ln2_gain,
    ln2_shift,
    w_up,
    bias_up,
    w_down,
    bias_down,
    cotangent,
):
    rows, width = tokens.shape
    bias = jnp.concatenate([bias_query, jnp.zeros_like(bias_query), bias_value])
    projected, own, hidden1, here, lengths = plan.start(
        tokens, clip_lengths, ln1_gain, ln1_shift, w_qkv, bias
    )

    clip_ends = jnp.cumsum(lengths.reshape(-1))
    position = plan.positions(rows)
    segment = jnp.sum((position[:, None] >= clip_ends[None, :]).astype(jnp.int32), 1)
    lane = jnp.arange(LANES, dtype=jnp.int32)[None, :]
    same = lane == segment[:, None]
    mark_k = same.astype(BF16)
    mark_q = jnp.where(same | (lane >= clip_ends.shape[0]), 0.0, masked_score).astype(BF16)

    attended, chances, log_totals, grad_out = attend(
        plan, own, projected, plan.own(mark_q), mark_k, cotangent
    )

    return tuple(
        plan.backward(
            (here, hidden1, grad_out, projected, own, mark_k, mark_q),
            (
                w_qkv,
                ln1_gain,
                w_out,
                bias_out,
                ln2_gain,
                ln2_shift,
                w_up,
                bias_up,
                w_down,
                bias_down,
            ),
            (chances, attended, log_totals),
        )
    )


def solution(mesh):
    sizes = dict(mesh.shape)
    plan = PairPlan() if sizes == {"dp": 8, "seq": 4} else PlainPlan(sizes["seq"])
    rows = P(("dp", "seq"), None)
    return jax.shard_map(
        functools.partial(body, plan),
        mesh=mesh,
        in_specs=(rows, P("dp", None)) + (P(),) * 13 + (rows,),
        out_specs=(
            rows,
            rows,
            P("dp"),
            P("dp"),
            P("dp", None),
            P("dp"),
            P("dp"),
            P("dp", None),
            P("dp"),
            P("dp"),
            P("dp"),
            P("dp", None),
            P("dp"),
            P("dp", None),
            P("dp"),
        ),
        check_vma=False,
    )
```

```python
import functools
import math

import jax
import jax.numpy as jnp
from jax import lax
from jax.experimental import pallas as pl
from jax.experimental.pallas import tpu as pltpu
from jax.sharding import PartitionSpec as P

HDIM = 64
LANES = 128
STATS = 16
F32 = jnp.float32
BF16 = jnp.bfloat16
VMEM_BYTES = 56 << 20
NT = (((1,), (1,)), ((), ()))
NN = (((1,), (0,)), ((), ()))

epsilon = 1e-06
masked_score = -1e30


def dot_as(left, right, dims):
    return lax.dot_general(left, right, dims, preferred_element_type=F32)


def matmul(left, right):
    return dot_as(left, right, NN)


def inner_rows(left, right):
    return dot_as(left, right, (((0,), (0,)), ((), ())))


def inner_cols(left, right):
    return dot_as(left, right, NT)


def layer_norm(values, gain, shift):
    center = values - jnp.mean(values, -1, keepdims=True)
    inverse = lax.rsqrt(jnp.mean(center * center, -1, keepdims=True) + epsilon)
    normed = center * inverse
    return (normed * gain + shift, normed, inverse)


def row_of(ref):
    return ref[...].reshape(1, -1)


def norm_back(grad_out, normed, inverse, gain):
    scaled = grad_out * gain
    grad_in = inverse * (
        scaled
        - jnp.mean(scaled, -1, keepdims=True)
        - normed * jnp.mean(scaled * normed, -1, keepdims=True)
    )
    return (grad_in, jnp.sum(grad_out * normed, 0), jnp.sum(grad_out, 0))


def neighbours():
    dp, z = lax.axis_index("dp"), lax.axis_index("seq")
    other = dp + 1 - 2 * lax.rem(dp, jnp.int32(2))
    pair = z + 1 - 2 * lax.rem(z, jnp.int32(2))
    return (other, z), (dp, pair), (other, lax.rem(z + 2, jnp.int32(4)))


def stays():
    dp, z = lax.axis_index("dp"), lax.axis_index("seq")
    return lax.rem(dp, jnp.int32(2)) == lax.div(z, jnp.int32(2))


def greet(devices):
    barrier = pltpu.get_barrier_semaphore()
    for device in devices:
        pl.semaphore_signal(barrier, inc=1, device_id=device, device_id_type=pl.DeviceIdType.MESH)
    pl.semaphore_wait(barrier, len(devices))


def remote(source, target, sent, landed, device):
    return pltpu.make_async_remote_copy(
        src_ref=source,
        dst_ref=target,
        send_sem=sent,
        recv_sem=landed,
        device_id=device,
        device_id_type=pl.DeviceIdType.MESH,
    )


def move_start(source, target, sent, landed):
    swap = neighbours()[2]

    @pl.when(stays())
    def _():
        pltpu.make_async_copy(source, target, landed).start()

    @pl.when(jnp.logical_not(stays()))
    def _():
        remote(source, target, sent, landed, swap).start()


def move_landed(source, target, sent, landed):
    swap = neighbours()[2]

    @pl.when(stays())
    def _():
        pltpu.make_async_copy(source, target, landed).wait()

    @pl.when(jnp.logical_not(stays()))
    def _():
        remote(source, target, sent, landed, swap).wait_recv()


def move_sent(source, target, sent, landed):
    swap = neighbours()[2]

    @pl.when(jnp.logical_not(stays()))
    def _():
        remote(source, target, sent, landed, swap).wait_send()


def two_heads(values):
    lane = lax.broadcasted_iota(jnp.int32, values.shape, 1)
    zero = jnp.zeros_like(values)
    return jnp.concatenate(
        [jnp.where(lane < HDIM, values, zero), jnp.where(lane < HDIM, zero, values)], 0
    )


def own_columns(values):
    rows = values.shape[0] // 2
    lane = lax.broadcasted_iota(jnp.int32, (rows, LANES), 1)
    return jnp.where(lane < HDIM, values[:rows], values[rows:])


def own_rows(values):
    count = values.shape[1] // 2
    return jnp.transpose(jnp.concatenate([values[:HDIM, :count], values[HDIM:, count:]], 0))


def scaled_down(values):
    return values * jnp.asarray(1.0 / math.sqrt(HDIM), values.dtype)


def attend_kernel(ways, q_ref, k_ref, v_ref, mark_q, mark_k, *refs):
    pair = pl.program_id(0)
    if ways is None:
        out_ref, chance_ref, lse_ref = refs
    else:
        home_ref, out_ref, chance_ref, lse_ref, here_ref, sent, landed = refs
        move = (home_ref, here_ref, sent, landed)

        @pl.when(pair == 0)
        def _():
            greet([neighbours()[2]])
            move_start(*move)

    rows = q_ref.shape[0]
    marks = mark_q[...]
    queries = jnp.concatenate(
        [two_heads(scaled_down(q_ref[...])), jnp.concatenate([marks, marks], 0)], 1
    )
    scores = dot_as(jnp.concatenate([k_ref[...], mark_k[...]], 1), queries, NT)
    highest = jnp.max(scores, 0, keepdims=True)
    powers = jnp.exp(scores - highest)
    total = jnp.sum(powers, 0, keepdims=True)
    chances = (powers * (1.0 / total)).astype(BF16)
    chance_ref[0] = chances[:, :rows]
    chance_ref[1] = chances[:, rows:]
    out_ref[...] = own_rows(dot_as(jnp.transpose(v_ref[...]), chances, NN)).astype(BF16)
    log_total = highest + jnp.log(total)
    lse_ref[pl.ds(2 * pair, 1), :] = log_total[:, :rows]
    lse_ref[pl.ds(2 * pair + 1, 1), :] = log_total[:, rows:]

    if ways is not None:

        @pl.when(pair == pl.num_programs(0) - 1)
        def _():
            move_landed(*move)
            move_sent(*move)


def query_grads(chance_ref, grad, keys, values, deltas, sub=512):
    turned, grads = jnp.transpose(keys), two_heads(grad)
    delta = jnp.concatenate(deltas, 1)
    total = jnp.zeros((LANES, grads.shape[0]), F32)
    for first in range(0, keys.shape[0], sub):
        at = slice(first, first + sub)
        grad_chances = dot_as(values[at], grads, NT)
        chances = jnp.concatenate([chance_ref[0, at, :], chance_ref[1, at, :]], 1)
        scores = (chances.astype(F32) * (grad_chances - delta)).astype(BF16)
        total += dot_as(turned[:, at], scores, NN)
    return scaled_down(own_rows(total)).astype(BF16)


def key_sums(key, value, mark_k, parts):
    rows = key.shape[0]
    keys = jnp.concatenate([two_heads(key), jnp.concatenate([mark_k, mark_k], 0)], 1)
    values = two_heads(value)
    dk = dv = jnp.zeros((2 * rows, LANES), F32)
    for queries, grads, marks, log_totals, deltas in parts:
        scores = dot_as(keys, jnp.concatenate([scaled_down(queries), marks], 1), NT)
        grad_chances = dot_as(values, grads, NT)
        chances, grad_scores = [], []
        for head in range(2):
            at = slice(head * rows, (head + 1) * rows)
            powers = jnp.exp(scores[at] - log_totals[head])
            chances.append(powers.astype(BF16))
            grad_scores.append((powers * (grad_chances[at] - deltas[head])).astype(BF16))
        dv += dot_as(jnp.concatenate(chances, 0), grads, NN)
        dk += dot_as(jnp.concatenate(grad_scores, 0), queries, NN)
    return own_columns(dk), own_columns(dv)


def grad_query_kernel(chance_ref, grad_ref, k_ref, v_ref, delta_ref, dq_ref):
    pair = pl.program_id(0)
    deltas = [delta_ref[pl.ds(2 * pair + head, 1), :] for head in range(2)]
    dq_ref[...] = query_grads(chance_ref, grad_ref[...], k_ref[...], v_ref[...], deltas)


def grad_key_kernel(pieces, k_ref, v_ref, q_ref, *refs):
    g_refs = refs[:pieces]
    lse_refs, delta_refs = refs[pieces : 2 * pieces], refs[2 * pieces : 3 * pieces]
    mark_k, mark_q, dk_ref, dv_ref = refs[3 * pieces :]
    pair = pl.program_id(0)
    rows = g_refs[0].shape[0]
    parts = []
    for i in range(pieces):
        at = pl.ds(i * rows, rows)
        stats = [
            [ref[i][pl.ds(2 * pair + head, 1), :] for head in range(2)]
            for ref in (lse_refs, delta_refs)
        ]
        parts.append((q_ref[at, :], g_refs[i][...], mark_q[at, :], *stats))
    dk, dv = key_sums(k_ref[...], v_ref[...], mark_k[...], parts)
    dk_ref[...], dv_ref[...] = scaled_down(dk).astype(BF16), dv.astype(BF16)


def columns(rows, first):
    return pl.BlockSpec((rows, LANES), lambda t: (0, first + t))


def whole(array):
    return pl.BlockSpec(array.shape, lambda t: (0,) * array.ndim)


def kernel_call(kernel, name, grid, in_specs, out_specs, out_shape, scratch, flops, moved, **params):
    return pl.pallas_call(
        kernel,
        grid=grid,
        in_specs=in_specs,
        out_specs=out_specs,
        out_shape=out_shape,
        scratch_shapes=scratch,
        compiler_params=pltpu.CompilerParams(vmem_limit_bytes=VMEM_BYTES, **params),
        cost_estimate=pl.CostEstimate(flops=flops, bytes_accessed=moved, transcendentals=0),
        name=name,
    )


def attend(plan, own, projected, mark_q, mark_k, cotangent):
    rows, width = cotangent.shape
    length, pairs = projected.shape[0], width // LANES
    stats = jax.ShapeDtypeStruct((STATS, rows), F32)
    anywhere = pl.BlockSpec(memory_space=pl.ANY)
    ways = plan.ways
    moving = [] if ways is None else [cotangent]
    params = {} if ways is None else {"collective_id": 1, "has_side_effects": True}
    results = kernel_call(
        functools.partial(attend_kernel, ways),
        "attend",
        (pairs,),
        [
            columns(rows, 0),
            columns(length, pairs),
            columns(length, 2 * pairs),
            pl.BlockSpec((rows, LANES), lambda t: (0, 0)),
            whole(mark_k),
        ]
        + [anywhere] * len(moving),
        [
            columns(rows, 0),
            pl.BlockSpec((2, length, rows), lambda t: (t, 0, 0)),
            whole(stats),
        ]
        + [anywhere] * len(moving),
        [
            jax.ShapeDtypeStruct((rows, width), BF16),
            jax.ShapeDtypeStruct((2 * pairs, length, rows), BF16),
            stats,
        ]
        + [jax.ShapeDtypeStruct(array.shape, array.dtype) for array in moving],
        [pltpu.SemaphoreType.DMA] * (2 * len(moving)),
        24 * rows * length * width,
        4 * pairs * rows * length,
        **params,
    )(own, projected, projected, mark_q, mark_k, *moving)
    return tuple(results) if moving else tuple(results) + (cotangent,)


def grad_query(chances, grad, projected, deltas):
    rows, width = grad.shape
    length, pairs = projected.shape[0], width // LANES
    return kernel_call(
        grad_query_kernel,
        "grad_query",
        (pairs,),
        [
            pl.BlockSpec((2, length, rows), lambda t: (t, 0, 0)),
            columns(rows, 0),
            columns(length, pairs),
            columns(length, 2 * pairs),
            whole(deltas),
        ],
        columns(rows, 0),
        jax.ShapeDtypeStruct((rows, width), BF16),
        [],
        16 * rows * length * width,
        4 * pairs * rows * length,
    )(chances, grad, projected, projected, deltas)


def grad_key_value(own, projected, grads, log_totals, deltas, mark_k, mark_q):
    rows, width = grads[0].shape
    pieces, pairs = len(grads), width // LANES
    length = rows * pieces
    result = jax.ShapeDtypeStruct((rows, width), BF16)
    return kernel_call(
        functools.partial(grad_key_kernel, pieces),
        "grad_key_value",
        (pairs,),
        [columns(rows, pairs), columns(rows, 2 * pairs), columns(length, 0)]
        + [columns(rows, 0)] * pieces
        + [whole(log_totals[0])] * (2 * pieces)
        + [whole(mark_k), whole(mark_q)],
        [columns(rows, 0)] * 2,
        [result] * 2,
        [],
        32 * rows * length * width,
        8 * length * width,
    )(own, own, projected, *grads, *log_totals, *deltas, mark_k, mark_q)


class Chunk:
    stages = ("start", "near", "far", "along", "meet", "spread", "finish")

    def __init__(self, source, rows, columns, y_first, when, held=False, dtype=BF16):
        self.source, self.rows, self.columns = source, rows, columns
        self.shape = (rows[1], columns[1])
        self.blocks = ((2, 3), 1) if y_first else ((1, 3), 2)
        self.y_first, self.when, self.held, self.dtype = y_first, when, held, dtype

    def scratch(self):
        rows, columns = self.shape
        lead = [(4,), (2,), (), (), ()] if self.held else [(4,), (2,), (), (), (), (4,)]
        return [pltpu.VMEM(first + (rows, columns), self.dtype) for first in lead] + [
            pltpu.SemaphoreType.DMA((7,)),
            pltpu.SemaphoreType.DMA((8,)),
        ]

    def bind(self, source, out, scratch, devices):
        at = (pl.ds(*self.rows), pl.ds(*self.columns))
        kept = source.at[(pl.ds(0, 4),) + at]
        self.out = out.at[at]
        core, first, second, z1, z2, *rest = scratch
        *rest, sent, landed = rest
        self.keep = kept if self.held else rest[0]
        self.core, self.first, self.second, self.z1, self.z2 = core, first, second, z1, z2
        near, far = (devices["y"], devices["x"]) if self.y_first else (devices["x"], devices["y"])
        sends, last = self.blocks
        self.load = pltpu.make_async_copy(kept, self.keep, landed.at[7])
        self.to_core = remote(
            source.at[(pl.ds(4, 4),) + at], core, sent.at[0], landed.at[0], devices["core"]
        )
        self.to_near = [
            remote(self.keep.at[b], first.at[i], sent.at[1 + i], landed.at[1 + i], near)
            for i, b in enumerate(sends)
        ]
        self.to_far = remote(self.keep.at[last], second, sent.at[3], landed.at[3], far)
        self.bind_along(sent, landed, devices)

    def bind_along(self, sent, landed, devices):
        pair, z1 = devices["pair"], self.z1
        self.inward = remote(self.keep.at[0], z1, sent.at[4], landed.at[4], pair)
        self.middle = remote(self.keep.at[0], self.z2, sent.at[5], landed.at[5], devices["mirror"])
        self.outward = remote(z1, self.out, sent.at[6], landed.at[6], pair)
        self.store = pltpu.make_async_copy(z1, self.out, landed.at[6])

    def add(self, target, one, other):
        target[...] = one[...] + other[...]

    def start(self):
        self.to_core.start()
        if not self.held:
            self.load.start()

    def near(self):
        if not self.held:
            self.load.wait()
        self.to_core.wait_recv()
        sends = self.blocks[0]
        for block in sends:
            self.add(self.keep.at[block], self.keep.at[block], self.core.at[block])
        for copy in self.to_near:
            copy.start()
        for block in range(4):
            if block not in sends:
                self.add(self.keep.at[block], self.keep.at[block], self.core.at[block])

    def join(self, block):
        stay = [b for b in range(4) if b not in self.blocks[0]]
        i = stay.index(block)
        self.to_near[i].wait_recv()
        self.add(self.keep.at[block], self.keep.at[block], self.first.at[i])

    def far(self):
        self.join(self.blocks[1])
        self.to_far.start()
        self.join(0)

    def along(self):
        self.to_far.wait_recv()
        self.add(self.keep.at[0], self.keep.at[0], self.second)

        @pl.when(jnp.logical_not(inner()))
        def _():
            self.inward.start()

    def meet(self):
        @pl.when(inner())
        def _():
            self.inward.wait_recv()
            self.add(self.keep.at[0], self.keep.at[0], self.z1)
            self.middle.start()

    def spread(self):
        @pl.when(inner())
        def _():
            self.middle.wait_recv()
            self.add(self.z1, self.keep.at[0], self.z2)
            self.outward.start()
            self.store.start()

    def finish(self):
        @pl.when(jnp.logical_not(inner()))
        def _():
            self.outward.wait_recv()
            self.inward.wait_send()

        @pl.when(inner())
        def _():
            self.store.wait()
            self.middle.wait_send()
            self.outward.wait_send()

        self.settle()

    def settle(self):
        self.to_core.wait_send()
        for copy in self.to_near:
            copy.wait_send()
        self.to_far.wait_send()


class DirectChunk:
    stages = ("start", "near", "far")

    def __init__(self, source, rows, columns, when, dtype=BF16):
        self.source, self.rows, self.columns = source, rows, columns
        self.shape = (rows[1], columns[1])
        self.when, self.dtype = when, dtype

    def scratch(self):
        rows, columns = self.shape
        return [pltpu.VMEM(first + (rows, columns), self.dtype) for first in ((8,), (3,), ())] + [
            pltpu.SemaphoreType.DMA((10,)),
            pltpu.SemaphoreType.DMA((11,)),
        ]

    def bind(self, source, out, scratch, devices):
        at = (pl.ds(*self.rows), pl.ds(*self.columns))
        self.mine = source.at[(0,) + at]
        self.landing, self.others, self.total, sent, landed = scratch
        self.around = [
            remote(
                source.at[(place,) + at],
                self.landing.at[place],
                sent.at[place - 1],
                landed.at[place - 1],
                devices["block"][place],
            )
            for place in range(1, 8)
        ]
        self.along_z = [
            remote(self.total, self.others.at[i], sent.at[7 + i], landed.at[7 + i], devices[name])
            for i, name in enumerate(("pair", "mirror", "opposite"))
        ]
        self.store = pltpu.make_async_copy(self.landing.at[0], out.at[at], landed.at[10])

    def start(self):
        for copy in self.around:
            copy.start()

    def near(self):
        total = self.mine[...].astype(F32)
        for i, copy in enumerate(self.around):
            copy.wait_recv()
            total = total + self.landing[1 + i].astype(F32)
        self.total[...] = total.astype(self.dtype)
        for copy in self.along_z:
            copy.start()

    def far(self):
        for copy in self.along_z:
            copy.wait_recv()
        total = self.total[...].astype(F32) + self.others[0].astype(F32)
        total = total + (self.others[1].astype(F32) + self.others[2].astype(F32))
        self.landing[0] = total.astype(self.dtype)
        self.store.start()

    def finish(self):
        self.store.wait()
        for copy in self.around + self.along_z:
            copy.wait_send()


def inner():
    z = lax.axis_index("seq")
    return jnp.logical_and(z > 0, z < 3)


def ring_devices():
    dp, z = lax.axis_index("dp"), lax.axis_index("seq")
    core, pair, swap = neighbours()

    def flip(index, bit):
        size = 1 << bit
        return index + size - 2 * size * lax.rem(lax.div(index, jnp.int32(size)), jnp.int32(2))

    blocks = []
    for place in range(8):
        index = dp
        for bit, flips in enumerate((place // 4, place % 2, place // 2 % 2)):
            if flips:
                index = flip(index, bit)
        blocks.append((index, z))
    return {
        "core": core,
        "pair": pair,
        "swap": swap,
        "x": blocks[1],
        "y": blocks[2],
        "mirror": (dp, 3 - z),
        "opposite": (dp, lax.rem(z + 2, jnp.int32(4))),
        "block": blocks,
    }


def relative_place(*bits):
    dp = lax.axis_index("dp")
    turned = [
        lax.rem(lax.div(dp, jnp.int32(1 << k)) + bit, jnp.int32(2)) for k, bit in enumerate(bits)
    ]
    return turned[0] * 4 + turned[1] + turned[2] * 2


def bits_of(block):
    return [(block >> k) % 2 for k in range(3)]


def store_blocks(target, columns, total):
    part = total.shape[0] // 8
    for block in range(8):
        target[relative_place(*bits_of(block)), :, columns] = total[block * part : (block + 1) * part].astype(BF16)


VECTORS = 16


def backward_chunks(shapes, width, pairs):
    down, up, _ = shapes
    part, quarter, share = width // 8, down[1] // 4, up[2] // 4
    end = 4 * pairs
    tile = LANES

    def when(*steps):
        return tuple(at if isinstance(at, tuple) else (at, 0) for at in steps)

    rows, whole_width = (0, part), (0, width)
    downs = [((i * quarter, quarter), whole_width, i % 2 == 0) for i in range(4)]
    ups = [(rows, (i * share, share), i % 2 == 0) for i in range(4)]
    return [
        Chunk("down", *downs[0], when(0, 1, 4, 8, 12, 15)),
        Chunk("down", *downs[1], when(0, 1, 4, 8, 12, 15)),
        Chunk("down", *downs[2], when(1, 3, 6, 10, 13, 16)),
        Chunk("down", *downs[3], when(1, 3, 6, 10, 13, 16)),
        Chunk("up", *ups[0], when(3, 5, 8, 12, 15, 18)),
        Chunk("up", *ups[1], when(3, 5, 8, 12, 15, 18)),
        Chunk("up", *ups[2], when(5, 7, 11, 14, 17, 20)),
        Chunk("up", *ups[3], when(5, 7, 11, 14, 17, 20)),
        Chunk("out", rows, whole_width, True, when(7, 10, 13, 16, 19, 21)),
        Chunk("pair", rows, (0 * tile, 4 * tile), False, when(14, 15, 17, 19, 21, 23), True),
        Chunk("pair", rows, (4 * tile, 4 * tile), True, when(16, 17, 19, 21, 23, (end, 0)), True),
        Chunk("pair", rows, (8 * tile, 4 * tile), False, when(18, 19, 21, 23, (end, 0), (end, 1)), True),
        Chunk("query", rows, (0, 2 * tile), True, when(20, 21, 23, (end, 0), (end, 1), (end, 2)), True),
        Chunk("query", rows, (2 * tile, 2 * tile), False, when(22, 23, (end, 0), (end, 1), (end, 2), (end, 3)), True),
        DirectChunk("query", rows, (4 * tile, tile), when(23, (end, 0), (end, 2))),
        DirectChunk("query", rows, (5 * tile, tile), when((end, 0), (end, 1), (end, 3))),
        DirectChunk("vector", (0, VECTORS), (0, LANES), when((end, 0), (end, 1), (end, 3)), F32),
    ]


def backward_kernel(
    shapes,
    pairs,
    chance_ref,
    grad_ref,
    attended_ref,
    k_ref,
    v_ref,
    q_ref,
    mark_k,
    mark_q,
    lse_ref,
    gain_ref,
    sums_ref,
    sum_up_ref,
    w_hbm,
    hidden_hbm,
    here_hbm,
    middle_hbm,
    grad_down,
    grad_up,
    grad_out,
    block_ref,
    home_ref,
    tokens_ref,
    down_ref,
    up_ref,
    out_ref,
    query_ref,
    pair_ref,
    vector_ref,
    grads,
    stats,
    own_stats,
    turned,
    dq,
    grad_hidden,
    query_grad,
    pair_grad,
    vector,
    late,
    tokens,
    partial,
    weights,
    hidden_ref,
    here_ref,
    middle_ref,
    sent,
    landed,
    loaded,
    *scratch,
):
    step = pl.program_id(0)
    rows, width = grad_ref.shape
    held = ((hidden_hbm, hidden_ref), (w_hbm, weights), (here_hbm, here_ref), (middle_hbm, middle_ref))
    loads = [
        pltpu.make_async_copy(source, target, loaded.at[i])
        for i, (source, target) in enumerate(held)
    ]
    half = rows // 2
    steps = 4 * pairs
    devices = ring_devices()
    chunks = backward_chunks(shapes, width, pairs)
    sources = {
        "down": (grad_down, down_ref),
        "up": (grad_up, up_ref),
        "out": (grad_out, out_ref),
        "query": (query_grad, query_ref),
        "pair": (pair_grad, pair_ref),
        "vector": (vector, vector_ref),
    }
    scratch = list(scratch)
    for chunk in chunks:
        count = len(chunk.scratch())
        chunk.bind(*sources[chunk.source], scratch[:count], devices)
        del scratch[:count]
    block_move = (block_ref, home_ref, sent.at[12], landed.at[12])

    def token_move(part):
        at = pl.ds(part * half, half)
        return (tokens.at[at], tokens_ref.at[at], sent.at[13 + part], landed.at[13 + part])

    def grad_copy(i, part, source, device):
        at = pl.ds(part * half, half)
        n = 2 * i + part
        return remote(source.at[at], grads.at[i - 1, at], sent.at[n], landed.at[n], device)

    def to_core(part):
        return grad_copy(1, part, grad_ref, devices["core"])

    def to_pair(part):
        return grad_copy(2, part, grad_ref, devices["pair"])

    def to_corner(part):
        return grad_copy(3, part, grads.at[1], devices["core"])

    def stat_copy(i, source, device):
        return remote(source, stats.at[i], sent.at[8 + i], landed.at[8 + i], device)

    stat_core = stat_copy(1, own_stats, devices["core"])
    stat_pair = stat_copy(2, own_stats, devices["pair"])
    stat_corner = stat_copy(3, stats.at[2], devices["core"])

    def begin():
        greet(devices["block"][1:] + [devices[name] for name in ("pair", "swap", "mirror", "opposite")])
        for part in range(2):
            to_pair(part).start()
        for part in range(2):
            to_core(part).start()
        for load in loads:
            load.start()

    def begin_stats():
        product = grad_ref[...].astype(F32) * attended_ref[...].astype(F32)
        high = product.astype(BF16)
        low = (product - high.astype(F32)).astype(BF16)
        head = lax.broadcasted_iota(jnp.int32, (STATS, width), 0)
        column = lax.broadcasted_iota(jnp.int32, (STATS, width), 1)
        mine = jnp.where(
            jnp.logical_and(column >= head * HDIM, column < (head + 1) * HDIM), 1.0, 0.0
        ).astype(BF16)
        own_stats[0:STATS, :] = lse_ref[...]
        own_stats[STATS:, :] = dot_as(mine, high, NT) + dot_as(mine, low, NT)
        stats[0] = own_stats[...]
        stat_pair.start()
        stat_core.start()
        late[...] = jnp.zeros_like(late)
        grad_hidden[...] = jnp.zeros_like(grad_hidden)
        stat_core.wait_recv()
        for part in range(2):
            to_core(part).wait_recv()

    def loaded_all():
        for load in loads:
            load.wait()
        turned[...] = jnp.transpose(hidden_ref[...])

    def corner_stats():
        stat_pair.wait_recv()
        stat_corner.start()

    def corner(part):
        def run():
            to_pair(part).wait_recv()
            to_corner(part).start()

        return run

    def far_grads():
        stat_corner.wait_recv()
        for part in range(2):
            to_corner(part).wait_recv()

    def first_norm(part):
        def run():
            at = pl.ds(part * half, half)
            _, unit, root = layer_norm(here_ref[at, :].astype(F32), 0.0, 0.0)
            grad = grad_hidden[at, :]
            scaled = grad * row_of(gain_ref)
            grad_in = root * (
                scaled
                - jnp.mean(scaled, -1, keepdims=True)
                - unit * jnp.mean(scaled * unit, -1, keepdims=True)
            )
            tokens[at, :] = (middle_ref[at, :] + grad_in).astype(BF16)
            move_start(*token_move(part))
            late[2:3, :] += jnp.sum(grad * unit, 0, keepdims=True)
            late[3:4, :] += jnp.sum(grad, 0, keepdims=True)

        return run

    def early_vectors():
        share = width // 8
        vector[...] = jnp.zeros_like(vector)
        for block in range(8):
            place = relative_place(*bits_of(block))
            vector[place, 0:4, 0:share] = sums_ref[0:4, block * share : (block + 1) * share]
            for i in range(4):
                first = (block * 4 + i) * share
                vector[place, 8 + i : 9 + i, 0:share] = sum_up_ref[0:1, first : first + share]

    def late_vectors():
        share = width // 8
        for block in range(8):
            vector[relative_place(*bits_of(block)), 4:8, 0:share] = late[
                0:4, block * share : (block + 1) * share
            ]

    def finish_moves():
        for move in (block_move, token_move(0), token_move(1)):
            move_landed(*move)
            move_sent(*move)
        for copy in (stat_core, stat_pair, stat_corner):
            copy.wait_send()
        for part in range(2):
            to_core(part).wait_send()
            to_pair(part).wait_send()
            to_corner(part).wait_send()

    events = [
        ((0, -2), begin),
        ((0, -1), begin_stats),
        ((1, 1), early_vectors),
        ((2, -1), corner_stats),
        ((8, -1), corner(0)),
        ((5, 1), loaded_all),
        ((4, 3), lambda: move_start(*block_move)),
        ((11, -1), corner(1)),
        ((2 * pairs, 1), far_grads),
        ((3 * pairs, -1), first_norm(0)),
        ((steps, -2), first_norm(1)),
        ((steps, -1), late_vectors),
        ((steps, 99), finish_moves),
    ]
    for order in (2, 1, 0, 3, 4, 5):
        for chunk in chunks:
            if order < len(chunk.when):
                events.append((chunk.when[order], getattr(chunk, chunk.stages[order])))
    events += [((steps, 98), chunk.finish) for chunk in chunks]
    events.sort(key=lambda event: event[0])

    def run(at):
        for (when, _), event in events:
            if when == at:
                event()

    for at in range(steps):
        if any(when == at for (when, _), _ in events):

            @pl.when(step == at)
            def _():
                run(at)

    pair = lax.rem(step, jnp.int32(pairs))
    tile = pl.ds(pl.multiple_of(pair * LANES, LANES), LANES)
    double = pl.ds(pl.multiple_of(pair * (2 * LANES), 2 * LANES), 2 * LANES)

    def weight(part):
        return weights[:, pl.ds(pl.multiple_of(part * width + pair * LANES, LANES), LANES)]

    def keys_of(pieces):
        parts = []
        for i, first in [(i, first) for i in pieces for first in (0, half)]:
            span, at = pl.ds(i * rows + first, half), pl.ds(first, half)
            rows_of = [
                [stats[i, pl.ds(start + 2 * pair + head, 1), at] for head in range(2)]
                for start in (0, STATS)
            ]
            piece = grad_ref if i == 0 else grads.at[i - 1]
            parts.append((q_ref[span, :], piece[at, tile], mark_q[span, :], *rows_of))
        return key_sums(k_ref[0:rows, :], v_ref[0:rows, :], mark_k[...], parts)

    @pl.when(step < pairs)
    def _():
        partial[pair, 0], partial[pair, 1] = keys_of((0, 1))

    @pl.when(jnp.logical_and(step >= 2 * pairs, step < 3 * pairs))
    def _():
        dk, dv = keys_of((2, 3))
        dk = scaled_down(dk + partial[pair, 0]).astype(BF16)
        dv = dv + partial[pair, 1]
        late[1:2, tile] = jnp.sum(dv.astype(BF16).astype(F32), 0, keepdims=True)
        both = jnp.concatenate([dk, dv.astype(BF16)], 1)
        store_blocks(pair_grad, double, dot_as(turned[...], both, NN))
        grad_hidden[...] += dot_as(both, jnp.concatenate([weight(1), weight(2)], 1), NT)

    @pl.when(lax.rem(lax.div(step, jnp.int32(pairs)), jnp.int32(2)) == 1)
    def _():
        part = lax.div(step, jnp.int32(2 * pairs))
        at = pl.ds(pl.multiple_of(part * half, half), half)
        deltas = [own_stats[pl.ds(STATS + 2 * pair + head, 1), at] for head in range(2)]
        found = query_grads(chance_ref, grad_ref[at, tile], k_ref[...], v_ref[...], deltas)
        dq[at, tile] = found
        late[0:1, tile] += jnp.sum(found.astype(F32), 0, keepdims=True)
        grad_hidden[at, :] += dot_as(found, weight(0), NT)

        @pl.when(part == 1)
        def _():
            store_blocks(query_grad, tile, dot_as(turned[...], dq[:, tile], NN))

    @pl.when(step == steps - 1)
    def _():
        run(steps)


def once(array):
    return pl.BlockSpec(array.shape, lambda *t: (0,) * array.ndim, pipeline_mode=pl.Buffered(1))


def backward(
    chances,
    grad,
    attended,
    projected,
    mark_k,
    mark_q,
    log_totals,
    weight,
    hidden,
    here,
    grad_middle,
    gain,
    sums,
    sum_up,
    totals,
    block_out,
):
    rows, width = grad.shape
    length, pairs = projected.shape[0], width // LANES
    shapes = [total.shape for total in totals]
    part = width // 8
    anywhere = pl.BlockSpec(memory_space=pl.ANY)
    result = jax.ShapeDtypeStruct((rows, width), BF16)
    outs = [result, result] + [
        jax.ShapeDtypeStruct(shape, BF16)
        for shape in [shape[1:] for shape in shapes] + [(part, width), (part, 2 * width)]
    ]
    outs.append(jax.ShapeDtypeStruct((VECTORS, LANES), F32))

    def tile(first):
        return pl.BlockSpec((length, LANES), lambda t: (0, first + lax.rem(t, pairs)))

    def chance_at(t):
        phase = lax.div(t, pairs)
        return jnp.where(lax.rem(phase, 2) == 1, lax.rem(t, pairs), 0), 0, lax.div(phase, 2)

    def query_at(t):
        return 0, jnp.where(lax.rem(lax.div(t, pairs), 2) == 0, lax.rem(t, pairs), pairs - 1)

    fixed = [mark_k, mark_q, log_totals, gain, sums, sum_up]
    held = [weight, hidden, here, grad_middle]
    chunks = backward_chunks(shapes, width, pairs)
    stats = (2 * STATS, rows)
    return kernel_call(
        functools.partial(backward_kernel, shapes, pairs),
        "backward",
        (4 * pairs,),
        [
            pl.BlockSpec((2, length, rows // 2), chance_at),
            once(grad),
            once(attended),
            tile(pairs),
            tile(2 * pairs),
            pl.BlockSpec((length, LANES), query_at),
        ]
        + [pl.BlockSpec((rows, LANES), lambda t: (0, 0), pipeline_mode=pl.Buffered(1))]
        + [once(array) for array in fixed[1:]]
        + [anywhere] * (len(held) + len(totals) + 1),
        [anywhere] * len(outs),
        outs,
        [
            pltpu.VMEM((3, rows, width), BF16),
            pltpu.VMEM((4,) + stats, F32),
            pltpu.VMEM(stats, F32),
            pltpu.VMEM((width, rows), BF16),
            pltpu.VMEM((rows, width), BF16),
            pltpu.VMEM((rows, width), F32),
            pltpu.VMEM((8, part, width), BF16),
            pltpu.VMEM((8, part, 2 * width), BF16),
            pltpu.VMEM((8, VECTORS, LANES), F32),
            pltpu.VMEM((8, width), F32),
            pltpu.VMEM((rows, width), BF16),
            pltpu.VMEM((pairs, 2, rows, LANES), F32),
        ]
        + [pltpu.VMEM(array.shape, array.dtype) for array in held]
        + [
            pltpu.SemaphoreType.DMA((15,)),
            pltpu.SemaphoreType.DMA((15,)),
            pltpu.SemaphoreType.DMA((len(held),)),
        ]
        + [entry for chunk in chunks for entry in chunk.scratch()],
        48 * rows * length * width,
        4 * pairs * rows * length,
        collective_id=2,
        has_side_effects=True,
    )(chances, grad, attended, projected, projected, projected, *fixed, *held, *totals, block_out)


def results_kernel(block, tokens, down, up, out, query, pair, vector, *outs):
    (
        block_ref,
        tokens_ref,
        ln1_gain,
        ln1_shift,
        w_qkv,
        bias_query,
        bias_value,
        w_out,
        bias_out,
        ln2_gain,
        ln2_shift,
        w_up,
        bias_up,
        w_down,
        bias_down,
    ) = outs
    block_ref[...] = block[...]
    tokens_ref[...] = tokens[...]
    width = query.shape[1]
    w_qkv[:, 0:width] = query[...].astype(F32)
    for i in range(width // LANES):
        for j in range(2):
            first = (2 * i + j) * LANES
            to = (1 + j) * width + i * LANES
            w_qkv[:, to : to + LANES] = pair[:, first : first + LANES].astype(F32)
    w_up[...] = up[...].astype(F32)
    w_down[...] = down[...].astype(F32)
    w_out[...] = out[...].astype(F32)
    share = width // 8
    order = (ln2_gain, ln2_shift, bias_out, bias_down, bias_query, bias_value, ln1_gain, ln1_shift)
    for i, ref in enumerate(order):
        ref[...] = vector[i, 0:share]
    bias_up[...] = jnp.concatenate([vector[8 + i : 9 + i, 0:share] for i in range(4)], 1)[0]


def results(block, tokens, down, up, out, query, pair, vector):
    part, width = query.shape
    vmem = pl.BlockSpec(memory_space=pltpu.VMEM)

    def line(size=part):
        return jax.ShapeDtypeStruct((size,), F32)

    def like(array):
        return jax.ShapeDtypeStruct(array.shape, F32)

    return pl.pallas_call(
        results_kernel,
        in_specs=[vmem] * 8,
        out_specs=[vmem] * 15,
        out_shape=[
            jax.ShapeDtypeStruct(block.shape, BF16),
            jax.ShapeDtypeStruct(tokens.shape, BF16),
            line(),
            line(),
            jax.ShapeDtypeStruct((part, 3 * width), F32),
            line(),
            line(),
            like(out),
            line(),
            line(),
            line(),
            like(up),
            line(4 * part),
            like(down),
            line(),
        ],
        compiler_params=pltpu.CompilerParams(vmem_limit_bytes=VMEM_BYTES),
        name="results",
    )(block, tokens, down, up, out, query, pair, vector)


def gelu_parts(pre_act):
    inside = 0.5 * (1.0 + lax.erf(pre_act * math.sqrt(0.5)))
    slope = inside + pre_act * jnp.exp(-0.5 * pre_act * pre_act) * (1.0 / math.sqrt(2.0 * math.pi))
    return pre_act * inside, slope


def relative(block, me):
    turned = block ^ me
    return (turned % 2) * 4 + turned // 2


def feed_kernel(
    sub,
    index_ref,
    here_ref,
    attended_ref,
    grad_ref,
    w_out_ref,
    bias_out_ref,
    gain_ref,
    shift_ref,
    w_up_ref,
    bias_up_ref,
    w_down_ref,
    bias_down_ref,
    block_ref,
    grad_attended_ref,
    grad_middle_ref,
    down_ref,
    up_ref,
    out_ref,
    sum_up_ref,
    sums_ref,
    middle,
    normed,
    inverse,
    hidden,
    turned,
    total,
    grad_hidden,
    activated,
    grad_upper,
):
    step, last = pl.program_id(0), pl.num_programs(0) - 1
    me = index_ref[0]
    rows, width = here_ref.shape
    blocks = rows // sub

    def span(i):
        return pl.ds(pl.multiple_of(i * sub, sub), sub)

    @pl.when(step == 0)
    def _():
        def norm(i, carry):
            at = span(i)
            values = (
                here_ref[at, :].astype(F32)
                + dot_as(attended_ref[at, :], w_out_ref[...], NN)
                + row_of(bias_out_ref)
            )
            out, unit, root = layer_norm(values, row_of(gain_ref), row_of(shift_ref))
            middle[at, :] = values
            normed[at, :] = unit
            inverse[at, :] = jnp.broadcast_to(root, (sub, LANES))
            hidden[at, :] = out.astype(BF16)
            total[at, :] = values + row_of(bias_down_ref)
            grad_hidden[at, :] = jnp.zeros((sub, width), F32)
            return carry

        lax.fori_loop(0, blocks, norm, 0)
        turned[...] = jnp.transpose(hidden[...])

    def tile(i, carry):
        at = span(i)
        upper = dot_as(hidden[at, :], w_up_ref[...], NN) + bias_up_ref[...]
        grad_activated = dot_as(grad_ref[at, :], w_down_ref[...], NT)
        active, slope = gelu_parts(upper)
        active = active.astype(BF16)
        grad_in = (grad_activated * slope).astype(BF16)
        activated[at, :] = active
        grad_upper[at, :] = grad_in
        total[at, :] += dot_as(active, w_down_ref[...], NN)
        grad_hidden[at, :] += dot_as(grad_in, w_up_ref[...], NT)
        return carry + jnp.sum(grad_in.astype(F32), 0, keepdims=True)

    sum_up_ref[...] = lax.fori_loop(0, blocks, tile, jnp.zeros(sum_up_ref.shape, F32))

    grad_up = dot_as(turned[...], grad_upper[...], NN)
    part = width // 8
    for block in range(8):
        up_ref[relative(block, me)] = grad_up[block * part : (block + 1) * part].astype(BF16)
    grad_down = inner_rows(activated[...], grad_ref[...])
    part = down_ref.shape[2]
    for i in range(2):
        down_ref[(i ^ me) % 2, 0] = grad_down[i * part : (i + 1) * part].astype(BF16)

    @pl.when(step == last)
    def _():
        def norm(i, carry):
            at = span(i)
            block_ref[at, :] = total[at, :].astype(BF16)
            grad, unit = grad_hidden[at, :], normed[at, :]
            scaled = grad * row_of(gain_ref)
            grad_in = inverse[at, 0:1] * (
                scaled
                - jnp.mean(scaled, -1, keepdims=True)
                - unit * jnp.mean(scaled * unit, -1, keepdims=True)
            )
            before = grad_ref[at, :].astype(F32)
            grad_in = before + grad_in
            branch = grad_in.astype(BF16)
            grad_middle_ref[at, :] = grad_in
            hidden[at, :] = branch
            grad_attended_ref[at, :] = dot_as(branch, w_out_ref[...], NT).astype(BF16)
            sums = [grad * unit, grad, branch.astype(F32), before]
            return tuple(
                old + jnp.sum(value, 0, keepdims=True) for old, value in zip(carry, sums)
            )

        zero = jnp.zeros((1, width), F32)
        sums = lax.fori_loop(0, blocks, norm, (zero,) * 4)
        sums_ref[...] = jnp.concatenate(list(sums) + [zero] * 4, 0)
        grad_out = inner_rows(attended_ref[...], hidden[...])
        part = width // 8
        for block in range(8):
            out_ref[relative(block, me)] = grad_out[block * part : (block + 1) * part].astype(BF16)


def feed(
    here, attended, grad, w_out, bias_out, gain, shift, w_up, bias_up, w_down, bias_down, me, sub=256
):
    rows, width = here.shape
    wide = w_up.shape[1]
    steps = 4
    tile = wide // steps
    part = width // 8

    def once(*shape):
        return pl.BlockSpec(shape, lambda f, at: (0,) * len(shape), pipeline_mode=pl.Buffered(1))

    act = once(rows, width)
    line = once(width)
    outs = [
        jax.ShapeDtypeStruct((rows, width), BF16),
        jax.ShapeDtypeStruct((rows, width), BF16),
        jax.ShapeDtypeStruct((rows, width), F32),
        jax.ShapeDtypeStruct((2, 4, wide // 8, width), BF16),
        jax.ShapeDtypeStruct((8, part, wide), BF16),
        jax.ShapeDtypeStruct((8, part, width), BF16),
        jax.ShapeDtypeStruct((1, wide), F32),
        jax.ShapeDtypeStruct((8, width), F32),
    ]
    return pl.pallas_call(
        functools.partial(feed_kernel, sub),
        grid_spec=pltpu.PrefetchScalarGridSpec(
            num_scalar_prefetch=1,
            grid=(steps,),
            in_specs=[
                act,
                act,
                act,
                once(width, width),
                line,
                line,
                line,
                pl.BlockSpec((width, tile), lambda f, at: (0, f)),
                pl.BlockSpec((1, tile), lambda f, at: (0, f)),
                pl.BlockSpec((tile, width), lambda f, at: (f, 0)),
                line,
            ],
            out_specs=[
                act,
                act,
                act,
                pl.BlockSpec((2, 1, wide // 8, width), lambda f, at: (0, f ^ (at[0] // 2), 0, 0)),
                pl.BlockSpec((8, part, tile), lambda f, at: (0, 0, f)),
                once(8, part, width),
                pl.BlockSpec((1, tile), lambda f, at: (0, f)),
                once(8, width),
            ],
            scratch_shapes=[
                pltpu.VMEM((rows, width), F32),
                pltpu.VMEM((rows, width), F32),
                pltpu.VMEM((rows, LANES), F32),
                pltpu.VMEM((rows, width), BF16),
                pltpu.VMEM((width, rows), BF16),
                pltpu.VMEM((rows, width), F32),
                pltpu.VMEM((rows, width), F32),
                pltpu.VMEM((rows, tile), BF16),
                pltpu.VMEM((rows, tile), BF16),
            ],
        ),
        out_shape=outs,
        compiler_params=pltpu.CompilerParams(vmem_limit_bytes=VMEM_BYTES),
        cost_estimate=pl.CostEstimate(
            flops=12 * rows * width * wide, bytes_accessed=8 * width * wide, transcendentals=0
        ),
        name="feed",
    )(
        me,
        here,
        attended,
        grad,
        w_out,
        bias_out,
        gain,
        shift,
        w_up,
        bias_up.reshape(1, -1),
        w_down,
        bias_down,
    )


def start_kernel(
    tokens_ref,
    lengths_ref,
    gain_ref,
    shift_ref,
    w_ref,
    bias_ref,
    projected_ref,
    hidden_ref,
    here_ref,
    found_ref,
    rows,
    staged,
    sent,
    landed,
    out_sem,
):
    core, across, swap = neighbours()
    parts = sent.shape[1]
    height = tokens_ref.shape[0]
    part = height // parts
    greet([core, across, swap])

    def span(i):
        return pl.ds(pl.multiple_of(i * part, part), part)

    def moved(i):
        return (tokens_ref.at[span(i)], rows.at[0, span(i)], sent.at[0, i], landed.at[0, i])

    def lengths():
        return remote(lengths_ref, found_ref, sent.at[4, 0], landed.at[4, 0], core)

    def forward(i, origin, piece, device):
        return remote(
            rows.at[origin, span(i)],
            rows.at[piece, span(i)],
            sent.at[piece, i],
            landed.at[piece, i],
            device,
        )

    def out_span(piece, i):
        return pl.ds(pl.multiple_of(piece * height + i * part, part), part)

    def to_hbm(piece, i):
        at = out_span(piece, i)
        return pltpu.make_async_copy(staged.at[at], projected_ref.at[at], out_sem.at[piece, i])

    def project(piece, i):
        values = rows[piece, span(i), :].astype(F32)
        hidden = layer_norm(values, row_of(gain_ref), row_of(shift_ref))[0].astype(BF16)
        staged[out_span(piece, i), :] = (
            dot_as(hidden, w_ref[...], NN) + row_of(bias_ref)
        ).astype(BF16)
        to_hbm(piece, i).start()
        return hidden

    for i in range(parts):
        move_start(*moved(i))
    lengths().start()

    def first(i, carry):
        move_landed(*moved(i))
        forward(i, 0, 2, across).start()
        forward(i, 0, 1, core).start()
        hidden_ref[span(i), :] = project(0, i)
        here_ref[span(i), :] = rows[0, span(i), :]
        return carry

    lax.fori_loop(0, parts, first, 0)

    def second(i, carry):
        forward(i, 0, 1, core).wait_recv()
        project(1, i)
        forward(i, 0, 2, across).wait_recv()
        forward(i, 2, 3, core).start()
        project(2, i)
        return carry

    lax.fori_loop(0, parts, second, 0)

    def third(i, carry):
        forward(i, 2, 3, core).wait_recv()
        project(3, i)
        return carry

    lax.fori_loop(0, parts, third, 0)
    lengths().wait()

    def last(i, carry):
        move_sent(*moved(i))
        forward(i, 0, 2, across).wait_send()
        forward(i, 0, 1, core).wait_send()
        forward(i, 2, 3, core).wait_send()
        for piece in range(4):
            to_hbm(piece, i).wait()
        return carry

    lax.fori_loop(0, parts, last, 0)


def start_work(tokens, clip_lengths, gain, shift, weight, bias):
    rows, width = tokens.shape
    vmem, anywhere = pl.BlockSpec(memory_space=pltpu.VMEM), pl.BlockSpec(memory_space=pl.ANY)
    projected, hidden, here, found = pl.pallas_call(
        start_kernel,
        in_specs=[anywhere] + [vmem] * 5,
        out_specs=[anywhere, vmem, vmem, vmem],
        out_shape=[
            jax.ShapeDtypeStruct((4 * rows, 3 * width), BF16),
            jax.ShapeDtypeStruct((rows, width), BF16),
            jax.ShapeDtypeStruct((rows, width), BF16),
            jax.ShapeDtypeStruct(clip_lengths.shape, jnp.int32),
        ],
        scratch_shapes=[
            pltpu.VMEM((4, rows, width), BF16),
            pltpu.VMEM((4 * rows, 3 * width), BF16),
            pltpu.SemaphoreType.DMA((5, 4)),
            pltpu.SemaphoreType.DMA((5, 4)),
            pltpu.SemaphoreType.DMA((4, 4)),
        ],
        compiler_params=pltpu.CompilerParams(
            vmem_limit_bytes=VMEM_BYTES, collective_id=0, has_side_effects=True
        ),
        cost_estimate=pl.CostEstimate(
            flops=24 * rows * width * width, bytes_accessed=32 * rows * width, transcendentals=0
        ),
        name="start_work",
    )(tokens, clip_lengths, gain, shift, weight, bias)
    return projected, hidden, here, jnp.where(stays(), clip_lengths, found)


class PairPlan:
    ways = True

    def start(self, tokens, clip_lengths, gain, shift, weight, bias):
        projected, hidden, here, lengths = start_work(
            tokens, clip_lengths, gain, shift, weight, bias
        )
        return projected, projected, hidden, here, lengths

    def positions(self, rows):
        core, z = lax.axis_index("dp") % 2, lax.axis_index("seq")
        found = []
        for piece in range(4):
            c, plane = core ^ (piece % 2), z ^ (piece // 2)
            shard = jnp.where(c == plane // 2, plane, plane ^ 2)
            found.append(shard * rows + jnp.arange(rows, dtype=jnp.int32))
        return jnp.concatenate(found)

    def own(self, gathered):
        return gathered

    def backward(self, work, weights, attention):
        here, hidden1, grad_out, projected, own, mark_k, mark_q = work
        chances, attended, log_totals = attention
        me = lax.axis_index("dp").astype(jnp.int32).reshape(1)
        block_out, grad, grad_middle, down, up, out, sum_up, sums = feed(
            here, attended, grad_out, *weights[2:], me
        )
        return results(
            *backward(
                chances,
                grad,
                attended,
                projected,
                self.own(mark_k),
                mark_q,
                log_totals,
                weights[0],
                hidden1,
                here,
                grad_middle,
                weights[1],
                sums,
                sum_up,
                [down.reshape((8,) + down.shape[2:]), up, out],
                block_out,
            )
        )


class PlainPlan:
    ways = None

    def __init__(self, pieces):
        self.pieces = pieces

    def start(self, tokens, clip_lengths, gain, shift, weight, bias):
        hidden = layer_norm(tokens.astype(F32), gain, shift)[0].astype(BF16)
        own = (matmul(hidden, weight) + bias).astype(BF16)
        projected = lax.all_gather(own, "seq", axis=0, tiled=True)
        return projected, own, hidden, tokens, clip_lengths

    def gather(self, own):
        gathered = lax.all_gather(own, "seq", axis=0, tiled=False)
        return [gathered[i] for i in range(self.pieces)]

    def positions(self, rows):
        return jnp.arange(rows * self.pieces, dtype=jnp.int32)

    def own(self, gathered):
        rows = gathered.shape[0] // self.pieces
        return lax.dynamic_slice_in_dim(gathered, lax.axis_index("seq") * rows, rows, 0)

    def backward(self, work, weights, attention):
        here, hidden1, grad_out, projected, own, mark_k, mark_q = work
        chances, attended, log_totals = attention
        w_qkv, ln1_gain, w_out, bias_out, gain, shift, w_up, bias_up, w_down, bias_down = weights
        middle = here.astype(F32) + matmul(attended, w_out) + bias_out
        normed_out, normed, inverse = layer_norm(middle, gain, shift)
        hidden = normed_out.astype(BF16)
        activated, slope = gelu_parts(matmul(hidden, w_up) + bias_up)
        activated = activated.astype(BF16)
        grad_upper = (inner_cols(grad_out, w_down) * slope).astype(BF16)
        grad_hidden = inner_cols(grad_upper, w_up)
        grad_norm, grad_gain, grad_shift = norm_back(grad_hidden, normed, inverse, gain)
        grad_middle = grad_out.astype(F32) + grad_norm
        grad_branch = grad_middle.astype(BF16)
        grad = inner_cols(grad_branch, w_out).astype(BF16)
        block_out = (middle + matmul(activated, w_down) + bias_down).astype(BF16)

        product = (grad.astype(F32) * attended.astype(F32)).reshape(grad.shape[0], -1, HDIM)
        deltas = jnp.sum(product, -1).T
        deltas = jnp.pad(deltas, ((0, STATS - deltas.shape[0]), (0, 0)))
        dq = grad_query(chances, grad, projected, deltas)
        dk, dv = grad_key_value(
            own,
            projected,
            self.gather(grad),
            self.gather(log_totals),
            self.gather(deltas),
            self.own(mark_k),
            mark_q,
        )
        grad_projected = jnp.concatenate([dq, dk, dv], 1)
        grad_hidden1 = inner_cols(grad_projected, w_qkv)
        _, normed1, inverse1 = layer_norm(here.astype(F32), 0.0, 0.0)
        grad_norm1, grad_ln1_gain, grad_ln1_shift = norm_back(
            grad_hidden1, normed1, inverse1, ln1_gain
        )

        def total(values):
            return jnp.sum(values.astype(F32), 0)

        return (block_out, (grad_middle + grad_norm1).astype(BF16)) + tuple(
            self.reduce(value)
            for value in (
                grad_ln1_gain,
                grad_ln1_shift,
                inner_rows(hidden1, grad_projected),
                total(dq),
                total(dv),
                inner_rows(attended, grad_branch),
                total(grad_branch),
                grad_gain,
                grad_shift,
                inner_rows(hidden, grad_upper),
                total(grad_upper),
                inner_rows(activated, grad_out),
                total(grad_out),
            )
        )

    def reduce(self, total):
        return lax.psum(lax.psum_scatter(total, "dp", scatter_dimension=0, tiled=True), "seq")


def body(
    plan,
    tokens,
    clip_lengths,
    ln1_gain,
    ln1_shift,
    w_qkv,
    bias_query,
    bias_value,
    w_out,
    bias_out,
    ln2_gain,
    ln2_shift,
    w_up,
    bias_up,
    w_down,
    bias_down,
    cotangent,
):
    rows, width = tokens.shape
    bias = jnp.concatenate([bias_query, jnp.zeros_like(bias_query), bias_value])
    projected, own, hidden1, here, lengths = plan.start(
        tokens, clip_lengths, ln1_gain, ln1_shift, w_qkv, bias
    )

    clip_ends = jnp.cumsum(lengths.reshape(-1))
    position = plan.positions(rows)
    segment = jnp.sum((position[:, None] >= clip_ends[None, :]).astype(jnp.int32), 1)
    lane = jnp.arange(LANES, dtype=jnp.int32)[None, :]
    same = lane == segment[:, None]
    mark_k = same.astype(BF16)
    mark_q = jnp.where(same | (lane >= clip_ends.shape[0]), 0.0, masked_score).astype(BF16)

    attended, chances, log_totals, grad_out = attend(
        plan, own, projected, plan.own(mark_q), mark_k, cotangent
    )

    return tuple(
        plan.backward(
            (here, hidden1, grad_out, projected, own, mark_k, mark_q),
            (
                w_qkv,
                ln1_gain,
                w_out,
                bias_out,
                ln2_gain,
                ln2_shift,
                w_up,
                bias_up,
                w_down,
                bias_down,
            ),
            (chances, attended, log_totals),
        )
    )


def solution(mesh):
    sizes = dict(mesh.shape)
    plan = PairPlan() if sizes == {"dp": 8, "seq": 4} else PlainPlan(sizes["seq"])
    rows = P(("dp", "seq"), None)
    return jax.shard_map(
        functools.partial(body, plan),
        mesh=mesh,
        in_specs=(rows, P("dp", None)) + (P(),) * 13 + (rows,),
        out_specs=(
            rows,
            rows,
            P("dp"),
            P("dp"),
            P("dp", None),
            P("dp"),
            P("dp"),
            P("dp", None),
            P("dp"),
            P("dp"),
            P("dp"),
            P("dp", None),
            P("dp"),
            P("dp", None),
            P("dp"),
        ),
        check_vma=False,
    )
```

```python
import functools
import math

import jax
import jax.numpy as jnp
from jax import lax
from jax.experimental import pallas as pl
from jax.experimental.pallas import tpu as pltpu
from jax.sharding import PartitionSpec as P

HDIM = 64
LANES = 128
STATS = 16
F32 = jnp.float32
BF16 = jnp.bfloat16
VMEM_BYTES = 56 << 20
NT = (((1,), (1,)), ((), ()))
NN = (((1,), (0,)), ((), ()))

epsilon = 1e-06
masked_score = -1e30


def dot_as(left, right, dims):
    return lax.dot_general(left, right, dims, preferred_element_type=F32)


def matmul(left, right):
    return dot_as(left, right, NN)


def inner_rows(left, right):
    return dot_as(left, right, (((0,), (0,)), ((), ())))


def inner_cols(left, right):
    return dot_as(left, right, NT)


def layer_norm(values, gain, shift):
    center = values - jnp.mean(values, -1, keepdims=True)
    inverse = lax.rsqrt(jnp.mean(center * center, -1, keepdims=True) + epsilon)
    normed = center * inverse
    return (normed * gain + shift, normed, inverse)


def row_of(ref):
    return ref[...].reshape(1, -1)


def norm_back(grad_out, normed, inverse, gain):
    scaled = grad_out * gain
    grad_in = inverse * (
        scaled
        - jnp.mean(scaled, -1, keepdims=True)
        - normed * jnp.mean(scaled * normed, -1, keepdims=True)
    )
    return (grad_in, jnp.sum(grad_out * normed, 0), jnp.sum(grad_out, 0))


def neighbours():
    dp, z = lax.axis_index("dp"), lax.axis_index("seq")
    other = dp + 1 - 2 * lax.rem(dp, jnp.int32(2))
    pair = z + 1 - 2 * lax.rem(z, jnp.int32(2))
    return (other, z), (dp, pair), (other, lax.rem(z + 2, jnp.int32(4)))


def stays():
    dp, z = lax.axis_index("dp"), lax.axis_index("seq")
    return lax.rem(dp, jnp.int32(2)) == lax.div(z, jnp.int32(2))


def greet(devices):
    barrier = pltpu.get_barrier_semaphore()
    for device in devices:
        pl.semaphore_signal(barrier, inc=1, device_id=device, device_id_type=pl.DeviceIdType.MESH)
    pl.semaphore_wait(barrier, len(devices))


def remote(source, target, sent, landed, device):
    return pltpu.make_async_remote_copy(
        src_ref=source,
        dst_ref=target,
        send_sem=sent,
        recv_sem=landed,
        device_id=device,
        device_id_type=pl.DeviceIdType.MESH,
    )


def move_start(source, target, sent, landed):
    swap = neighbours()[2]

    @pl.when(stays())
    def _():
        pltpu.make_async_copy(source, target, landed).start()

    @pl.when(jnp.logical_not(stays()))
    def _():
        remote(source, target, sent, landed, swap).start()


def move_landed(source, target, sent, landed):
    swap = neighbours()[2]

    @pl.when(stays())
    def _():
        pltpu.make_async_copy(source, target, landed).wait()

    @pl.when(jnp.logical_not(stays()))
    def _():
        remote(source, target, sent, landed, swap).wait_recv()


def move_sent(source, target, sent, landed):
    swap = neighbours()[2]

    @pl.when(jnp.logical_not(stays()))
    def _():
        remote(source, target, sent, landed, swap).wait_send()


def two_heads(values):
    lane = lax.broadcasted_iota(jnp.int32, values.shape, 1)
    zero = jnp.zeros_like(values)
    return jnp.concatenate(
        [jnp.where(lane < HDIM, values, zero), jnp.where(lane < HDIM, zero, values)], 0
    )


def own_columns(values):
    rows = values.shape[0] // 2
    lane = lax.broadcasted_iota(jnp.int32, (rows, LANES), 1)
    return jnp.where(lane < HDIM, values[:rows], values[rows:])


def own_rows(values):
    count = values.shape[1] // 2
    return jnp.transpose(jnp.concatenate([values[:HDIM, :count], values[HDIM:, count:]], 0))


def scaled_down(values):
    return values * jnp.asarray(1.0 / math.sqrt(HDIM), values.dtype)


def attend_kernel(ways, q_ref, k_ref, v_ref, mark_q, mark_k, *refs):
    pair = pl.program_id(0)
    if ways is None:
        out_ref, chance_ref, lse_ref = refs
    else:
        home_ref, out_ref, chance_ref, lse_ref, here_ref, sent, landed = refs
        move = (home_ref, here_ref, sent, landed)

        @pl.when(pair == 0)
        def _():
            greet([neighbours()[2]])
            move_start(*move)

    rows = q_ref.shape[0]
    marks = mark_q[...]
    queries = jnp.concatenate(
        [two_heads(scaled_down(q_ref[...])), jnp.concatenate([marks, marks], 0)], 1
    )
    scores = dot_as(jnp.concatenate([k_ref[...], mark_k[...]], 1), queries, NT)
    highest = jnp.max(scores, 0, keepdims=True)
    powers = jnp.exp(scores - highest)
    total = jnp.sum(powers, 0, keepdims=True)
    chances = (powers * (1.0 / total)).astype(BF16)
    chance_ref[0] = chances[:, :rows]
    chance_ref[1] = chances[:, rows:]
    out_ref[...] = own_rows(dot_as(jnp.transpose(v_ref[...]), chances, NN)).astype(BF16)
    log_total = highest + jnp.log(total)
    lse_ref[pl.ds(2 * pair, 1), :] = log_total[:, :rows]
    lse_ref[pl.ds(2 * pair + 1, 1), :] = log_total[:, rows:]

    if ways is not None:

        @pl.when(pair == pl.num_programs(0) - 1)
        def _():
            move_landed(*move)
            move_sent(*move)


def query_grads(chance_ref, grad, keys, values, deltas, sub=512):
    turned, grads = jnp.transpose(keys), two_heads(grad)
    delta = jnp.concatenate(deltas, 1)
    total = jnp.zeros((LANES, grads.shape[0]), F32)
    for first in range(0, keys.shape[0], sub):
        at = slice(first, first + sub)
        grad_chances = dot_as(values[at], grads, NT)
        chances = jnp.concatenate([chance_ref[0, at, :], chance_ref[1, at, :]], 1)
        scores = (chances.astype(F32) * (grad_chances - delta)).astype(BF16)
        total += dot_as(turned[:, at], scores, NN)
    return scaled_down(own_rows(total)).astype(BF16)


def key_sums(key, value, mark_k, parts):
    rows = key.shape[0]
    keys = jnp.concatenate([two_heads(key), jnp.concatenate([mark_k, mark_k], 0)], 1)
    values = two_heads(value)
    dk = dv = jnp.zeros((2 * rows, LANES), F32)
    for queries, grads, marks, log_totals, deltas in parts:
        scores = dot_as(keys, jnp.concatenate([scaled_down(queries), marks], 1), NT)
        grad_chances = dot_as(values, grads, NT)
        chances, grad_scores = [], []
        for head in range(2):
            at = slice(head * rows, (head + 1) * rows)
            powers = jnp.exp(scores[at] - log_totals[head])
            chances.append(powers.astype(BF16))
            grad_scores.append((powers * (grad_chances[at] - deltas[head])).astype(BF16))
        dv += dot_as(jnp.concatenate(chances, 0), grads, NN)
        dk += dot_as(jnp.concatenate(grad_scores, 0), queries, NN)
    return own_columns(dk), own_columns(dv)


def grad_query_kernel(chance_ref, grad_ref, k_ref, v_ref, delta_ref, dq_ref):
    pair = pl.program_id(0)
    deltas = [delta_ref[pl.ds(2 * pair + head, 1), :] for head in range(2)]
    dq_ref[...] = query_grads(chance_ref, grad_ref[...], k_ref[...], v_ref[...], deltas)


def grad_key_kernel(pieces, k_ref, v_ref, q_ref, *refs):
    g_refs = refs[:pieces]
    lse_refs, delta_refs = refs[pieces : 2 * pieces], refs[2 * pieces : 3 * pieces]
    mark_k, mark_q, dk_ref, dv_ref = refs[3 * pieces :]
    pair = pl.program_id(0)
    rows = g_refs[0].shape[0]
    parts = []
    for i in range(pieces):
        at = pl.ds(i * rows, rows)
        stats = [
            [ref[i][pl.ds(2 * pair + head, 1), :] for head in range(2)]
            for ref in (lse_refs, delta_refs)
        ]
        parts.append((q_ref[at, :], g_refs[i][...], mark_q[at, :], *stats))
    dk, dv = key_sums(k_ref[...], v_ref[...], mark_k[...], parts)
    dk_ref[...], dv_ref[...] = scaled_down(dk).astype(BF16), dv.astype(BF16)


def columns(rows, first):
    return pl.BlockSpec((rows, LANES), lambda t: (0, first + t))


def whole(array):
    return pl.BlockSpec(array.shape, lambda t: (0,) * array.ndim)


def kernel_call(kernel, name, grid, in_specs, out_specs, out_shape, scratch, flops, moved, **params):
    return pl.pallas_call(
        kernel,
        grid=grid,
        in_specs=in_specs,
        out_specs=out_specs,
        out_shape=out_shape,
        scratch_shapes=scratch,
        compiler_params=pltpu.CompilerParams(vmem_limit_bytes=VMEM_BYTES, **params),
        cost_estimate=pl.CostEstimate(flops=flops, bytes_accessed=moved, transcendentals=0),
        name=name,
    )


def attend(plan, own, projected, mark_q, mark_k, cotangent):
    rows, width = cotangent.shape
    length, pairs = projected.shape[0], width // LANES
    stats = jax.ShapeDtypeStruct((STATS, rows), F32)
    anywhere = pl.BlockSpec(memory_space=pl.ANY)
    ways = plan.ways
    moving = [] if ways is None else [cotangent]
    params = {} if ways is None else {"collective_id": 1, "has_side_effects": True}
    results = kernel_call(
        functools.partial(attend_kernel, ways),
        "attend",
        (pairs,),
        [
            columns(rows, 0),
            columns(length, pairs),
            columns(length, 2 * pairs),
            pl.BlockSpec((rows, LANES), lambda t: (0, 0)),
            whole(mark_k),
        ]
        + [anywhere] * len(moving),
        [
            columns(rows, 0),
            pl.BlockSpec((2, length, rows), lambda t: (t, 0, 0)),
            whole(stats),
        ]
        + [anywhere] * len(moving),
        [
            jax.ShapeDtypeStruct((rows, width), BF16),
            jax.ShapeDtypeStruct((2 * pairs, length, rows), BF16),
            stats,
        ]
        + [jax.ShapeDtypeStruct(array.shape, array.dtype) for array in moving],
        [pltpu.SemaphoreType.DMA] * (2 * len(moving)),
        24 * rows * length * width,
        4 * pairs * rows * length,
        **params,
    )(own, projected, projected, mark_q, mark_k, *moving)
    return tuple(results) if moving else tuple(results) + (cotangent,)


def grad_query(chances, grad, projected, deltas):
    rows, width = grad.shape
    length, pairs = projected.shape[0], width // LANES
    return kernel_call(
        grad_query_kernel,
        "grad_query",
        (pairs,),
        [
            pl.BlockSpec((2, length, rows), lambda t: (t, 0, 0)),
            columns(rows, 0),
            columns(length, pairs),
            columns(length, 2 * pairs),
            whole(deltas),
        ],
        columns(rows, 0),
        jax.ShapeDtypeStruct((rows, width), BF16),
        [],
        16 * rows * length * width,
        4 * pairs * rows * length,
    )(chances, grad, projected, projected, deltas)


def grad_key_value(own, projected, grads, log_totals, deltas, mark_k, mark_q):
    rows, width = grads[0].shape
    pieces, pairs = len(grads), width // LANES
    length = rows * pieces
    result = jax.ShapeDtypeStruct((rows, width), BF16)
    return kernel_call(
        functools.partial(grad_key_kernel, pieces),
        "grad_key_value",
        (pairs,),
        [columns(rows, pairs), columns(rows, 2 * pairs), columns(length, 0)]
        + [columns(rows, 0)] * pieces
        + [whole(log_totals[0])] * (2 * pieces)
        + [whole(mark_k), whole(mark_q)],
        [columns(rows, 0)] * 2,
        [result] * 2,
        [],
        32 * rows * length * width,
        8 * length * width,
    )(own, own, projected, *grads, *log_totals, *deltas, mark_k, mark_q)


class Chunk:
    stages = ("start", "near", "far", "along", "meet", "spread", "finish")

    def __init__(self, source, rows, columns, y_first, when, held=False, dtype=BF16):
        self.source, self.rows, self.columns = source, rows, columns
        self.shape = (rows[1], columns[1])
        self.blocks = ((2, 3), 1) if y_first else ((1, 3), 2)
        self.y_first, self.when, self.held, self.dtype = y_first, when, held, dtype

    def scratch(self):
        rows, columns = self.shape
        lead = [(4,), (2,), (), (), ()] if self.held else [(4,), (2,), (), (), (), (4,)]
        return [pltpu.VMEM(first + (rows, columns), self.dtype) for first in lead] + [
            pltpu.SemaphoreType.DMA((7,)),
            pltpu.SemaphoreType.DMA((8,)),
        ]

    def bind(self, source, out, scratch, devices):
        at = (pl.ds(*self.rows), pl.ds(*self.columns))
        kept = source.at[(pl.ds(0, 4),) + at]
        self.out = out.at[at]
        core, first, second, z1, z2, *rest = scratch
        *rest, sent, landed = rest
        self.keep = kept if self.held else rest[0]
        self.core, self.first, self.second, self.z1, self.z2 = core, first, second, z1, z2
        near, far = (devices["y"], devices["x"]) if self.y_first else (devices["x"], devices["y"])
        sends, last = self.blocks
        self.load = pltpu.make_async_copy(kept, self.keep, landed.at[7])
        self.to_core = remote(
            source.at[(pl.ds(4, 4),) + at], core, sent.at[0], landed.at[0], devices["core"]
        )
        self.to_near = [
            remote(self.keep.at[b], first.at[i], sent.at[1 + i], landed.at[1 + i], near)
            for i, b in enumerate(sends)
        ]
        self.to_far = remote(self.keep.at[last], second, sent.at[3], landed.at[3], far)
        self.bind_along(sent, landed, devices)

    def bind_along(self, sent, landed, devices):
        pair, z1 = devices["pair"], self.z1
        self.inward = remote(self.keep.at[0], z1, sent.at[4], landed.at[4], pair)
        self.middle = remote(self.keep.at[0], self.z2, sent.at[5], landed.at[5], devices["mirror"])
        self.outward = remote(z1, self.out, sent.at[6], landed.at[6], pair)
        self.store = pltpu.make_async_copy(z1, self.out, landed.at[6])

    def add(self, target, one, other):
        target[...] = one[...] + other[...]

    def start(self):
        self.to_core.start()
        if not self.held:
            self.load.start()

    def near(self):
        if not self.held:
            self.load.wait()
        self.to_core.wait_recv()
        sends = self.blocks[0]
        for block in sends:
            self.add(self.keep.at[block], self.keep.at[block], self.core.at[block])
        for copy in self.to_near:
            copy.start()
        for block in range(4):
            if block not in sends:
                self.add(self.keep.at[block], self.keep.at[block], self.core.at[block])

    def join(self, block):
        stay = [b for b in range(4) if b not in self.blocks[0]]
        i = stay.index(block)
        self.to_near[i].wait_recv()
        self.add(self.keep.at[block], self.keep.at[block], self.first.at[i])

    def far(self):
        self.join(self.blocks[1])
        self.to_far.start()
        self.join(0)

    def along(self):
        self.to_far.wait_recv()
        self.add(self.keep.at[0], self.keep.at[0], self.second)

        @pl.when(jnp.logical_not(inner()))
        def _():
            self.inward.start()

    def meet(self):
        @pl.when(inner())
        def _():
            self.inward.wait_recv()
            self.add(self.keep.at[0], self.keep.at[0], self.z1)
            self.middle.start()

    def spread(self):
        @pl.when(inner())
        def _():
            self.middle.wait_recv()
            self.add(self.z1, self.keep.at[0], self.z2)
            self.outward.start()
            self.store.start()

    def finish(self):
        @pl.when(jnp.logical_not(inner()))
        def _():
            self.outward.wait_recv()
            self.inward.wait_send()

        @pl.when(inner())
        def _():
            self.store.wait()
            self.middle.wait_send()
            self.outward.wait_send()

        self.settle()

    def settle(self):
        self.to_core.wait_send()
        for copy in self.to_near:
            copy.wait_send()
        self.to_far.wait_send()


class DirectChunk:
    stages = ("start", "near", "far")

    def __init__(self, source, rows, columns, when, dtype=BF16):
        self.source, self.rows, self.columns = source, rows, columns
        self.shape = (rows[1], columns[1])
        self.when, self.dtype = when, dtype

    def scratch(self):
        rows, columns = self.shape
        return [pltpu.VMEM(first + (rows, columns), self.dtype) for first in ((8,), (3,), ())] + [
            pltpu.SemaphoreType.DMA((10,)),
            pltpu.SemaphoreType.DMA((11,)),
        ]

    def bind(self, source, out, scratch, devices):
        at = (pl.ds(*self.rows), pl.ds(*self.columns))
        self.mine = source.at[(0,) + at]
        self.landing, self.others, self.total, sent, landed = scratch
        self.around = [
            remote(
                source.at[(place,) + at],
                self.landing.at[place],
                sent.at[place - 1],
                landed.at[place - 1],
                devices["block"][place],
            )
            for place in range(1, 8)
        ]
        self.along_z = [
            remote(self.total, self.others.at[i], sent.at[7 + i], landed.at[7 + i], devices[name])
            for i, name in enumerate(("pair", "mirror", "opposite"))
        ]
        self.store = pltpu.make_async_copy(self.landing.at[0], out.at[at], landed.at[10])

    def start(self):
        for copy in self.around:
            copy.start()

    def near(self):
        total = self.mine[...].astype(F32)
        for i, copy in enumerate(self.around):
            copy.wait_recv()
            total = total + self.landing[1 + i].astype(F32)
        self.total[...] = total.astype(self.dtype)
        for copy in self.along_z:
            copy.start()

    def far(self):
        for copy in self.along_z:
            copy.wait_recv()
        total = self.total[...].astype(F32) + self.others[0].astype(F32)
        total = total + (self.others[1].astype(F32) + self.others[2].astype(F32))
        self.landing[0] = total.astype(self.dtype)
        self.store.start()

    def finish(self):
        self.store.wait()
        for copy in self.around + self.along_z:
            copy.wait_send()


def inner():
    z = lax.axis_index("seq")
    return jnp.logical_and(z > 0, z < 3)


def ring_devices():
    dp, z = lax.axis_index("dp"), lax.axis_index("seq")
    core, pair, swap = neighbours()

    def flip(index, bit):
        size = 1 << bit
        return index + size - 2 * size * lax.rem(lax.div(index, jnp.int32(size)), jnp.int32(2))

    blocks = []
    for place in range(8):
        index = dp
        for bit, flips in enumerate((place // 4, place % 2, place // 2 % 2)):
            if flips:
                index = flip(index, bit)
        blocks.append((index, z))
    return {
        "core": core,
        "pair": pair,
        "swap": swap,
        "x": blocks[1],
        "y": blocks[2],
        "mirror": (dp, 3 - z),
        "opposite": (dp, lax.rem(z + 2, jnp.int32(4))),
        "block": blocks,
    }


def relative_place(*bits):
    dp = lax.axis_index("dp")
    turned = [
        lax.rem(lax.div(dp, jnp.int32(1 << k)) + bit, jnp.int32(2)) for k, bit in enumerate(bits)
    ]
    return turned[0] * 4 + turned[1] + turned[2] * 2


def bits_of(block):
    return [(block >> k) % 2 for k in range(3)]


def store_blocks(target, columns, total):
    part = total.shape[0] // 8
    for block in range(8):
        target[relative_place(*bits_of(block)), :, columns] = total[block * part : (block + 1) * part].astype(BF16)


VECTORS = 16


def backward_chunks(shapes, width, pairs):
    down, up, _ = shapes
    part, quarter, share = width // 8, down[1] // 4, up[2] // 4
    end = 4 * pairs
    tile = LANES

    def when(*steps):
        return tuple(at if isinstance(at, tuple) else (at, 0) for at in steps)

    rows, whole_width = (0, part), (0, width)
    downs = [((i * quarter, quarter), whole_width, i % 2 == 0) for i in range(4)]
    ups = [(rows, (i * share, share), i % 2 == 0) for i in range(4)]
    return [
        Chunk("down", *downs[0], when(0, 1, 4, 8, 12, 15)),
        Chunk("down", *downs[1], when(0, 1, 4, 8, 12, 15)),
        Chunk("down", *downs[2], when(1, 3, 6, 10, 13, 16)),
        Chunk("down", *downs[3], when(1, 3, 6, 10, 13, 16)),
        Chunk("up", *ups[0], when(3, 5, 8, 12, 15, 18)),
        Chunk("up", *ups[1], when(3, 5, 8, 12, 15, 18)),
        Chunk("up", *ups[2], when(5, 7, 11, 14, 17, 20)),
        Chunk("up", *ups[3], when(5, 7, 11, 14, 17, 20)),
        Chunk("out", rows, whole_width, True, when(7, 10, 13, 16, 19, 21)),
        Chunk("pair", rows, (0 * tile, 4 * tile), False, when(14, 15, 17, 19, 21, 23), True),
        Chunk("pair", rows, (4 * tile, 4 * tile), True, when(16, 17, 19, 21, 23, (end, 0)), True),
        Chunk("pair", rows, (8 * tile, 4 * tile), False, when(18, 19, 21, 23, (end, 0), (end, 1)), True),
        Chunk("query", rows, (0, 2 * tile), True, when(20, 21, 23, (end, 0), (end, 1), (end, 2)), True),
        Chunk("query", rows, (2 * tile, 2 * tile), False, when(22, 23, (end, 0), (end, 1), (end, 2), (end, 3)), True),
        DirectChunk("query", rows, (4 * tile, tile), when(23, (end, 0), (end, 2))),
        DirectChunk("query", rows, (5 * tile, tile), when((end, 0), (end, 1), (end, 3))),
        DirectChunk("vector", (0, VECTORS), (0, LANES), when((end, 0), (end, 1), (end, 3)), F32),
    ]


def backward_kernel(
    shapes,
    pairs,
    chance_ref,
    grad_ref,
    attended_ref,
    k_ref,
    v_ref,
    q_ref,
    mark_k,
    mark_q,
    lse_ref,
    gain_ref,
    sums_ref,
    sum_up_ref,
    w_hbm,
    hidden_hbm,
    here_hbm,
    middle_hbm,
    grad_down,
    grad_up,
    grad_out,
    block_ref,
    home_ref,
    tokens_ref,
    down_ref,
    up_ref,
    out_ref,
    query_ref,
    pair_ref,
    vector_ref,
    grads,
    stats,
    own_stats,
    turned,
    dq,
    grad_hidden,
    query_grad,
    pair_grad,
    vector,
    late,
    tokens,
    partial,
    weights,
    hidden_ref,
    here_ref,
    middle_ref,
    sent,
    landed,
    loaded,
    *scratch,
):
    step = pl.program_id(0)
    rows, width = grad_ref.shape
    held = ((hidden_hbm, hidden_ref), (w_hbm, weights), (here_hbm, here_ref), (middle_hbm, middle_ref))
    loads = [
        pltpu.make_async_copy(source, target, loaded.at[i])
        for i, (source, target) in enumerate(held)
    ]
    half = rows // 2
    steps = 4 * pairs
    devices = ring_devices()
    chunks = backward_chunks(shapes, width, pairs)
    sources = {
        "down": (grad_down, down_ref),
        "up": (grad_up, up_ref),
        "out": (grad_out, out_ref),
        "query": (query_grad, query_ref),
        "pair": (pair_grad, pair_ref),
        "vector": (vector, vector_ref),
    }
    scratch = list(scratch)
    for chunk in chunks:
        count = len(chunk.scratch())
        chunk.bind(*sources[chunk.source], scratch[:count], devices)
        del scratch[:count]
    block_move = (block_ref, home_ref, sent.at[12], landed.at[12])

    def token_move(part):
        at = pl.ds(part * half, half)
        return (tokens.at[at], tokens_ref.at[at], sent.at[13 + part], landed.at[13 + part])

    def grad_copy(i, part, source, device):
        at = pl.ds(part * half, half)
        n = 2 * i + part
        return remote(source.at[at], grads.at[i - 1, at], sent.at[n], landed.at[n], device)

    def to_core(part):
        return grad_copy(1, part, grad_ref, devices["core"])

    def to_pair(part):
        return grad_copy(2, part, grad_ref, devices["pair"])

    def to_corner(part):
        return grad_copy(3, part, grads.at[1], devices["core"])

    def stat_copy(i, source, device):
        return remote(source, stats.at[i], sent.at[8 + i], landed.at[8 + i], device)

    stat_core = stat_copy(1, own_stats, devices["core"])
    stat_pair = stat_copy(2, own_stats, devices["pair"])
    stat_corner = stat_copy(3, stats.at[2], devices["core"])

    def begin():
        greet(devices["block"][1:] + [devices[name] for name in ("pair", "swap", "mirror", "opposite")])
        for part in range(2):
            to_pair(part).start()
        for part in range(2):
            to_core(part).start()
        for load in loads:
            load.start()

    def begin_stats():
        product = grad_ref[...].astype(F32) * attended_ref[...].astype(F32)
        high = product.astype(BF16)
        low = (product - high.astype(F32)).astype(BF16)
        head = lax.broadcasted_iota(jnp.int32, (STATS, width), 0)
        column = lax.broadcasted_iota(jnp.int32, (STATS, width), 1)
        mine = jnp.where(
            jnp.logical_and(column >= head * HDIM, column < (head + 1) * HDIM), 1.0, 0.0
        ).astype(BF16)
        own_stats[0:STATS, :] = lse_ref[...]
        own_stats[STATS:, :] = dot_as(mine, high, NT) + dot_as(mine, low, NT)
        stats[0] = own_stats[...]
        stat_pair.start()
        stat_core.start()
        late[...] = jnp.zeros_like(late)
        grad_hidden[...] = jnp.zeros_like(grad_hidden)
        stat_core.wait_recv()
        for part in range(2):
            to_core(part).wait_recv()

    def loaded_all():
        for load in loads:
            load.wait()
        turned[...] = jnp.transpose(hidden_ref[...])

    def corner_stats():
        stat_pair.wait_recv()
        stat_corner.start()

    def corner(part):
        def run():
            to_pair(part).wait_recv()
            to_corner(part).start()

        return run

    def far_grads():
        stat_corner.wait_recv()
        for part in range(2):
            to_corner(part).wait_recv()

    def first_norm(part):
        def run():
            at = pl.ds(part * half, half)
            _, unit, root = layer_norm(here_ref[at, :].astype(F32), 0.0, 0.0)
            grad = grad_hidden[at, :]
            scaled = grad * row_of(gain_ref)
            grad_in = root * (
                scaled
                - jnp.mean(scaled, -1, keepdims=True)
                - unit * jnp.mean(scaled * unit, -1, keepdims=True)
            )
            tokens[at, :] = (middle_ref[at, :] + grad_in).astype(BF16)
            move_start(*token_move(part))
            late[2:3, :] += jnp.sum(grad * unit, 0, keepdims=True)
            late[3:4, :] += jnp.sum(grad, 0, keepdims=True)

        return run

    def early_vectors():
        share = width // 8
        vector[...] = jnp.zeros_like(vector)
        for block in range(8):
            place = relative_place(*bits_of(block))
            vector[place, 0:4, 0:share] = sums_ref[0:4, block * share : (block + 1) * share]
            for i in range(4):
                first = (block * 4 + i) * share
                vector[place, 8 + i : 9 + i, 0:share] = sum_up_ref[0:1, first : first + share]

    def late_vectors():
        share = width // 8
        for block in range(8):
            vector[relative_place(*bits_of(block)), 4:8, 0:share] = late[
                0:4, block * share : (block + 1) * share
            ]

    def finish_moves():
        for move in (block_move, token_move(0), token_move(1)):
            move_landed(*move)
            move_sent(*move)
        for copy in (stat_core, stat_pair, stat_corner):
            copy.wait_send()
        for part in range(2):
            to_core(part).wait_send()
            to_pair(part).wait_send()
            to_corner(part).wait_send()

    events = [
        ((0, -2), begin),
        ((0, -1), begin_stats),
        ((1, 1), early_vectors),
        ((2, -1), corner_stats),
        ((8, -1), corner(0)),
        ((5, 1), loaded_all),
        ((4, 3), lambda: move_start(*block_move)),
        ((11, -1), corner(1)),
        ((2 * pairs, 1), far_grads),
        ((3 * pairs, -1), first_norm(0)),
        ((steps, -2), first_norm(1)),
        ((steps, -1), late_vectors),
        ((steps, 99), finish_moves),
    ]
    for order in (2, 1, 0, 3, 4, 5):
        for chunk in chunks:
            if order < len(chunk.when):
                events.append((chunk.when[order], getattr(chunk, chunk.stages[order])))
    events += [((steps, 98), chunk.finish) for chunk in chunks]
    events.sort(key=lambda event: event[0])

    def run(at):
        for (when, _), event in events:
            if when == at:
                event()

    for at in range(steps):
        if any(when == at for (when, _), _ in events):

            @pl.when(step == at)
            def _():
                run(at)

    pair = lax.rem(step, jnp.int32(pairs))
    tile = pl.ds(pl.multiple_of(pair * LANES, LANES), LANES)
    double = pl.ds(pl.multiple_of(pair * (2 * LANES), 2 * LANES), 2 * LANES)

    def weight(part):
        return weights[:, pl.ds(pl.multiple_of(part * width + pair * LANES, LANES), LANES)]

    def keys_of(pieces):
        parts = []
        for i, first in [(i, first) for i in pieces for first in (0, half)]:
            span, at = pl.ds(i * rows + first, half), pl.ds(first, half)
            rows_of = [
                [stats[i, pl.ds(start + 2 * pair + head, 1), at] for head in range(2)]
                for start in (0, STATS)
            ]
            piece = grad_ref if i == 0 else grads.at[i - 1]
            parts.append((q_ref[span, :], piece[at, tile], mark_q[span, :], *rows_of))
        return key_sums(k_ref[0:rows, :], v_ref[0:rows, :], mark_k[...], parts)

    @pl.when(step < pairs)
    def _():
        partial[pair, 0], partial[pair, 1] = keys_of((0, 1))

    @pl.when(jnp.logical_and(step >= 2 * pairs, step < 3 * pairs))
    def _():
        dk, dv = keys_of((2, 3))
        dk = scaled_down(dk + partial[pair, 0]).astype(BF16)
        dv = dv + partial[pair, 1]
        late[1:2, tile] = jnp.sum(dv.astype(BF16).astype(F32), 0, keepdims=True)
        both = jnp.concatenate([dk, dv.astype(BF16)], 1)
        store_blocks(pair_grad, double, dot_as(turned[...], both, NN))
        grad_hidden[...] += dot_as(both, jnp.concatenate([weight(1), weight(2)], 1), NT)

    @pl.when(lax.rem(lax.div(step, jnp.int32(pairs)), jnp.int32(2)) == 1)
    def _():
        part = lax.div(step, jnp.int32(2 * pairs))
        at = pl.ds(pl.multiple_of(part * half, half), half)
        deltas = [own_stats[pl.ds(STATS + 2 * pair + head, 1), at] for head in range(2)]
        found = query_grads(chance_ref, grad_ref[at, tile], k_ref[...], v_ref[...], deltas)
        dq[at, tile] = found
        late[0:1, tile] += jnp.sum(found.astype(F32), 0, keepdims=True)
        grad_hidden[at, :] += dot_as(found, weight(0), NT)

        @pl.when(part == 1)
        def _():
            store_blocks(query_grad, tile, dot_as(turned[...], dq[:, tile], NN))

    @pl.when(step == steps - 1)
    def _():
        run(steps)


def once(array):
    return pl.BlockSpec(array.shape, lambda *t: (0,) * array.ndim, pipeline_mode=pl.Buffered(1))


def backward(
    chances,
    grad,
    attended,
    projected,
    mark_k,
    mark_q,
    log_totals,
    weight,
    hidden,
    here,
    grad_middle,
    gain,
    sums,
    sum_up,
    totals,
    block_out,
):
    rows, width = grad.shape
    length, pairs = projected.shape[0], width // LANES
    shapes = [total.shape for total in totals]
    part = width // 8
    anywhere = pl.BlockSpec(memory_space=pl.ANY)
    result = jax.ShapeDtypeStruct((rows, width), BF16)
    outs = [result, result] + [
        jax.ShapeDtypeStruct(shape, BF16)
        for shape in [shape[1:] for shape in shapes] + [(part, width), (part, 2 * width)]
    ]
    outs.append(jax.ShapeDtypeStruct((VECTORS, LANES), F32))

    def tile(first):
        return pl.BlockSpec((length, LANES), lambda t: (0, first + lax.rem(t, pairs)))

    def chance_at(t):
        phase = lax.div(t, pairs)
        return jnp.where(lax.rem(phase, 2) == 1, lax.rem(t, pairs), 0), 0, lax.div(phase, 2)

    def query_at(t):
        return 0, jnp.where(lax.rem(lax.div(t, pairs), 2) == 0, lax.rem(t, pairs), pairs - 1)

    fixed = [mark_k, mark_q, log_totals, gain, sums, sum_up]
    held = [weight, hidden, here, grad_middle]
    chunks = backward_chunks(shapes, width, pairs)
    stats = (2 * STATS, rows)
    return kernel_call(
        functools.partial(backward_kernel, shapes, pairs),
        "backward",
        (4 * pairs,),
        [
            pl.BlockSpec((2, length, rows // 2), chance_at),
            once(grad),
            once(attended),
            tile(pairs),
            tile(2 * pairs),
            pl.BlockSpec((length, LANES), query_at),
        ]
        + [pl.BlockSpec((rows, LANES), lambda t: (0, 0), pipeline_mode=pl.Buffered(1))]
        + [once(array) for array in fixed[1:]]
        + [anywhere] * (len(held) + len(totals) + 1),
        [anywhere] * len(outs),
        outs,
        [
            pltpu.VMEM((3, rows, width), BF16),
            pltpu.VMEM((4,) + stats, F32),
            pltpu.VMEM(stats, F32),
            pltpu.VMEM((width, rows), BF16),
            pltpu.VMEM((rows, width), BF16),
            pltpu.VMEM((rows, width), F32),
            pltpu.VMEM((8, part, width), BF16),
            pltpu.VMEM((8, part, 2 * width), BF16),
            pltpu.VMEM((8, VECTORS, LANES), F32),
            pltpu.VMEM((8, width), F32),
            pltpu.VMEM((rows, width), BF16),
            pltpu.VMEM((pairs, 2, rows, LANES), F32),
        ]
        + [pltpu.VMEM(array.shape, array.dtype) for array in held]
        + [
            pltpu.SemaphoreType.DMA((15,)),
            pltpu.SemaphoreType.DMA((15,)),
            pltpu.SemaphoreType.DMA((len(held),)),
        ]
        + [entry for chunk in chunks for entry in chunk.scratch()],
        48 * rows * length * width,
        4 * pairs * rows * length,
        collective_id=2,
        has_side_effects=True,
    )(chances, grad, attended, projected, projected, projected, *fixed, *held, *totals, block_out)


def results_kernel(block, tokens, down, up, out, query, pair, vector, *outs):
    (
        block_ref,
        tokens_ref,
        ln1_gain,
        ln1_shift,
        w_qkv,
        bias_query,
        bias_value,
        w_out,
        bias_out,
        ln2_gain,
        ln2_shift,
        w_up,
        bias_up,
        w_down,
        bias_down,
    ) = outs
    block_ref[...] = block[...]
    tokens_ref[...] = tokens[...]
    width = query.shape[1]
    w_qkv[:, 0:width] = query[...].astype(F32)
    for i in range(width // LANES):
        for j in range(2):
            first = (2 * i + j) * LANES
            to = (1 + j) * width + i * LANES
            w_qkv[:, to : to + LANES] = pair[:, first : first + LANES].astype(F32)
    w_up[...] = up[...].astype(F32)
    w_down[...] = down[...].astype(F32)
    w_out[...] = out[...].astype(F32)
    share = width // 8
    order = (ln2_gain, ln2_shift, bias_out, bias_down, bias_query, bias_value, ln1_gain, ln1_shift)
    for i, ref in enumerate(order):
        ref[...] = vector[i, 0:share]
    bias_up[...] = jnp.concatenate([vector[8 + i : 9 + i, 0:share] for i in range(4)], 1)[0]


def results(block, tokens, down, up, out, query, pair, vector):
    part, width = query.shape
    vmem = pl.BlockSpec(memory_space=pltpu.VMEM)

    def line(size=part):
        return jax.ShapeDtypeStruct((size,), F32)

    def like(array):
        return jax.ShapeDtypeStruct(array.shape, F32)

    return pl.pallas_call(
        results_kernel,
        in_specs=[vmem] * 8,
        out_specs=[vmem] * 15,
        out_shape=[
            jax.ShapeDtypeStruct(block.shape, BF16),
            jax.ShapeDtypeStruct(tokens.shape, BF16),
            line(),
            line(),
            jax.ShapeDtypeStruct((part, 3 * width), F32),
            line(),
            line(),
            like(out),
            line(),
            line(),
            line(),
            like(up),
            line(4 * part),
            like(down),
            line(),
        ],
        compiler_params=pltpu.CompilerParams(vmem_limit_bytes=VMEM_BYTES),
        name="results",
    )(block, tokens, down, up, out, query, pair, vector)


def gelu_parts(pre_act):
    inside = 0.5 * (1.0 + lax.erf(pre_act * math.sqrt(0.5)))
    slope = inside + pre_act * jnp.exp(-0.5 * pre_act * pre_act) * (1.0 / math.sqrt(2.0 * math.pi))
    return pre_act * inside, slope


def relative(block, me):
    turned = block ^ me
    return (turned % 2) * 4 + turned // 2


def feed_kernel(
    sub,
    index_ref,
    here_ref,
    attended_ref,
    grad_ref,
    w_out_ref,
    bias_out_ref,
    gain_ref,
    shift_ref,
    w_up_ref,
    bias_up_ref,
    w_down_ref,
    bias_down_ref,
    block_ref,
    grad_attended_ref,
    grad_middle_ref,
    down_ref,
    up_ref,
    out_ref,
    sum_up_ref,
    sums_ref,
    middle,
    normed,
    inverse,
    hidden,
    turned,
    total,
    grad_hidden,
    activated,
    grad_upper,
):
    step, last = pl.program_id(0), pl.num_programs(0) - 1
    me = index_ref[0]
    rows, width = here_ref.shape
    blocks = rows // sub

    def span(i):
        return pl.ds(pl.multiple_of(i * sub, sub), sub)

    @pl.when(step == 0)
    def _():
        def norm(i, carry):
            at = span(i)
            values = (
                here_ref[at, :].astype(F32)
                + dot_as(attended_ref[at, :], w_out_ref[...], NN)
                + row_of(bias_out_ref)
            )
            out, unit, root = layer_norm(values, row_of(gain_ref), row_of(shift_ref))
            middle[at, :] = values
            normed[at, :] = unit
            inverse[at, :] = jnp.broadcast_to(root, (sub, LANES))
            hidden[at, :] = out.astype(BF16)
            total[at, :] = values + row_of(bias_down_ref)
            grad_hidden[at, :] = jnp.zeros((sub, width), F32)
            return carry

        lax.fori_loop(0, blocks, norm, 0)
        turned[...] = jnp.transpose(hidden[...])

    def tile(i, carry):
        at = span(i)
        upper = dot_as(hidden[at, :], w_up_ref[...], NN) + bias_up_ref[...]
        grad_activated = dot_as(grad_ref[at, :], w_down_ref[...], NT)
        active, slope = gelu_parts(upper)
        active = active.astype(BF16)
        grad_in = (grad_activated * slope).astype(BF16)
        activated[at, :] = active
        grad_upper[at, :] = grad_in
        total[at, :] += dot_as(active, w_down_ref[...], NN)
        grad_hidden[at, :] += dot_as(grad_in, w_up_ref[...], NT)
        return carry + jnp.sum(grad_in.astype(F32), 0, keepdims=True)

    sum_up_ref[...] = lax.fori_loop(0, blocks, tile, jnp.zeros(sum_up_ref.shape, F32))

    grad_up = dot_as(turned[...], grad_upper[...], NN)
    part = width // 8
    for block in range(8):
        up_ref[relative(block, me)] = grad_up[block * part : (block + 1) * part].astype(BF16)
    grad_down = inner_rows(activated[...], grad_ref[...])
    part = down_ref.shape[2]
    for i in range(2):
        down_ref[(i ^ me) % 2, 0] = grad_down[i * part : (i + 1) * part].astype(BF16)

    @pl.when(step == last)
    def _():
        def norm(i, carry):
            at = span(i)
            block_ref[at, :] = total[at, :].astype(BF16)
            grad, unit = grad_hidden[at, :], normed[at, :]
            scaled = grad * row_of(gain_ref)
            grad_in = inverse[at, 0:1] * (
                scaled
                - jnp.mean(scaled, -1, keepdims=True)
                - unit * jnp.mean(scaled * unit, -1, keepdims=True)
            )
            before = grad_ref[at, :].astype(F32)
            grad_in = before + grad_in
            branch = grad_in.astype(BF16)
            grad_middle_ref[at, :] = grad_in
            hidden[at, :] = branch
            grad_attended_ref[at, :] = dot_as(branch, w_out_ref[...], NT).astype(BF16)
            sums = [grad * unit, grad, branch.astype(F32), before]
            return tuple(
                old + jnp.sum(value, 0, keepdims=True) for old, value in zip(carry, sums)
            )

        zero = jnp.zeros((1, width), F32)
        sums = lax.fori_loop(0, blocks, norm, (zero,) * 4)
        sums_ref[...] = jnp.concatenate(list(sums) + [zero] * 4, 0)
        grad_out = inner_rows(attended_ref[...], hidden[...])
        part = width // 8
        for block in range(8):
            out_ref[relative(block, me)] = grad_out[block * part : (block + 1) * part].astype(BF16)


def feed(
    here, attended, grad, w_out, bias_out, gain, shift, w_up, bias_up, w_down, bias_down, me, sub=256
):
    rows, width = here.shape
    wide = w_up.shape[1]
    steps = 4
    tile = wide // steps
    part = width // 8

    def once(*shape):
        return pl.BlockSpec(shape, lambda f, at: (0,) * len(shape), pipeline_mode=pl.Buffered(1))

    act = once(rows, width)
    line = once(width)
    outs = [
        jax.ShapeDtypeStruct((rows, width), BF16),
        jax.ShapeDtypeStruct((rows, width), BF16),
        jax.ShapeDtypeStruct((rows, width), F32),
        jax.ShapeDtypeStruct((2, 4, wide // 8, width), BF16),
        jax.ShapeDtypeStruct((8, part, wide), BF16),
        jax.ShapeDtypeStruct((8, part, width), BF16),
        jax.ShapeDtypeStruct((1, wide), F32),
        jax.ShapeDtypeStruct((8, width), F32),
    ]
    return pl.pallas_call(
        functools.partial(feed_kernel, sub),
        grid_spec=pltpu.PrefetchScalarGridSpec(
            num_scalar_prefetch=1,
            grid=(steps,),
            in_specs=[
                act,
                act,
                act,
                once(width, width),
                line,
                line,
                line,
                pl.BlockSpec((width, tile), lambda f, at: (0, f)),
                pl.BlockSpec((1, tile), lambda f, at: (0, f)),
                pl.BlockSpec((tile, width), lambda f, at: (f, 0)),
                line,
            ],
            out_specs=[
                act,
                act,
                act,
                pl.BlockSpec((2, 1, wide // 8, width), lambda f, at: (0, f ^ (at[0] // 2), 0, 0)),
                pl.BlockSpec((8, part, tile), lambda f, at: (0, 0, f)),
                once(8, part, width),
                pl.BlockSpec((1, tile), lambda f, at: (0, f)),
                once(8, width),
            ],
            scratch_shapes=[
                pltpu.VMEM((rows, width), F32),
                pltpu.VMEM((rows, width), F32),
                pltpu.VMEM((rows, LANES), F32),
                pltpu.VMEM((rows, width), BF16),
                pltpu.VMEM((width, rows), BF16),
                pltpu.VMEM((rows, width), F32),
                pltpu.VMEM((rows, width), F32),
                pltpu.VMEM((rows, tile), BF16),
                pltpu.VMEM((rows, tile), BF16),
            ],
        ),
        out_shape=outs,
        compiler_params=pltpu.CompilerParams(vmem_limit_bytes=VMEM_BYTES),
        cost_estimate=pl.CostEstimate(
            flops=12 * rows * width * wide, bytes_accessed=8 * width * wide, transcendentals=0
        ),
        name="feed",
    )(
        me,
        here,
        attended,
        grad,
        w_out,
        bias_out,
        gain,
        shift,
        w_up,
        bias_up.reshape(1, -1),
        w_down,
        bias_down,
    )


def start_kernel(
    tokens_ref,
    lengths_ref,
    gain_ref,
    shift_ref,
    w_ref,
    query_ref,
    value_ref,
    projected_ref,
    hidden_ref,
    here_ref,
    found_ref,
    rows,
    staged,
    sent,
    landed,
    out_sem,
):
    core, across, swap = neighbours()
    query = row_of(query_ref)
    bias = jnp.concatenate([query, jnp.zeros_like(query), row_of(value_ref)], 1)
    parts = sent.shape[1]
    height = tokens_ref.shape[0]
    part = height // parts
    greet([core, across, swap])

    def span(i):
        return pl.ds(pl.multiple_of(i * part, part), part)

    def moved(i):
        return (tokens_ref.at[span(i)], rows.at[0, span(i)], sent.at[0, i], landed.at[0, i])

    def lengths():
        return remote(lengths_ref, found_ref, sent.at[4, 0], landed.at[4, 0], core)

    def forward(i, origin, piece, device):
        return remote(
            rows.at[origin, span(i)],
            rows.at[piece, span(i)],
            sent.at[piece, i],
            landed.at[piece, i],
            device,
        )

    def out_span(piece, i):
        return pl.ds(pl.multiple_of(piece * height + i * part, part), part)

    def to_hbm(piece, i):
        at = out_span(piece, i)
        return pltpu.make_async_copy(staged.at[at], projected_ref.at[at], out_sem.at[piece, i])

    def project(piece, i):
        values = rows[piece, span(i), :].astype(F32)
        hidden = layer_norm(values, row_of(gain_ref), row_of(shift_ref))[0].astype(BF16)
        staged[out_span(piece, i), :] = (
            dot_as(hidden, w_ref[...], NN) + bias
        ).astype(BF16)
        to_hbm(piece, i).start()
        return hidden

    for i in range(parts):
        move_start(*moved(i))
    lengths().start()

    def first(i, carry):
        move_landed(*moved(i))
        forward(i, 0, 2, across).start()
        forward(i, 0, 1, core).start()
        hidden_ref[span(i), :] = project(0, i)
        here_ref[span(i), :] = rows[0, span(i), :]
        return carry

    lax.fori_loop(0, parts, first, 0)

    def second(i, carry):
        forward(i, 0, 1, core).wait_recv()
        project(1, i)
        forward(i, 0, 2, across).wait_recv()
        forward(i, 2, 3, core).start()
        project(2, i)
        return carry

    lax.fori_loop(0, parts, second, 0)

    def third(i, carry):
        forward(i, 2, 3, core).wait_recv()
        project(3, i)
        return carry

    lax.fori_loop(0, parts, third, 0)
    lengths().wait()

    def last(i, carry):
        move_sent(*moved(i))
        forward(i, 0, 2, across).wait_send()
        forward(i, 0, 1, core).wait_send()
        forward(i, 2, 3, core).wait_send()
        for piece in range(4):
            to_hbm(piece, i).wait()
        return carry

    lax.fori_loop(0, parts, last, 0)


def start_work(tokens, clip_lengths, gain, shift, weight, query, value):
    rows, width = tokens.shape
    vmem, anywhere = pl.BlockSpec(memory_space=pltpu.VMEM), pl.BlockSpec(memory_space=pl.ANY)
    projected, hidden, here, found = pl.pallas_call(
        start_kernel,
        in_specs=[anywhere] + [vmem] * 6,
        out_specs=[anywhere, vmem, vmem, vmem],
        out_shape=[
            jax.ShapeDtypeStruct((4 * rows, 3 * width), BF16),
            jax.ShapeDtypeStruct((rows, width), BF16),
            jax.ShapeDtypeStruct((rows, width), BF16),
            jax.ShapeDtypeStruct(clip_lengths.shape, jnp.int32),
        ],
        scratch_shapes=[
            pltpu.VMEM((4, rows, width), BF16),
            pltpu.VMEM((4 * rows, 3 * width), BF16),
            pltpu.SemaphoreType.DMA((5, 4)),
            pltpu.SemaphoreType.DMA((5, 4)),
            pltpu.SemaphoreType.DMA((4, 4)),
        ],
        compiler_params=pltpu.CompilerParams(
            vmem_limit_bytes=VMEM_BYTES, collective_id=0, has_side_effects=True
        ),
        cost_estimate=pl.CostEstimate(
            flops=24 * rows * width * width, bytes_accessed=32 * rows * width, transcendentals=0
        ),
        name="start_work",
    )(tokens, clip_lengths, gain, shift, weight, query, value)
    return projected, hidden, here, jnp.where(stays(), clip_lengths, found)


class PairPlan:
    ways = True

    def start(self, tokens, clip_lengths, gain, shift, weight, query, value):
        projected, hidden, here, lengths = start_work(
            tokens, clip_lengths, gain, shift, weight, query, value
        )
        return projected, projected, hidden, here, lengths

    def positions(self, rows):
        core, z = lax.axis_index("dp") % 2, lax.axis_index("seq")
        found = []
        for piece in range(4):
            c, plane = core ^ (piece % 2), z ^ (piece // 2)
            shard = jnp.where(c == plane // 2, plane, plane ^ 2)
            found.append(shard * rows + jnp.arange(rows, dtype=jnp.int32))
        return jnp.concatenate(found)

    def own(self, gathered):
        return gathered

    def backward(self, work, weights, attention):
        here, hidden1, grad_out, projected, own, mark_k, mark_q = work
        chances, attended, log_totals = attention
        me = lax.axis_index("dp").astype(jnp.int32).reshape(1)
        block_out, grad, grad_middle, down, up, out, sum_up, sums = feed(
            here, attended, grad_out, *weights[2:], me
        )
        return results(
            *backward(
                chances,
                grad,
                attended,
                projected,
                self.own(mark_k),
                mark_q,
                log_totals,
                weights[0],
                hidden1,
                here,
                grad_middle,
                weights[1],
                sums,
                sum_up,
                [down.reshape((8,) + down.shape[2:]), up, out],
                block_out,
            )
        )


class PlainPlan:
    ways = None

    def __init__(self, pieces):
        self.pieces = pieces

    def start(self, tokens, clip_lengths, gain, shift, weight, query, value):
        hidden = layer_norm(tokens.astype(F32), gain, shift)[0].astype(BF16)
        bias = jnp.concatenate([query, jnp.zeros_like(query), value])
        own = (matmul(hidden, weight) + bias).astype(BF16)
        projected = lax.all_gather(own, "seq", axis=0, tiled=True)
        return projected, own, hidden, tokens, clip_lengths

    def gather(self, own):
        gathered = lax.all_gather(own, "seq", axis=0, tiled=False)
        return [gathered[i] for i in range(self.pieces)]

    def positions(self, rows):
        return jnp.arange(rows * self.pieces, dtype=jnp.int32)

    def own(self, gathered):
        rows = gathered.shape[0] // self.pieces
        return lax.dynamic_slice_in_dim(gathered, lax.axis_index("seq") * rows, rows, 0)

    def backward(self, work, weights, attention):
        here, hidden1, grad_out, projected, own, mark_k, mark_q = work
        chances, attended, log_totals = attention
        w_qkv, ln1_gain, w_out, bias_out, gain, shift, w_up, bias_up, w_down, bias_down = weights
        middle = here.astype(F32) + matmul(attended, w_out) + bias_out
        normed_out, normed, inverse = layer_norm(middle, gain, shift)
        hidden = normed_out.astype(BF16)
        activated, slope = gelu_parts(matmul(hidden, w_up) + bias_up)
        activated = activated.astype(BF16)
        grad_upper = (inner_cols(grad_out, w_down) * slope).astype(BF16)
        grad_hidden = inner_cols(grad_upper, w_up)
        grad_norm, grad_gain, grad_shift = norm_back(grad_hidden, normed, inverse, gain)
        grad_middle = grad_out.astype(F32) + grad_norm
        grad_branch = grad_middle.astype(BF16)
        grad = inner_cols(grad_branch, w_out).astype(BF16)
        block_out = (middle + matmul(activated, w_down) + bias_down).astype(BF16)

        product = (grad.astype(F32) * attended.astype(F32)).reshape(grad.shape[0], -1, HDIM)
        deltas = jnp.sum(product, -1).T
        deltas = jnp.pad(deltas, ((0, STATS - deltas.shape[0]), (0, 0)))
        dq = grad_query(chances, grad, projected, deltas)
        dk, dv = grad_key_value(
            own,
            projected,
            self.gather(grad),
            self.gather(log_totals),
            self.gather(deltas),
            self.own(mark_k),
            mark_q,
        )
        grad_projected = jnp.concatenate([dq, dk, dv], 1)
        grad_hidden1 = inner_cols(grad_projected, w_qkv)
        _, normed1, inverse1 = layer_norm(here.astype(F32), 0.0, 0.0)
        grad_norm1, grad_ln1_gain, grad_ln1_shift = norm_back(
            grad_hidden1, normed1, inverse1, ln1_gain
        )

        def total(values):
            return jnp.sum(values.astype(F32), 0)

        return (block_out, (grad_middle + grad_norm1).astype(BF16)) + tuple(
            self.reduce(value)
            for value in (
                grad_ln1_gain,
                grad_ln1_shift,
                inner_rows(hidden1, grad_projected),
                total(dq),
                total(dv),
                inner_rows(attended, grad_branch),
                total(grad_branch),
                grad_gain,
                grad_shift,
                inner_rows(hidden, grad_upper),
                total(grad_upper),
                inner_rows(activated, grad_out),
                total(grad_out),
            )
        )

    def reduce(self, total):
        return lax.psum(lax.psum_scatter(total, "dp", scatter_dimension=0, tiled=True), "seq")


def body(
    plan,
    tokens,
    clip_lengths,
    ln1_gain,
    ln1_shift,
    w_qkv,
    bias_query,
    bias_value,
    w_out,
    bias_out,
    ln2_gain,
    ln2_shift,
    w_up,
    bias_up,
    w_down,
    bias_down,
    cotangent,
):
    rows, width = tokens.shape
    projected, own, hidden1, here, lengths = plan.start(
        tokens, clip_lengths, ln1_gain, ln1_shift, w_qkv, bias_query, bias_value
    )

    clip_ends = jnp.cumsum(lengths.reshape(-1))
    position = plan.positions(rows)
    segment = jnp.sum((position[:, None] >= clip_ends[None, :]).astype(jnp.int32), 1)
    lane = jnp.arange(LANES, dtype=jnp.int32)[None, :]
    same = lane == segment[:, None]
    mark_k = same.astype(BF16)
    mark_q = jnp.where(same | (lane >= clip_ends.shape[0]), 0.0, masked_score).astype(BF16)

    attended, chances, log_totals, grad_out = attend(
        plan, own, projected, plan.own(mark_q), mark_k, cotangent
    )

    return tuple(
        plan.backward(
            (here, hidden1, grad_out, projected, own, mark_k, mark_q),
            (
                w_qkv,
                ln1_gain,
                w_out,
                bias_out,
                ln2_gain,
                ln2_shift,
                w_up,
                bias_up,
                w_down,
                bias_down,
            ),
            (chances, attended, log_totals),
        )
    )


def solution(mesh):
    sizes = dict(mesh.shape)
    plan = PairPlan() if sizes == {"dp": 8, "seq": 4} else PlainPlan(sizes["seq"])
    rows = P(("dp", "seq"), None)
    return jax.shard_map(
        functools.partial(body, plan),
        mesh=mesh,
        in_specs=(rows, P("dp", None)) + (P(),) * 13 + (rows,),
        out_specs=(
            rows,
            rows,
            P("dp"),
            P("dp"),
            P("dp", None),
            P("dp"),
            P("dp"),
            P("dp", None),
            P("dp"),
            P("dp"),
            P("dp"),
            P("dp", None),
            P("dp"),
            P("dp", None),
            P("dp"),
        ),
        check_vma=False,
    )
```
